512 devices in a mesh: ja: 64 (over z, x, core), aa: 8 (over y).
Axes of the slice: x: 4, y: 8, z: 8, core: 2. Of those that a mesh axis runs over, the one named last changes fastest.
Arguments:
- state: float32 [12, 131072], P(None, 'ja'), may hold values from -6 to 6
- mass: float32 [131072], P('ja'), may hold values from 0.2 to 5
- levels: int32 [131072], P('ja'), may hold values from 0 to 5, as said below
- ticks: int32 [131072], P('ja'), may hold values from 0 to 32, as said below
- active: int32 [10240], replicated, may hold values from 0 to 131071, as said below
Outputs:
- new_active: float32 [12, 10240], P(None, 'aa')
- new_state: float32 [12, 131072], P(None, 'ja')
The draws below stay inside these ranges and needn't reach their ends.
Inputs may be any that keep to these rules, and one draw needn't show every extreme that they name: `levels`: a star's step is 0.25 * 2**(-level). `ticks`: below 2**(5 - levels) for a star not in active, equal to 2**(5 - levels) for a star in active. Distinct star indices; entries b * 1280 to (b + 1) * 1280 - 1 form active block b.
All inputs are finite; a program needn't handle non-finite values.
Results may differ from the reference program's by a relative error of at most 0.0003.
Values sent between devices are 32-bit elements; how exact they have to be, the bound alone decides.
No kernel may reach another device: no remote copies, remote signals or barrier semaphores. Data moves between devices by JAX's collectives and lax.ppermute only.
A program may use at most 64 MiB of HBM per device.

```python
import math
import jax
import jax.numpy as jnp
from jax import lax

LEVELS = 5
N_STARS = 131072
ACTIVE = 10240


def common_stars(key):
    keys = jax.random.split(key, 5)
    total = N_STARS
    count = ACTIVE
    level_draw = jax.random.randint(keys[0], (total,), 0, LEVELS + 1)
    full = jnp.left_shift(jnp.ones_like(level_draw), LEVELS - level_draw)
    tick_draw = jax.random.randint(keys[1], (total,), 0, 2 ** LEVELS) % full
    quarter = total // 4
    inner_rest = 1 + jax.random.permutation(keys[2], quarter - 1)[:count // 2 - 1]
    inner = jnp.concatenate([jnp.zeros((1,), inner_rest.dtype), inner_rest])
    outer_rest = quarter + jax.random.permutation(keys[3], total - quarter - 1)[:count - count // 2 - 1]
    outer = jnp.concatenate([jnp.full((1,), total - 1, outer_rest.dtype), outer_rest])
    chosen = jax.random.permutation(keys[4], jnp.concatenate([inner, outer]))
    tick_draw = tick_draw.at[chosen].set(full[chosen])
    return (level_draw.astype(jnp.int32), tick_draw.astype(jnp.int32), chosen.astype(jnp.int32))


def draw_levels(key, part):
    level_draw, tick_draw, chosen = common_stars(key)
    return level_draw


def draw_ticks(key, part):
    level_draw, tick_draw, chosen = common_stars(key)
    return tick_draw


def draw_active(key, part):
    level_draw, tick_draw, chosen = common_stars(key)
    return chosen


def level_of(key, shape, cuts, least, largest):
    gain = 1.0
    for dim, parts in cuts:
        steps = jax.random.uniform(jax.random.fold_in(jax.random.fold_in(key, 6), dim), (parts,), jnp.float32, least / len(cuts), largest / len(cuts))
        gain = gain * jnp.repeat(jnp.exp(steps), shape[dim] // parts).reshape((-1,) + (1,) * (len(shape) - 1 - dim))
    return gain


def bell_draw(key, extent, scale, most, pieces=(), kind=jnp.bfloat16):
    drawn = scale * jax.random.normal(key, extent, jnp.float32)
    if pieces:
        drawn = drawn * level_of(key, extent, pieces, -0.22, 0.18)
    return jnp.clip(drawn, -most, most).astype(kind)


def setup_inputs(seed: int = 0) -> dict:
    streams_of = jax.random.split(jax.random.key(seed), 6)
    return {
        "state": bell_draw(streams_of[0], (12, N_STARS), 1.0, 6.0, ((1, 64),), jnp.float32),
        "mass": jnp.clip(jnp.exp(math.log(5.0) - 3.218876 * jax.random.uniform(streams_of[1], (N_STARS,), jnp.float32) ** level_of(streams_of[1], (N_STARS,), ((0, 64),), -0.2, 0.2)), 0.2, 5.0),
        "levels": draw_levels(jax.random.fold_in(streams_of[5], 71), 0),
        "ticks": draw_ticks(jax.random.fold_in(streams_of[5], 71), 0),
        "active": draw_active(jax.random.fold_in(streams_of[5], 71), 0),
    }


EPS2 = 0.0001
H_MAX = 0.25

def predict(state, ticks):
    dt = ticks.astype(jnp.float32) * (H_MAX / 2 ** LEVELS)
    pos, vel, acc, jerk = (state[0:3], state[3:6], state[6:9], state[9:12])
    predicted = pos + dt * (vel + dt * (0.5 * acc + dt * (jerk / 6.0)))
    predicted_vel = vel + dt * (acc + dt * (0.5 * jerk))
    return (predicted, predicted_vel)

def field_terms(targets, predicted, predicted_vel, mass):
    dx = predicted[0][None, :] - targets[0][:, None]
    dy = predicted[1][None, :] - targets[1][:, None]
    dz = predicted[2][None, :] - targets[2][:, None]
    wx = predicted_vel[0][None, :] - targets[3][:, None]
    wy = predicted_vel[1][None, :] - targets[4][:, None]
    wz = predicted_vel[2][None, :] - targets[5][:, None]
    total = dx * dx + dy * dy + dz * dz + EPS2
    inverse = lax.rsqrt(total)
    weight = mass[None, :] * inverse * inverse * inverse
    rate = 3.0 * (dx * wx + dy * wy + dz * wz) / total
    return jnp.stack([lax.optimization_barrier(jnp.sum(weight * dx, axis=1)), lax.optimization_barrier(jnp.sum(weight * dy, axis=1)), lax.optimization_barrier(jnp.sum(weight * dz, axis=1)), lax.optimization_barrier(jnp.sum(weight * (wx - rate * dx), axis=1)), lax.optimization_barrier(jnp.sum(weight * (wy - rate * dy), axis=1)), lax.optimization_barrier(jnp.sum(weight * (wz - rate * dz), axis=1))])

def correct(states, step, forces):
    pos, vel, old_acc, old_jerk = (states[0:3], states[3:6], states[6:9], states[9:12])
    acc_new, jerk_new = (forces[0:3], forces[3:6])
    error = old_acc - acc_new
    second = -6.0 * error - step * (4.0 * old_jerk + 2.0 * jerk_new)
    third = 12.0 * error + 6.0 * step * (old_jerk + jerk_new)
    fixed_pos = pos + step * step * (second / 24.0 + third / 120.0)
    fixed_vel = vel + step * (second / 6.0 + third / 24.0)
    return jnp.concatenate([fixed_pos, fixed_vel, acc_new, jerk_new], axis=0)

def reference(state, mass, levels, ticks, active):
    predicted, predicted_vel = predict(state, ticks)
    table = jnp.concatenate([predicted, predicted_vel, state[6:12]], axis=0)
    chosen = jnp.take(table, active, axis=1)
    step = H_MAX * jnp.exp2(-jnp.take(levels, active).astype(jnp.float32))
    count = chosen.shape[1]
    blocks = chosen[0:6].reshape(6, count // 64, 64).transpose(1, 0, 2)
    terms = lax.map(lambda targets: field_terms(targets, predicted, predicted_vel, mass), blocks)
    forces = terms.transpose(1, 0, 2).reshape(6, count) * (1.0 / N_STARS)
    new_active = correct(chosen, step, forces)
    new_state = state.at[:, active].set(new_active)
    return (new_active, new_state)
```

```python
import jax
import jax.numpy as jnp
from jax import lax
from jax.experimental import pallas as pl
from jax.experimental.pallas import tpu as pltpu
from jax.sharding import Mesh, PartitionSpec as P

LEVELS = 5
EPS2 = 0.0001
H_MAX = 0.25
TICK = H_MAX / 2**LEVELS

X, C = 4, 2
GROUPS = X * C
TILES = 16
MAIN, TAIL = 128, 32
PER = MAIN + TAIL
FIELD = 8 * TILES
CHUNK = 512

f32, bf16 = jnp.float32, jnp.bfloat16


def params():
    return pltpu.CompilerParams(vmem_limit_bytes=48 * 1024 * 1024)


def vmem(n):
    return [pl.BlockSpec(memory_space=pltpu.VMEM)] * n


def predict(pos, vel, acc, jerk, dt):
    predicted = pos + dt * (vel + dt * (0.5 * acc + dt * (jerk / 6.0)))
    predicted_vel = vel + dt * (acc + dt * (0.5 * jerk))
    return predicted, predicted_vel


def step_of(levels):
    return jnp.left_shift(jnp.ones_like(levels), LEVELS - levels).astype(f32) * TICK


def correct(pos, vel, old_acc, old_jerk, step, acc_new, jerk_new):
    error = old_acc - acc_new
    second = -6.0 * error - step * (4.0 * old_jerk + 2.0 * jerk_new)
    third = 12.0 * error + 6.0 * step * (old_jerk + jerk_new)
    fixed_pos = pos + step * step * (second / 24.0 + third / 120.0)
    fixed_vel = vel + step * (second / 6.0 + third / 24.0)
    return fixed_pos, fixed_vel


def split3(value):
    first = value.astype(bf16)
    rest = value - first.astype(f32)
    second = rest.astype(bf16)
    return first, second, (rest - second.astype(f32)).astype(bf16)


def pack(main, tail, spare=None):
    if spare is None:
        spare = jnp.zeros((1, TAIL), f32)
    last = jnp.concatenate([tail[0:1], tail[1:2], tail[2:3], spare], axis=1)
    return jnp.concatenate([main, last], axis=0)


def first_star():
    return ((lax.axis_index("z") * X + lax.axis_index("x")) * C + lax.axis_index("c")) * (TILES * 128)


def pick_kernel(state_ref, mass_ref, ticks_ref, levels_ref, active_ref, msg_ref, table_ref):
    start = first_star()
    block = lax.axis_index("aa") * 10
    zero = jnp.zeros((1, 128), f32)
    for i in range(TILES):
        s = state_ref[:, i * 128 : (i + 1) * 128]
        dt = ticks_ref[i : i + 1, :].astype(f32) * TICK
        pos, vel = predict(s[0:3], s[3:6], s[6:9], s[9:12], dt)
        step = step_of(levels_ref[i : i + 1, :])
        field = jnp.concatenate([pos, vel, mass_ref[i : i + 1, :], zero], axis=0)
        both = jnp.concatenate([field, s[6:12], step, zero], axis=0)
        for n, part in enumerate(split3(both)):
            table_ref[n * 256 + i * 16 : n * 256 + (i + 1) * 16, :] = part
        for g in range(GROUPS):
            msg_ref[g, i * 8 : (i + 1) * 8, :] = field
    rows = lax.broadcasted_iota(jnp.int32, (128, 128), 0)
    picks = []
    for k in range(10):
        local = active_ref[pl.ds(block + k, 1), :] - start
        high = jnp.broadcast_to(jnp.right_shift(local, 7), (16, 128))
        low = jnp.bitwise_and(local, 127)
        chosen = jnp.where(rows == low, 1.0, 0.0).astype(bf16)
        found = jnp.dot(table_ref[...], chosen, preferred_element_type=f32)
        pick = jnp.zeros((16, 128), f32)
        for h in range(TILES):
            r = slice(h * 16, (h + 1) * 16)
            value = (found[0:256][r] + found[256:512][r]) + found[512:768][r]
            pick = jnp.where(high == h, value, pick)
        picks.append(pick)
    for g in range(GROUPS):
        main = picks[g]
        tail = picks[8 + g // 4][:, (g % 4) * TAIL : (g % 4 + 1) * TAIL]
        msg_ref[g, FIELD : FIELD + 4, :] = pack(main[0:3], tail[0:3])
        msg_ref[g, FIELD + 4 : FIELD + 8, :] = pack(main[3:6], tail[3:6])
        msg_ref[g, FIELD + 8 : FIELD + 12, :] = pack(main[8:11], tail[8:11], tail[14:15])
        msg_ref[g, FIELD + 12 : FIELD + 16, :] = pack(main[11:14], tail[11:14])
        msg_ref[g, 7:8, :] = main[14:15]


def sum_kernel(got_ref, first_ref, out_ref, keep_ref):
    total = got_ref[0]
    step = first_ref[0]
    for g in range(1, GROUPS):
        total = total + got_ref[g]
        step = step + first_ref[g]
    for z in range(out_ref.shape[0]):
        out_ref[z] = total[0:8]
    keep_ref[0:8, :] = total[8:16]
    keep_ref[8:16, :] = step


def force_kernel(targets_ref, got_ref, keep_ref, out_ref, seen_ref, weight_ref, left0_ref, left1_ref, sums_ref):
    target = targets_ref[0]
    for z in range(1, targets_ref.shape[0]):
        target = target + targets_ref[z]
    columns = jnp.transpose(target)
    for half in range(2):
        for q in range(3):
            seen_ref[half * 3 + q, 0:MAIN, :] = jnp.broadcast_to(columns[:, half * 4 + q : half * 4 + q + 1], (MAIN, 128))
            seen_ref[half * 3 + q, MAIN:PER, :] = jnp.broadcast_to(
                columns[q * TAIL : (q + 1) * TAIL, half * 4 + 3 : half * 4 + 4], (TAIL, 128)
            )

    row = lax.broadcasted_iota(jnp.int32, (8, 128), 0)

    def weigh(g, _):
        for i in range(TILES):
            tile = got_ref[g, i * 8 : (i + 1) * 8, :]
            mass = tile[6:7]
            value = jnp.where(row < 6, tile * mass, jnp.where(row == 6, tile, 0.0))
            first = value.astype(bf16).astype(f32)
            rest = value - first
            second = rest.astype(bf16).astype(f32)
            rows = jnp.concatenate([first, second, rest - second, jnp.zeros_like(value)], axis=0).astype(bf16)
            weight_ref[:, pl.ds(pl.multiple_of((g * TILES + i) * 128, 128), 128)] = rows
        return 0

    lax.fori_loop(0, GROUPS, weigh, 0)
    sums_ref[...] = jnp.zeros_like(sums_ref)

    def fill(left_ref, chunk):
        per_group = TILES * 128 // CHUNK
        g, part = chunk // per_group, chunk % per_group
        for j in range(CHUNK // 128):
            base = pl.multiple_of(part * (CHUNK // 16) + j * 8, 8)
            star = [jnp.broadcast_to(got_ref[g, pl.ds(base + q, 1), :], (16, 128)) for q in range(6)]
            for b in range(PER // 16):
                r = slice(b * 16, (b + 1) * 16)
                dx, dy, dz, wx, wy, wz = [star[q] - seen_ref[q, r, :] for q in range(6)]
                total = (dx * dx + EPS2) + dy * dy + dz * dz
                along = dx * wx + dy * wy + dz * wz
                inverse = lax.rsqrt(total)
                square = inverse * inverse
                cube = square * inverse
                rate = cube * (square * along)
                cube_high = cube.astype(bf16)
                cube_low = (cube - cube_high.astype(f32)).astype(bf16)
                rate_high = rate.astype(bf16)
                rate_low = (rate - rate_high.astype(f32)).astype(bf16)
                for n, part_value in enumerate((cube_high, cube_low, rate_high, rate_low)):
                    left_ref[n * PER + b * 16 : n * PER + (b + 1) * 16, j * 128 : (j + 1) * 128] = part_value

    def gather(left_ref, chunk):
        weight = weight_ref[:, pl.ds(pl.multiple_of(chunk * CHUNK, CHUNK), CHUNK)]
        sums_ref[...] += lax.dot_general(left_ref[...], weight, (((1,), (1,)), ((), ())), preferred_element_type=f32)

    chunks = GROUPS * TILES * 128 // CHUNK
    fill(left0_ref, 0)

    def body(n, _):
        fill(left1_ref, 2 * n + 1)
        gather(left0_ref, 2 * n)
        fill(left0_ref, jnp.minimum(2 * n + 2, chunks - 1))
        gather(left1_ref, 2 * n + 1)
        return 0

    lax.fori_loop(0, chunks // 2, body, 0)

    def columns_of(first):
        total = sums_ref[first : first + PER, :] + sums_ref[first + PER : first + 2 * PER, :]
        main = jnp.transpose(total[0:MAIN])
        tail = jnp.transpose(total[MAIN:PER])
        return main[0:8] + main[8:16] + main[16:24], tail[0:8] + tail[8:16] + tail[16:24]

    def three(value):
        return jnp.concatenate([value, value, value], axis=0)

    main, tail = columns_of(0)
    cube_pos = pack(main[0:3], tail[0:3])
    cube_vel = pack(main[3:6], tail[3:6])
    cube_one = pack(three(main[6:7]), three(tail[6:7]))
    main, tail = columns_of(2 * PER)
    rate_pos = pack(main[0:3], tail[0:3])
    rate_one = pack(three(main[6:7]), three(tail[6:7]))
    acc = cube_pos - target[0:4] * cube_one
    jerk = (cube_vel - target[4:8] * cube_one) - 3.0 * (rate_pos - target[0:4] * rate_one)
    forces = jnp.concatenate([acc, jerk], axis=0)
    for z in range(out_ref.shape[0]):
        out_ref[z, 0:8, :] = forces
        out_ref[z, 8:24, :] = keep_ref[...]


def correct_kernel(scale, targets_ref, got_ref, out_ref):
    target = targets_ref[0]
    total = got_ref[0]
    for z in range(1, targets_ref.shape[0]):
        target = target + targets_ref[z]
        total = total + got_ref[z]
    forces = total[0:8] * scale
    old = total[8:16]
    main = total[23:24]
    tail = old[3:4, 96:128]
    step = pack(jnp.concatenate([main, main, main], axis=0), jnp.concatenate([tail, tail, tail], axis=0))
    pos, vel = correct(target[0:4], target[4:8], old[0:4], old[4:8], step, forces[0:4], forces[4:8])
    both = jnp.concatenate([pos, vel], axis=0)
    for d in range(out_ref.shape[0]):
        out_ref[d, 0:8, :] = forces
        out_ref[d, 8:16, :] = both


def store_kernel(state_ref, ticks_ref, levels_ref, active_ref, got_ref, new_active_ref, new_state_ref, left_ref, low_ref, sums_ref):
    start = first_star()
    mine = lax.axis_index("aa")

    def tails(c, y, row):
        parts = [got_ref[c, y * X + x, row : row + 1, :] for x in range(X)]
        return jnp.concatenate(
            [jnp.concatenate([p[:, q * TAIL : (q + 1) * TAIL] for p in parts], axis=1) for q in range(3)], axis=0
        )

    for c in range(C):
        for x in range(X):
            lanes = slice((c * X + x) * 128, (c * X + x + 1) * 128)
            tile = got_ref[c, mine * X + x]
            new_active_ref[0:3, lanes] = tile[8:11]
            new_active_ref[3:6, lanes] = tile[12:15]
            new_active_ref[6:9, lanes] = tile[0:3]
            new_active_ref[9:12, lanes] = tile[4:7]
        lanes = slice(1024 + c * 128, 1024 + (c + 1) * 128)
        new_active_ref[0:3, lanes] = tails(c, mine, 11)
        new_active_ref[3:6, lanes] = tails(c, mine, 15)
        new_active_ref[6:9, lanes] = tails(c, mine, 3)
        new_active_ref[9:12, lanes] = tails(c, mine, 7)

    row8 = lax.broadcasted_iota(jnp.int32, (8, 128), 0)
    rows = lax.broadcasted_iota(jnp.int32, (128, 128), 0)
    one = jnp.ones((1, 128), f32)
    sums_ref[...] = jnp.zeros_like(sums_ref)

    def block(y, _):
        def put(k, value):
            local = active_ref[pl.ds(y * 10 + k, 1), :] - start
            high = jnp.broadcast_to(jnp.right_shift(local, 7), (16, 128))
            low = jnp.bitwise_and(local, 127)
            lanes = slice(k * 128, (k + 1) * 128)
            low_ref[:, lanes] = jnp.where(rows == low, 1.0, 0.0).astype(bf16)
            first = value.astype(bf16).astype(f32)
            both = jnp.concatenate([first, value - first], axis=0)
            for h in range(TILES):
                left_ref[h * 16 : (h + 1) * 16, lanes] = jnp.where(high == h, both, 0.0).astype(bf16)

        for c in range(C):
            for x in range(X):
                put(c * X + x, jnp.where(row8 == 3, 1.0, got_ref[c, y * X + x, 0:8, :]))
            put(8 + c, jnp.concatenate([tails(c, y, 3), one, tails(c, y, 7), one], axis=0))
        sums_ref[...] += lax.dot_general(
            left_ref[...], low_ref[...], (((1,), (1,)), ((), ())), preferred_element_type=f32
        )
        return 0

    lax.fori_loop(0, got_ref.shape[1] // X, block, 0)

    for i in range(TILES):
        lanes = slice(i * 128, (i + 1) * 128)
        s = state_ref[:, lanes]
        forces = sums_ref[i * 16 : i * 16 + 8, :] + sums_ref[i * 16 + 8 : i * 16 + 16, :]
        acc, jerk, hit = forces[0:3], forces[4:7], forces[3:4] > 0.5
        dt = ticks_ref[i : i + 1, :].astype(f32) * TICK
        step = step_of(levels_ref[i : i + 1, :])
        pos, vel = predict(s[0:3], s[3:6], s[6:9], s[9:12], dt)
        pos, vel = correct(pos, vel, s[6:9], s[9:12], step, acc, jerk)
        new = jnp.concatenate([pos, vel, acc, jerk], axis=0)
        new_state_ref[:, lanes] = jnp.where(hit, new, s)


def per_device(state, mass, levels, ticks, active):
    z_count, y_count = lax.axis_size("z"), lax.axis_size("aa")
    n_stars = state.shape[1] * z_count * GROUPS
    mass, levels, ticks = [a.reshape(TILES, 128) for a in (mass, levels, ticks)]
    active = active.reshape(-1, 128)

    message = pl.pallas_call(
        pick_kernel,
        out_shape=jax.ShapeDtypeStruct((GROUPS, FIELD + 16, 128), f32),
        in_specs=vmem(5),
        out_specs=vmem(1)[0],
        scratch_shapes=[pltpu.VMEM((768, 128), bf16)],
        compiler_params=params(),
    )(state, mass, ticks, levels, active)
    got = lax.all_to_all(message, ("c", "x"), 0, 0, tiled=True)

    targets, keep = pl.pallas_call(
        sum_kernel,
        grid=(1,),
        out_shape=[jax.ShapeDtypeStruct((z_count, 8, 128), f32), jax.ShapeDtypeStruct((16, 128), f32)],
        in_specs=[
            pl.BlockSpec((GROUPS, 16, 128), lambda i: (0, FIELD // 16, 0)),
            pl.BlockSpec((GROUPS, 8, 128), lambda i: (0, 0, 0)),
        ],
        out_specs=[pl.BlockSpec((z_count, 8, 128), lambda i: (0, 0, 0)), pl.BlockSpec((16, 128), lambda i: (0, 0))],
        compiler_params=params(),
    )(got, got)
    targets = lax.all_to_all(targets, "z", 0, 0, tiled=True)

    partial = pl.pallas_call(
        force_kernel,
        out_shape=jax.ShapeDtypeStruct((z_count, 24, 128), f32),
        in_specs=vmem(3),
        out_specs=vmem(1)[0],
        scratch_shapes=[
            pltpu.VMEM((6, PER, 128), f32),
            pltpu.VMEM((32, GROUPS * TILES * 128), bf16),
            pltpu.VMEM((4 * PER, CHUNK), bf16),
            pltpu.VMEM((4 * PER, CHUNK), bf16),
            pltpu.VMEM((4 * PER, 32), f32),
        ],
        compiler_params=params(),
    )(targets, got, keep)
    partial = lax.all_to_all(partial, "z", 0, 0, tiled=True)

    updates = pl.pallas_call(
        lambda *refs: correct_kernel(1.0 / n_stars, *refs),
        out_shape=jax.ShapeDtypeStruct((y_count * X, 16, 128), f32),
        in_specs=vmem(2),
        out_specs=vmem(1)[0],
        compiler_params=params(),
    )(targets, partial)
    updates = lax.all_to_all(updates, ("aa", "x"), 0, 0, tiled=True)
    updates = lax.all_gather(updates, "c")

    new_active, new_state = pl.pallas_call(
        store_kernel,
        out_shape=[jax.ShapeDtypeStruct((12, 1280), f32), jax.ShapeDtypeStruct(state.shape, f32)],
        in_specs=vmem(5),
        out_specs=vmem(2),
        scratch_shapes=[
            pltpu.VMEM((256, 1280), bf16),
            pltpu.VMEM((128, 1280), bf16),
            pltpu.VMEM((256, 128), f32),
        ],
        compiler_params=params(),
    )(state, ticks, levels, active, updates)
    return new_active, new_state


def solution(mesh):
    shape = (mesh.shape["ja"] // GROUPS, X, C, mesh.shape["aa"])
    fine = Mesh(mesh.devices.reshape(shape), ("z", "x", "c", "aa"))
    ja = ("z", "x", "c")
    return jax.shard_map(
        per_device,
        mesh=fine,
        in_specs=(P(None, ja), P(ja), P(ja), P(ja), P()),
        out_specs=(P(None, "aa"), P(None, ja)),
        check_vma=False,
    )
```

```python
import jax
import jax.numpy as jnp
from jax import lax
from jax.experimental import pallas as pl
from jax.experimental.pallas import tpu as pltpu
from jax.sharding import Mesh, PartitionSpec as P

LEVELS = 5
EPS2 = 0.0001
H_MAX = 0.25
TICK = H_MAX / 2**LEVELS

X, C = 4, 2
GROUPS = X * C
TILES = 16
MAIN, TAIL = 128, 32
PER = MAIN + TAIL
FIELD = 8 * TILES
CHUNK = 512
ROWS = 16
BLOCKS = PER // ROWS

f32, bf16 = jnp.float32, jnp.bfloat16


def params():
    return pltpu.CompilerParams(vmem_limit_bytes=48 * 1024 * 1024)


def vmem(n):
    return [pl.BlockSpec(memory_space=pltpu.VMEM)] * n


def predict(pos, vel, acc, jerk, dt):
    predicted = pos + dt * (vel + dt * (0.5 * acc + dt * (jerk / 6.0)))
    predicted_vel = vel + dt * (acc + dt * (0.5 * jerk))
    return predicted, predicted_vel


def step_of(levels):
    return jnp.left_shift(jnp.ones_like(levels), LEVELS - levels).astype(f32) * TICK


def correct(pos, vel, old_acc, old_jerk, step, acc_new, jerk_new):
    error = old_acc - acc_new
    second = -6.0 * error - step * (4.0 * old_jerk + 2.0 * jerk_new)
    third = 12.0 * error + 6.0 * step * (old_jerk + jerk_new)
    fixed_pos = pos + step * step * (second / 24.0 + third / 120.0)
    fixed_vel = vel + step * (second / 6.0 + third / 24.0)
    return fixed_pos, fixed_vel


def split3(value):
    first = value.astype(bf16)
    rest = value - first.astype(f32)
    second = rest.astype(bf16)
    return first, second, (rest - second.astype(f32)).astype(bf16)


def pack(main, tail, spare=None):
    if spare is None:
        spare = jnp.zeros((1, TAIL), f32)
    last = jnp.concatenate([tail[0:1], tail[1:2], tail[2:3], spare], axis=1)
    return jnp.concatenate([main, last], axis=0)


def first_star():
    return ((lax.axis_index("z") * X + lax.axis_index("x")) * C + lax.axis_index("c")) * (TILES * 128)


def pick_kernel(*refs):
    given, msg_ref, table_ref, held, sems = refs[:5], refs[5], refs[6], refs[7:12], refs[12]
    copies = [pltpu.make_async_copy(a, b, sems.at[n]) for n, (a, b) in enumerate(zip(given, held))]
    for copy in copies:
        copy.start()
    for copy in copies:
        copy.wait()
    state_ref, mass_ref, ticks_ref, levels_ref, active_ref = held
    start = first_star()
    block = lax.axis_index("aa") * 10
    zero = jnp.zeros((1, 128), f32)
    for i in range(TILES):
        s = state_ref[:, i * 128 : (i + 1) * 128]
        dt = ticks_ref[i : i + 1, :].astype(f32) * TICK
        pos, vel = predict(s[0:3], s[3:6], s[6:9], s[9:12], dt)
        step = step_of(levels_ref[i : i + 1, :])
        field = jnp.concatenate([pos, vel, mass_ref[i : i + 1, :], zero], axis=0)
        both = jnp.concatenate([field, s[6:12], step, zero], axis=0)
        for n, part in enumerate(split3(both)):
            table_ref[n * 256 + i * 16 : n * 256 + (i + 1) * 16, :] = part
        for g in range(GROUPS):
            msg_ref[g, i * 8 : (i + 1) * 8, :] = field
    rows = lax.broadcasted_iota(jnp.int32, (128, 128), 0)
    picks = []
    for k in range(10):
        local = active_ref[pl.ds(block + k, 1), :] - start
        high = jnp.broadcast_to(jnp.right_shift(local, 7), (16, 128))
        low = jnp.bitwise_and(local, 127)
        chosen = jnp.where(rows == low, 1.0, 0.0).astype(bf16)
        found = jnp.dot(table_ref[...], chosen, preferred_element_type=f32)
        pick = jnp.zeros((16, 128), f32)
        for h in range(TILES):
            r = slice(h * 16, (h + 1) * 16)
            value = (found[0:256][r] + found[256:512][r]) + found[512:768][r]
            pick = jnp.where(high == h, value, pick)
        picks.append(pick)
    for g in range(GROUPS):
        main = picks[g]
        tail = picks[8 + g // 4][:, (g % 4) * TAIL : (g % 4 + 1) * TAIL]
        msg_ref[g, FIELD : FIELD + 4, :] = pack(main[0:3], tail[0:3])
        msg_ref[g, FIELD + 4 : FIELD + 8, :] = pack(main[3:6], tail[3:6])
        msg_ref[g, FIELD + 8 : FIELD + 12, :] = pack(main[8:11], tail[8:11], tail[14:15])
        msg_ref[g, FIELD + 12 : FIELD + 16, :] = pack(main[11:14], tail[11:14])
        msg_ref[g, 7:8, :] = main[14:15]


def sum_kernel(got_ref, first_ref, out_ref, keep_ref):
    total = got_ref[0]
    step = first_ref[0]
    for g in range(1, GROUPS):
        total = total + got_ref[g]
        step = step + first_ref[g]
    for z in range(out_ref.shape[0]):
        out_ref[z] = total[0:8]
    keep_ref[0:8, :] = total[8:16]
    keep_ref[8:16, :] = step


def force_kernel(targets_ref, got_ref, keep_ref, out_ref, seen_ref, weight_ref, sums_ref):
    target = targets_ref[0]
    for z in range(1, targets_ref.shape[0]):
        target = target + targets_ref[z]
    columns = jnp.transpose(target)
    for half in range(2):
        for q in range(3):
            seen_ref[half * 3 + q, 0:MAIN, :] = jnp.broadcast_to(columns[:, half * 4 + q : half * 4 + q + 1], (MAIN, 128))
            seen_ref[half * 3 + q, MAIN:PER, :] = jnp.broadcast_to(
                columns[q * TAIL : (q + 1) * TAIL, half * 4 + 3 : half * 4 + 4], (TAIL, 128)
            )

    row = lax.broadcasted_iota(jnp.int32, (8, 128), 0)

    def weigh(g, _):
        for i in range(TILES):
            tile = got_ref[g, i * 8 : (i + 1) * 8, :]
            mass = tile[6:7]
            value = jnp.where(row < 6, tile * mass, jnp.where(row == 6, tile, 0.0))
            first = value.astype(bf16).astype(f32)
            rest = value - first
            second = rest.astype(bf16).astype(f32)
            rows = jnp.concatenate([first, second, rest - second, jnp.zeros_like(value)], axis=0).astype(bf16)
            weight_ref[:, pl.ds(pl.multiple_of((g * TILES + i) * 128, 128), 128)] = rows
        return 0

    lax.fori_loop(0, GROUPS, weigh, 0)
    sums_ref[...] = jnp.zeros_like(sums_ref)

    def chunk(n, _):
        g, part = n // (TILES * 128 // CHUNK), n % (TILES * 128 // CHUNK)
        base = pl.multiple_of(part * (CHUNK // 16), 8)
        across = CHUNK // 128
        star = [
            jnp.concatenate(
                [jnp.broadcast_to(got_ref[g, pl.ds(base + j * 8 + q, 1), :], (ROWS, 128)) for j in range(across)], axis=1
            )
            for q in range(6)
        ]
        weight = weight_ref[:, pl.ds(pl.multiple_of(n * CHUNK, CHUNK), CHUNK)]
        values = []
        for b in range(BLOCKS):
            r = slice(b * ROWS, (b + 1) * ROWS)
            seen = [jnp.concatenate([seen_ref[q, r, :]] * across, axis=1) for q in range(6)]
            dx, dy, dz, wx, wy, wz = [star[q] - seen[q] for q in range(6)]
            total = (dx * dx + EPS2) + dy * dy + dz * dz
            along = dx * wx + dy * wy + dz * wz
            inverse = lax.rsqrt(total)
            square = inverse * inverse
            cube = square * inverse
            rate = cube * (square * along)
            for value in (cube, rate):
                high = value.astype(bf16)
                values += [high, (value - high.astype(f32)).astype(bf16)]
            if (b + 1) * 4 * ROWS % 256 == 0 or b == BLOCKS - 1:
                right = jnp.concatenate(values, axis=0)
                values = []
                end = (b + 1) * 4 * ROWS
                sums_ref[:, end - right.shape[0] : end] += lax.dot_general(
                    weight, right, (((1,), (1,)), ((), ())), preferred_element_type=f32
                )
        return 0

    lax.fori_loop(0, GROUPS * TILES * 128 // CHUNK, chunk, 0, unroll=4)
    sums = jnp.transpose(sums_ref[...])

    def columns_of(part):
        total = jnp.concatenate(
            [
                sums[b * 4 * ROWS + part * ROWS : b * 4 * ROWS + (part + 1) * ROWS]
                + sums[b * 4 * ROWS + (part + 1) * ROWS : b * 4 * ROWS + (part + 2) * ROWS]
                for b in range(BLOCKS)
            ],
            axis=0,
        )
        main = jnp.transpose(total[0:MAIN])
        tail = jnp.transpose(total[MAIN:PER])
        return main[0:8] + main[8:16] + main[16:24], tail[0:8] + tail[8:16] + tail[16:24]

    def three(value):
        return jnp.concatenate([value, value, value], axis=0)

    main, tail = columns_of(0)
    cube_pos = pack(main[0:3], tail[0:3])
    cube_vel = pack(main[3:6], tail[3:6])
    cube_one = pack(three(main[6:7]), three(tail[6:7]))
    main, tail = columns_of(2)
    rate_pos = pack(main[0:3], tail[0:3])
    rate_one = pack(three(main[6:7]), three(tail[6:7]))
    acc = cube_pos - target[0:4] * cube_one
    jerk = (cube_vel - target[4:8] * cube_one) - 3.0 * (rate_pos - target[0:4] * rate_one)
    forces = jnp.concatenate([acc, jerk], axis=0)
    for z in range(out_ref.shape[0]):
        out_ref[z, 0:8, :] = forces
        out_ref[z, 8:24, :] = keep_ref[...]


def correct_kernel(scale, targets_ref, got_ref, out_ref):
    target = targets_ref[0]
    total = got_ref[0]
    for z in range(1, targets_ref.shape[0]):
        target = target + targets_ref[z]
        total = total + got_ref[z]
    forces = total[0:8] * scale
    old = total[8:16]
    main = total[23:24]
    tail = old[3:4, 96:128]
    step = pack(jnp.concatenate([main, main, main], axis=0), jnp.concatenate([tail, tail, tail], axis=0))
    pos, vel = correct(target[0:4], target[4:8], old[0:4], old[4:8], step, forces[0:4], forces[4:8])
    both = jnp.concatenate([pos, vel], axis=0)
    for d in range(out_ref.shape[0]):
        out_ref[d, 0:8, :] = forces
        out_ref[d, 8:16, :] = both


def store_kernel(state_ref, ticks_ref, levels_ref, active_ref, got_ref, new_active_ref, new_state_ref, sums_ref):
    start = first_star()
    mine = lax.axis_index("aa")

    def tails(c, y, row):
        parts = [got_ref[c, y * X + x, row : row + 1, :] for x in range(X)]
        return jnp.concatenate(
            [jnp.concatenate([p[:, q * TAIL : (q + 1) * TAIL] for p in parts], axis=1) for q in range(3)], axis=0
        )

    for c in range(C):
        for x in range(X):
            lanes = slice((c * X + x) * 128, (c * X + x + 1) * 128)
            tile = got_ref[c, mine * X + x]
            new_active_ref[0:3, lanes] = tile[8:11]
            new_active_ref[3:6, lanes] = tile[12:15]
            new_active_ref[6:9, lanes] = tile[0:3]
            new_active_ref[9:12, lanes] = tile[4:7]
        lanes = slice(1024 + c * 128, 1024 + (c + 1) * 128)
        new_active_ref[0:3, lanes] = tails(c, mine, 11)
        new_active_ref[3:6, lanes] = tails(c, mine, 15)
        new_active_ref[6:9, lanes] = tails(c, mine, 3)
        new_active_ref[9:12, lanes] = tails(c, mine, 7)

    row8 = lax.broadcasted_iota(jnp.int32, (8, 128), 0)
    rows = lax.broadcasted_iota(jnp.int32, (128, 128), 0)
    one = jnp.ones((1, 128), f32)
    sums_ref[...] = jnp.zeros_like(sums_ref)

    def block(y, _):
        tiles = [jnp.where(row8 == 3, 1.0, got_ref[c, y * X + x, 0:8, :]) for c in range(C) for x in range(X)]
        for c in range(C):
            tiles.append(jnp.concatenate([tails(c, y, 3), one, tails(c, y, 7), one], axis=0))
        total = None
        for pair in range(5):
            lefts, lows = [], []
            for k in (2 * pair, 2 * pair + 1):
                local = active_ref[pl.ds(y * 10 + k, 1), :] - start
                high = jnp.broadcast_to(jnp.right_shift(local, 7), (16, 128))
                lows.append(jnp.where(rows == jnp.bitwise_and(local, 127), 1.0, 0.0).astype(bf16))
                first = tiles[k].astype(bf16).astype(f32)
                both = jnp.concatenate([first, tiles[k] - first], axis=0)
                lefts.append(
                    jnp.concatenate([jnp.where(high == h, both, 0.0).astype(bf16) for h in range(TILES)], axis=0)
                )
            product = lax.dot_general(
                jnp.concatenate(lefts, axis=1),
                jnp.concatenate(lows, axis=1),
                (((1,), (1,)), ((), ())),
                preferred_element_type=f32,
            )
            total = product if total is None else total + product
        sums_ref[...] += total
        return 0

    lax.fori_loop(0, got_ref.shape[1] // X, block, 0)

    for i in range(TILES):
        lanes = slice(i * 128, (i + 1) * 128)
        s = state_ref[:, lanes]
        forces = sums_ref[i * 16 : i * 16 + 8, :] + sums_ref[i * 16 + 8 : i * 16 + 16, :]
        acc, jerk, hit = forces[0:3], forces[4:7], forces[3:4] > 0.5
        dt = ticks_ref[i : i + 1, :].astype(f32) * TICK
        step = step_of(levels_ref[i : i + 1, :])
        pos, vel = predict(s[0:3], s[3:6], s[6:9], s[9:12], dt)
        pos, vel = correct(pos, vel, s[6:9], s[9:12], step, acc, jerk)
        new = jnp.concatenate([pos, vel, acc, jerk], axis=0)
        new_state_ref[:, lanes] = jnp.where(hit, new, s)


def per_device(state, mass, levels, ticks, active):
    z_count, y_count = lax.axis_size("z"), lax.axis_size("aa")
    n_stars = state.shape[1] * z_count * GROUPS
    mass, levels, ticks = [a.reshape(TILES, 128) for a in (mass, levels, ticks)]
    active = active.reshape(-1, 128)

    message = pl.pallas_call(
        pick_kernel,
        out_shape=jax.ShapeDtypeStruct((GROUPS, FIELD + 16, 128), f32),
        in_specs=[pl.BlockSpec(memory_space=pltpu.HBM)] * 5,
        out_specs=vmem(1)[0],
        scratch_shapes=[pltpu.VMEM((768, 128), bf16)]
        + [pltpu.VMEM(a.shape, a.dtype) for a in (state, mass, ticks, levels, active)]
        + [pltpu.SemaphoreType.DMA((5,))],
        compiler_params=params(),
    )(*[pltpu.with_memory_space_constraint(a, pltpu.HBM) for a in (state, mass, ticks, levels, active)])
    got = lax.all_to_all(message, ("c", "x"), 0, 0, tiled=True)

    targets, keep = pl.pallas_call(
        sum_kernel,
        grid=(1,),
        out_shape=[jax.ShapeDtypeStruct((z_count, 8, 128), f32), jax.ShapeDtypeStruct((16, 128), f32)],
        in_specs=[
            pl.BlockSpec((GROUPS, 16, 128), lambda i: (0, FIELD // 16, 0)),
            pl.BlockSpec((GROUPS, 8, 128), lambda i: (0, 0, 0)),
        ],
        out_specs=[pl.BlockSpec((z_count, 8, 128), lambda i: (0, 0, 0)), pl.BlockSpec((16, 128), lambda i: (0, 0))],
        compiler_params=params(),
    )(got, got)
    targets = lax.all_to_all(targets, "z", 0, 0, tiled=True)

    partial = pl.pallas_call(
        force_kernel,
        out_shape=jax.ShapeDtypeStruct((z_count, 24, 128), f32),
        in_specs=vmem(3),
        out_specs=vmem(1)[0],
        scratch_shapes=[
            pltpu.VMEM((6, PER, 128), f32),
            pltpu.VMEM((32, GROUPS * TILES * 128), bf16),
            pltpu.VMEM((32, 4 * PER), f32),
        ],
        compiler_params=params(),
    )(targets, got, keep)
    partial = lax.all_to_all(partial, "z", 0, 0, tiled=True)

    updates = pl.pallas_call(
        lambda *refs: correct_kernel(1.0 / n_stars, *refs),
        out_shape=jax.ShapeDtypeStruct((y_count * X, 16, 128), f32),
        in_specs=vmem(2),
        out_specs=vmem(1)[0],
        compiler_params=params(),
    )(targets, partial)
    updates = lax.all_to_all(updates, ("aa", "x"), 0, 0, tiled=True)
    updates = lax.all_gather(updates, "c")

    new_active, new_state = pl.pallas_call(
        store_kernel,
        out_shape=[jax.ShapeDtypeStruct((12, 1280), f32), jax.ShapeDtypeStruct(state.shape, f32)],
        in_specs=vmem(5),
        out_specs=vmem(2),
        scratch_shapes=[
            pltpu.VMEM((256, 128), f32),
        ],
        compiler_params=params(),
    )(state, ticks, levels, active, updates)
    return new_active, new_state


def solution(mesh):
    shape = (mesh.shape["ja"] // GROUPS, X, C, mesh.shape["aa"])
    fine = Mesh(mesh.devices.reshape(shape), ("z", "x", "c", "aa"))
    ja = ("z", "x", "c")
    return jax.shard_map(
        per_device,
        mesh=fine,
        in_specs=(P(None, ja), P(ja), P(ja), P(ja), P()),
        out_specs=(P(None, "aa"), P(None, ja)),
        check_vma=False,
    )
```

```python
import jax
import jax.numpy as jnp
from jax import lax
from jax.experimental import pallas as pl
from jax.experimental.pallas import tpu as pltpu
from jax.sharding import Mesh, PartitionSpec as P

LEVELS = 5
EPS2 = 0.0001
H_MAX = 0.25
TICK = H_MAX / 2**LEVELS

X, C = 4, 2
GROUPS = X * C
TILES = 16
MAIN, TAIL = 128, 32
PER = MAIN + TAIL
FIELD = 8 * TILES
CHUNK = 512
ROWS = 16
BLOCKS = PER // ROWS

f32, bf16 = jnp.float32, jnp.bfloat16


def params():
    return pltpu.CompilerParams(vmem_limit_bytes=48 * 1024 * 1024)


def vmem(n):
    return [pl.BlockSpec(memory_space=pltpu.VMEM)] * n


def predict(pos, vel, acc, jerk, dt):
    predicted = pos + dt * (vel + dt * (0.5 * acc + dt * (jerk / 6.0)))
    predicted_vel = vel + dt * (acc + dt * (0.5 * jerk))
    return predicted, predicted_vel


def step_of(levels):
    return jnp.left_shift(jnp.ones_like(levels), LEVELS - levels).astype(f32) * TICK


def correct(pos, vel, old_acc, old_jerk, step, acc_new, jerk_new):
    error = old_acc - acc_new
    second = -6.0 * error - step * (4.0 * old_jerk + 2.0 * jerk_new)
    third = 12.0 * error + 6.0 * step * (old_jerk + jerk_new)
    fixed_pos = pos + step * step * (second / 24.0 + third / 120.0)
    fixed_vel = vel + step * (second / 6.0 + third / 24.0)
    return fixed_pos, fixed_vel


def split3(value):
    first = value.astype(bf16)
    rest = value - first.astype(f32)
    second = rest.astype(bf16)
    return first, second, (rest - second.astype(f32)).astype(bf16)


def pack(main, tail, spare=None):
    if spare is None:
        spare = jnp.zeros((1, TAIL), f32)
    last = jnp.concatenate([tail[0:1], tail[1:2], tail[2:3], spare], axis=1)
    return jnp.concatenate([main, last], axis=0)


def first_star():
    return ((lax.axis_index("z") * X + lax.axis_index("x")) * C + lax.axis_index("c")) * (TILES * 128)


def pick_kernel(*refs):
    given, msg_ref, table_ref, held, sems = refs[:5], refs[5], refs[6], refs[7:12], refs[12]
    copies = [pltpu.make_async_copy(a, b, sems.at[n]) for n, (a, b) in enumerate(zip(given, held))]
    for copy in copies:
        copy.start()
    for copy in copies:
        copy.wait()
    state_ref, mass_ref, ticks_ref, levels_ref, active_ref = held
    start = first_star()
    block = lax.axis_index("aa") * 10
    zero = jnp.zeros((1, 128), f32)
    for i in range(TILES):
        s = state_ref[:, i * 128 : (i + 1) * 128]
        dt = ticks_ref[i : i + 1, :].astype(f32) * TICK
        pos, vel = predict(s[0:3], s[3:6], s[6:9], s[9:12], dt)
        step = step_of(levels_ref[i : i + 1, :])
        field = jnp.concatenate([pos, vel, mass_ref[i : i + 1, :], zero], axis=0)
        both = jnp.concatenate([field, s[6:12], step, zero], axis=0)
        for n, part in enumerate(split3(both)):
            table_ref[n * 256 + i * 16 : n * 256 + (i + 1) * 16, :] = part
        for x in range(X):
            msg_ref[x, i * 8 : (i + 1) * 8, :] = field
    rows = lax.broadcasted_iota(jnp.int32, (128, 128), 0)
    picks = []
    for k in range(10):
        local = active_ref[pl.ds(block + k, 1), :] - start
        high = jnp.broadcast_to(jnp.right_shift(local, 7), (16, 128))
        low = jnp.bitwise_and(local, 127)
        chosen = jnp.where(rows == low, 1.0, 0.0).astype(bf16)
        found = jnp.dot(table_ref[...], chosen, preferred_element_type=f32)
        pick = jnp.zeros((16, 128), f32)
        for h in range(TILES):
            r = slice(h * 16, (h + 1) * 16)
            value = (found[0:256][r] + found[256:512][r]) + found[512:768][r]
            pick = jnp.where(high == h, value, pick)
        picks.append(pick)
    for g in range(GROUPS):
        main = picks[g]
        tail = picks[8 + g // 4][:, (g % 4) * TAIL : (g % 4 + 1) * TAIL]
        step = [main[14:15, n * TAIL : (n + 1) * TAIL] for n in range(4)]
        x, row = g % X, FIELD + 16 * (g // X)
        for n, q in enumerate((0, 3, 8, 11)):
            msg_ref[x, row + 4 * n : row + 4 * n + 4, :] = pack(main[q : q + 3], tail[q : q + 3], step[n])
        msg_ref[x, 8 * (g // X) + 7 : 8 * (g // X) + 8, :] = jnp.concatenate([tail[14:15], jnp.zeros((1, 96), f32)], axis=1)


def sum_kernel(got_ref, out_ref, keep_ref):
    c = lax.axis_index("c")
    picks = pl.ds(pl.multiple_of(FIELD + 16 * c, 16), 16)
    total = got_ref[0, picks, :]
    step = got_ref[0, pl.ds(8 * c + 7, 1), :]
    for g in range(1, GROUPS):
        total = total + got_ref[g, picks, :]
        step = step + got_ref[g, pl.ds(8 * c + 7, 1), :]
    for z in range(out_ref.shape[0]):
        out_ref[z] = total[0:8]
    keep_ref[0:8, :] = total[8:16]
    keep_ref[8:16, :] = jnp.broadcast_to(step, (8, 128))


def force_kernel(targets_ref, got_ref, keep_ref, out_ref, seen_ref, weight_ref, sums_ref):
    target = targets_ref[0]
    for z in range(1, targets_ref.shape[0]):
        target = target + targets_ref[z]
    columns = jnp.transpose(target)
    for half in range(2):
        for q in range(3):
            seen_ref[half * 3 + q, 0:MAIN, :] = jnp.broadcast_to(columns[:, half * 4 + q : half * 4 + q + 1], (MAIN, 128))
            seen_ref[half * 3 + q, MAIN:PER, :] = jnp.broadcast_to(
                columns[q * TAIL : (q + 1) * TAIL, half * 4 + 3 : half * 4 + 4], (TAIL, 128)
            )

    row = lax.broadcasted_iota(jnp.int32, (8, 128), 0)

    def weigh(g, _):
        for i in range(TILES):
            tile = got_ref[g, i * 8 : (i + 1) * 8, :]
            mass = tile[6:7]
            value = jnp.where(row < 6, tile * mass, jnp.where(row == 6, tile, 0.0))
            first = value.astype(bf16).astype(f32)
            rest = value - first
            second = rest.astype(bf16).astype(f32)
            rows = jnp.concatenate([first, second, rest - second, jnp.zeros_like(value)], axis=0).astype(bf16)
            weight_ref[:, pl.ds(pl.multiple_of((g * TILES + i) * 128, 128), 128)] = rows
        return 0

    lax.fori_loop(0, GROUPS, weigh, 0)
    sums_ref[...] = jnp.zeros_like(sums_ref)

    def chunk(n, _):
        g, part = n // (TILES * 128 // CHUNK), n % (TILES * 128 // CHUNK)
        base = pl.multiple_of(part * (CHUNK // 16), 8)
        across = CHUNK // 128
        star = [
            jnp.concatenate(
                [jnp.broadcast_to(got_ref[g, pl.ds(base + j * 8 + q, 1), :], (ROWS, 128)) for j in range(across)], axis=1
            )
            for q in range(6)
        ]
        weight = weight_ref[:, pl.ds(pl.multiple_of(n * CHUNK, CHUNK), CHUNK)]
        values = []
        for b in range(BLOCKS):
            r = slice(b * ROWS, (b + 1) * ROWS)
            seen = [jnp.concatenate([seen_ref[q, r, :]] * across, axis=1) for q in range(6)]
            dx, dy, dz, wx, wy, wz = [star[q] - seen[q] for q in range(6)]
            total = (dx * dx + EPS2) + dy * dy + dz * dz
            along = dx * wx + dy * wy + dz * wz
            inverse = lax.rsqrt(total)
            square = inverse * inverse
            cube = square * inverse
            rate = cube * (square * along)
            for value in (cube, rate):
                high = value.astype(bf16)
                values += [high, (value - high.astype(f32)).astype(bf16)]
            if (b + 1) * 4 * ROWS % 256 == 0 or b == BLOCKS - 1:
                right = jnp.concatenate(values, axis=0)
                values = []
                end = (b + 1) * 4 * ROWS
                sums_ref[:, end - right.shape[0] : end] += lax.dot_general(
                    weight, right, (((1,), (1,)), ((), ())), preferred_element_type=f32
                )
        return 0

    lax.fori_loop(0, GROUPS * TILES * 128 // CHUNK, chunk, 0, unroll=4)
    sums = jnp.transpose(sums_ref[...])

    def columns_of(part):
        total = jnp.concatenate(
            [
                sums[b * 4 * ROWS + part * ROWS : b * 4 * ROWS + (part + 1) * ROWS]
                + sums[b * 4 * ROWS + (part + 1) * ROWS : b * 4 * ROWS + (part + 2) * ROWS]
                for b in range(BLOCKS)
            ],
            axis=0,
        )
        main = jnp.transpose(total[0:MAIN])
        tail = jnp.transpose(total[MAIN:PER])
        return main[0:8] + main[8:16] + main[16:24], tail[0:8] + tail[8:16] + tail[16:24]

    def three(value):
        return jnp.concatenate([value, value, value], axis=0)

    main, tail = columns_of(0)
    cube_pos = pack(main[0:3], tail[0:3])
    cube_vel = pack(main[3:6], tail[3:6])
    cube_one = pack(three(main[6:7]), three(tail[6:7]))
    main, tail = columns_of(2)
    rate_pos = pack(main[0:3], tail[0:3])
    rate_one = pack(three(main[6:7]), three(tail[6:7]))
    acc = cube_pos - target[0:4] * cube_one
    jerk = (cube_vel - target[4:8] * cube_one) - 3.0 * (rate_pos - target[0:4] * rate_one)
    last = jnp.concatenate([acc[3:4, 0:96], keep_ref[8:9, 0:TAIL]], axis=1)
    forces = jnp.concatenate([acc[0:3], last, jerk], axis=0)
    for z in range(out_ref.shape[0]):
        out_ref[z, 0:8, :] = forces
        out_ref[z, 8:16, :] = keep_ref[0:8, :]


def correct_kernel(scale, targets_ref, got_ref, out_ref):
    target = targets_ref[0]
    total = got_ref[0]
    for z in range(1, targets_ref.shape[0]):
        target = target + targets_ref[z]
        total = total + got_ref[z]
    forces = total[0:8] * scale
    old = total[8:16]
    main = jnp.concatenate([a[r : r + 1, 96:128] for a in (target, old) for r in (3, 7)], axis=1)
    tail = total[3:4, 96:128]
    step = pack(jnp.concatenate([main, main, main], axis=0), jnp.concatenate([tail, tail, tail], axis=0))
    pos, vel = correct(target[0:4], target[4:8], old[0:4], old[4:8], step, forces[0:4], forces[4:8])
    both = jnp.concatenate([pos, vel], axis=0)
    for d in range(out_ref.shape[0]):
        out_ref[d, 0:8, :] = forces
        out_ref[d, 8:16, :] = both


def store_kernel(state_ref, ticks_ref, levels_ref, active_ref, got_ref, new_active_ref, new_state_ref, sums_ref):
    start = first_star()
    mine = lax.axis_index("aa")

    def tails(c, y, row):
        parts = [got_ref[c * X + x, y, row : row + 1, :] for x in range(X)]
        return jnp.concatenate(
            [jnp.concatenate([p[:, q * TAIL : (q + 1) * TAIL] for p in parts], axis=1) for q in range(3)], axis=0
        )

    for c in range(C):
        for x in range(X):
            lanes = slice((c * X + x) * 128, (c * X + x + 1) * 128)
            tile = got_ref[c * X + x, mine]
            new_active_ref[0:3, lanes] = tile[8:11]
            new_active_ref[3:6, lanes] = tile[12:15]
            new_active_ref[6:9, lanes] = tile[0:3]
            new_active_ref[9:12, lanes] = tile[4:7]
        lanes = slice(1024 + c * 128, 1024 + (c + 1) * 128)
        new_active_ref[0:3, lanes] = tails(c, mine, 11)
        new_active_ref[3:6, lanes] = tails(c, mine, 15)
        new_active_ref[6:9, lanes] = tails(c, mine, 3)
        new_active_ref[9:12, lanes] = tails(c, mine, 7)

    row8 = lax.broadcasted_iota(jnp.int32, (8, 128), 0)
    rows = lax.broadcasted_iota(jnp.int32, (128, 128), 0)
    one = jnp.ones((1, 128), f32)
    sums_ref[...] = jnp.zeros_like(sums_ref)

    def block(y, _):
        tiles = [jnp.where(row8 == 3, 1.0, got_ref[c * X + x, y, 0:8, :]) for c in range(C) for x in range(X)]
        for c in range(C):
            tiles.append(jnp.concatenate([tails(c, y, 3), one, tails(c, y, 7), one], axis=0))
        lefts, lows = [], []
        for k, tile in enumerate(tiles):
            local = active_ref[pl.ds(y * 10 + k, 1), :] - start
            high = jnp.broadcast_to(jnp.right_shift(local, 7), (16, 128))
            lows.append(jnp.where(rows == jnp.bitwise_and(local, 127), 1.0, 0.0).astype(bf16))
            first = tile.astype(bf16).astype(f32)
            both = jnp.concatenate([first, tile - first], axis=0)
            lefts.append(jnp.concatenate([jnp.where(high == h, both, 0.0).astype(bf16) for h in range(TILES)], axis=0))
        total = lax.dot_general(
            jnp.concatenate(lefts, axis=1),
            jnp.concatenate(lows, axis=1),
            (((1,), (1,)), ((), ())),
            preferred_element_type=f32,
        )
        sums_ref[...] += total
        return 0

    lax.fori_loop(0, got_ref.shape[1], block, 0, unroll=4)

    for i in range(TILES):
        lanes = slice(i * 128, (i + 1) * 128)
        s = state_ref[:, lanes]
        forces = sums_ref[i * 16 : i * 16 + 8, :] + sums_ref[i * 16 + 8 : i * 16 + 16, :]
        acc, jerk, hit = forces[0:3], forces[4:7], forces[3:4] > 0.5
        dt = ticks_ref[i : i + 1, :].astype(f32) * TICK
        step = step_of(levels_ref[i : i + 1, :])
        pos, vel = predict(s[0:3], s[3:6], s[6:9], s[9:12], dt)
        pos, vel = correct(pos, vel, s[6:9], s[9:12], step, acc, jerk)
        new = jnp.concatenate([pos, vel, acc, jerk], axis=0)
        new_state_ref[:, lanes] = jnp.where(hit, new, s)


def per_device(state, mass, levels, ticks, active):
    z_count, y_count = lax.axis_size("z"), lax.axis_size("aa")
    n_stars = state.shape[1] * z_count * GROUPS
    mass, levels, ticks = [a.reshape(TILES, 128) for a in (mass, levels, ticks)]
    active = active.reshape(-1, 128)

    message = pl.pallas_call(
        pick_kernel,
        out_shape=jax.ShapeDtypeStruct((X, FIELD + 16 * C, 128), f32),
        in_specs=[pl.BlockSpec(memory_space=pltpu.HBM)] * 5,
        out_specs=vmem(1)[0],
        scratch_shapes=[pltpu.VMEM((768, 128), bf16)]
        + [pltpu.VMEM(a.shape, a.dtype) for a in (state, mass, ticks, levels, active)]
        + [pltpu.SemaphoreType.DMA((5,))],
        compiler_params=params(),
    )(*[pltpu.with_memory_space_constraint(a, pltpu.HBM) for a in (state, mass, ticks, levels, active)])
    got = lax.all_to_all(message, "x", 0, 0, tiled=True)
    got = lax.all_gather(got, "c", tiled=True)

    targets, keep = pl.pallas_call(
        sum_kernel,
        out_shape=[jax.ShapeDtypeStruct((z_count, 8, 128), f32), jax.ShapeDtypeStruct((16, 128), f32)],
        in_specs=vmem(1),
        out_specs=vmem(2),
        compiler_params=params(),
    )(got)
    targets = lax.all_to_all(targets, "z", 0, 0, tiled=True)

    partial = pl.pallas_call(
        force_kernel,
        out_shape=jax.ShapeDtypeStruct((z_count, 16, 128), f32),
        in_specs=vmem(3),
        out_specs=vmem(1)[0],
        scratch_shapes=[
            pltpu.VMEM((6, PER, 128), f32),
            pltpu.VMEM((32, GROUPS * TILES * 128), bf16),
            pltpu.VMEM((32, 4 * PER), f32),
        ],
        compiler_params=params(),
    )(targets, got, keep)
    partial = lax.all_to_all(partial, "z", 0, 0, tiled=True)

    updates = pl.pallas_call(
        lambda *refs: correct_kernel(1.0 / n_stars, *refs),
        out_shape=jax.ShapeDtypeStruct((y_count * X, 16, 128), f32),
        in_specs=vmem(2),
        out_specs=vmem(1)[0],
        compiler_params=params(),
    )(targets, partial)
    updates = lax.all_to_all(updates, ("x", "aa"), 0, 0, tiled=True)
    updates = lax.all_gather(updates, "c", tiled=True).reshape(GROUPS, y_count, 16, 128)

    new_active, new_state = pl.pallas_call(
        store_kernel,
        out_shape=[jax.ShapeDtypeStruct((12, 1280), f32), jax.ShapeDtypeStruct(state.shape, f32)],
        in_specs=vmem(5),
        out_specs=vmem(2),
        scratch_shapes=[
            pltpu.VMEM((256, 128), f32),
        ],
        compiler_params=params(),
    )(state, ticks, levels, active, updates)
    return new_active, new_state


def solution(mesh):
    shape = (mesh.shape["ja"] // GROUPS, X, C, mesh.shape["aa"])
    fine = Mesh(mesh.devices.reshape(shape), ("z", "x", "c", "aa"))
    ja = ("z", "x", "c")
    return jax.shard_map(
        per_device,
        mesh=fine,
        in_specs=(P(None, ja), P(ja), P(ja), P(ja), P()),
        out_specs=(P(None, "aa"), P(None, ja)),
        check_vma=False,
    )
```

```python
import jax
import jax.numpy as jnp
from jax import lax
from jax.experimental import pallas as pl
from jax.experimental.pallas import tpu as pltpu
from jax.sharding import Mesh, PartitionSpec as P

LEVELS = 5
EPS2 = 0.0001
H_MAX = 0.25
TICK = H_MAX / 2**LEVELS

X, C = 4, 2
GROUPS = X * C
TILES = 16
MAIN, TAIL = 128, 32
PER = MAIN + TAIL
FIELD = 8 * TILES
CHUNK = 512
ROWS = 16
BLOCKS = PER // ROWS

f32, bf16 = jnp.float32, jnp.bfloat16


def params():
    return pltpu.CompilerParams(vmem_limit_bytes=48 * 1024 * 1024)


def vmem(n):
    return [pl.BlockSpec(memory_space=pltpu.VMEM)] * n


def predict(pos, vel, acc, jerk, dt):
    predicted = pos + dt * (vel + dt * (0.5 * acc + dt * (jerk / 6.0)))
    predicted_vel = vel + dt * (acc + dt * (0.5 * jerk))
    return predicted, predicted_vel


def step_of(levels):
    return jnp.left_shift(jnp.ones_like(levels), LEVELS - levels).astype(f32) * TICK


def correct(pos, vel, old_acc, old_jerk, step, acc_new, jerk_new):
    error = old_acc - acc_new
    second = -6.0 * error - step * (4.0 * old_jerk + 2.0 * jerk_new)
    third = 12.0 * error + 6.0 * step * (old_jerk + jerk_new)
    fixed_pos = pos + step * step * (second / 24.0 + third / 120.0)
    fixed_vel = vel + step * (second / 6.0 + third / 24.0)
    return fixed_pos, fixed_vel


def split3(value):
    first = value.astype(bf16)
    rest = value - first.astype(f32)
    second = rest.astype(bf16)
    return first, second, (rest - second.astype(f32)).astype(bf16)


def pack(main, tail, spare=None):
    if spare is None:
        spare = jnp.zeros((1, TAIL), f32)
    last = jnp.concatenate([tail[0:1], tail[1:2], tail[2:3], spare], axis=1)
    return jnp.concatenate([main, last], axis=0)


def first_star():
    return ((lax.axis_index("z") * X + lax.axis_index("x")) * C + lax.axis_index("c")) * (TILES * 128)


def pick_kernel(*refs):
    given, msg_ref, table_ref, held, sems = refs[:5], refs[5], refs[6], refs[7:12], refs[12]
    copies = [pltpu.make_async_copy(a, b, sems.at[n]) for n, (a, b) in enumerate(zip(given, held))]
    for copy in copies:
        copy.start()
    for copy in copies:
        copy.wait()
    state_ref, mass_ref, ticks_ref, levels_ref, active_ref = held
    start = first_star()
    block = lax.axis_index("aa") * 10
    zero = jnp.zeros((1, 128), f32)
    for i in range(TILES):
        s = state_ref[:, i * 128 : (i + 1) * 128]
        dt = ticks_ref[i : i + 1, :].astype(f32) * TICK
        pos, vel = predict(s[0:3], s[3:6], s[6:9], s[9:12], dt)
        step = step_of(levels_ref[i : i + 1, :])
        field = jnp.concatenate([pos, vel, mass_ref[i : i + 1, :], zero], axis=0)
        both = jnp.concatenate([field, s[6:12], step, zero], axis=0)
        for n, part in enumerate(split3(both)):
            table_ref[n * 256 + i * 16 : n * 256 + (i + 1) * 16, :] = part
        for x in range(X):
            msg_ref[x, i * 8 : (i + 1) * 8, :] = field
    rows = lax.broadcasted_iota(jnp.int32, (128, 128), 0)
    picks = []
    for k in range(10):
        local = active_ref[pl.ds(block + k, 1), :] - start
        high = jnp.broadcast_to(jnp.right_shift(local, 7), (16, 128))
        low = jnp.bitwise_and(local, 127)
        chosen = jnp.where(rows == low, 1.0, 0.0).astype(bf16)
        found = jnp.dot(table_ref[...], chosen, preferred_element_type=f32)
        pick = jnp.zeros((16, 128), f32)
        for h in range(TILES):
            r = slice(h * 16, (h + 1) * 16)
            value = (found[0:256][r] + found[256:512][r]) + found[512:768][r]
            pick = jnp.where(high == h, value, pick)
        picks.append(pick)
    for g in range(GROUPS):
        main = picks[g]
        tail = picks[8 + g // 4][:, (g % 4) * TAIL : (g % 4 + 1) * TAIL]
        step = [main[14:15, n * TAIL : (n + 1) * TAIL] for n in range(4)]
        x, row = g % X, FIELD + 16 * (g // X)
        for n, q in enumerate((0, 3, 8, 11)):
            msg_ref[x, row + 4 * n : row + 4 * n + 4, :] = pack(main[q : q + 3], tail[q : q + 3], step[n])
        msg_ref[x, 8 * (g // X) + 7 : 8 * (g // X) + 8, :] = jnp.concatenate([tail[14:15], jnp.zeros((1, 96), f32)], axis=1)


def sum_kernel(got_ref, out_ref, keep_ref):
    c = lax.axis_index("c")
    picks = pl.ds(pl.multiple_of(FIELD + 16 * c, 16), 16)
    total = got_ref[0, picks, :]
    step = got_ref[0, pl.ds(8 * c + 7, 1), :]
    for g in range(1, GROUPS):
        total = total + got_ref[g, picks, :]
        step = step + got_ref[g, pl.ds(8 * c + 7, 1), :]
    for z in range(out_ref.shape[0]):
        out_ref[z] = total[0:8]
    keep_ref[0:8, :] = total[8:16]
    keep_ref[8:16, :] = jnp.broadcast_to(step, (8, 128))


def star_kernel(got_ref, weight_ref, cross_ref, center_ref):
    row = lax.broadcasted_iota(jnp.int32, (8, 128), 0)
    center = jnp.broadcast_to(jnp.mean(got_ref[0, 0:8, :], axis=1, keepdims=True), (8, 128))
    center = jnp.where(row < 6, center, 0.0)
    center_ref[...] = center

    def group(g, _):
        for i in range(TILES):
            lanes = pl.ds(pl.multiple_of((g * TILES + i) * 128, 128), 128)
            tile = got_ref[g, i * 8 : (i + 1) * 8, :]
            value = jnp.where(row < 6, tile * tile[6:7], jnp.where(row == 6, tile, 0.0))
            first = value.astype(bf16).astype(f32)
            rest = value - first
            second = rest.astype(bf16).astype(f32)
            weight_ref[:, lanes] = jnp.concatenate([first, second, rest - second, rest - rest], axis=0).astype(bf16)
            tile = tile - center
            dot = jnp.sum(tile[0:3] * tile[3:6], axis=0, keepdims=True)
            value = jnp.where(row < 6, tile, jnp.where(row == 6, 1.0, dot))
            first = value.astype(bf16).astype(f32)
            rest = value - first
            second = rest.astype(bf16).astype(f32)
            third = rest - second
            cross_ref[:, lanes] = jnp.concatenate(
                [first, second, first, second, third, first, third, second], axis=0
            ).astype(bf16)
        return 0

    lax.fori_loop(0, GROUPS, group, 0)


def target_rows(pos, vel, center):
    pos, vel = pos - center[0:3, 0:1], vel - center[3:6, 0:1]
    value = jnp.concatenate([-vel, -pos, jnp.sum(pos * vel, axis=0, keepdims=True), jnp.ones_like(pos[0:1])], axis=0)
    first = value.astype(bf16).astype(f32)
    rest = value - first
    second = rest.astype(bf16).astype(f32)
    third = rest - second
    return jnp.transpose(jnp.concatenate([first, first, second, second, first, third, second, third], axis=0)).astype(bf16)


def force_kernel(targets_ref, got_ref, keep_ref, weight_ref, cross_ref, center_ref, out_ref, seen_ref, left_ref, sums_ref):
    target = targets_ref[0]
    for z in range(1, targets_ref.shape[0]):
        target = target + targets_ref[z]
    columns = jnp.transpose(target)
    for q in range(3):
        seen_ref[q, 0:MAIN, :] = jnp.broadcast_to(columns[:, q : q + 1], (MAIN, 128))
        seen_ref[q, MAIN:PER, :] = jnp.broadcast_to(columns[q * TAIL : (q + 1) * TAIL, 3:4], (TAIL, 128))
    tails = [
        jnp.concatenate([target[r : r + 1, q * TAIL : (q + 1) * TAIL] for q in range(3)], axis=0) for r in (3, 7)
    ]
    left_ref[0:MAIN, :] = target_rows(target[0:3], target[4:7], center_ref[...])
    left_ref[MAIN:PER, :] = target_rows(tails[0], tails[1], center_ref[...])
    sums_ref[...] = jnp.zeros_like(sums_ref)

    def chunk(n, _):
        g, part = n // (TILES * 128 // CHUNK), n % (TILES * 128 // CHUNK)
        base = pl.multiple_of(part * (CHUNK // 16), 8)
        across = CHUNK // 128
        star = [
            jnp.concatenate(
                [jnp.broadcast_to(got_ref[g, pl.ds(base + j * 8 + q, 1), :], (ROWS, 128)) for j in range(across)], axis=1
            )
            for q in range(3)
        ]
        lanes = pl.ds(pl.multiple_of(n * CHUNK, CHUNK), CHUNK)
        weight = weight_ref[:, lanes]
        alongs = jnp.dot(left_ref[...], cross_ref[:, lanes], preferred_element_type=f32)
        values = []
        for b in range(BLOCKS):
            r = slice(b * ROWS, (b + 1) * ROWS)
            dx, dy, dz = [star[q] - jnp.concatenate([seen_ref[q, r, :]] * across, axis=1) for q in range(3)]
            total = (dx * dx + EPS2) + dy * dy + dz * dz
            along = alongs[r]
            inverse = lax.rsqrt(total)
            square = inverse * inverse
            cube = square * inverse
            rate = cube * (square * along)
            for value in (cube, rate):
                high = value.astype(bf16)
                values += [high, (value - high.astype(f32)).astype(bf16)]
            if (b + 1) * 4 * ROWS % 256 == 0 or b == BLOCKS - 1:
                right = jnp.concatenate(values, axis=0)
                values = []
                end = (b + 1) * 4 * ROWS
                sums_ref[:, end - right.shape[0] : end] += lax.dot_general(
                    weight, right, (((1,), (1,)), ((), ())), preferred_element_type=f32
                )
        return 0

    lax.fori_loop(0, GROUPS * TILES * 128 // CHUNK, chunk, 0, unroll=4)
    sums = jnp.transpose(sums_ref[...])

    def columns_of(part):
        total = jnp.concatenate(
            [
                sums[b * 4 * ROWS + part * ROWS : b * 4 * ROWS + (part + 1) * ROWS]
                + sums[b * 4 * ROWS + (part + 1) * ROWS : b * 4 * ROWS + (part + 2) * ROWS]
                for b in range(BLOCKS)
            ],
            axis=0,
        )
        main = jnp.transpose(total[0:MAIN])
        tail = jnp.transpose(total[MAIN:PER])
        return main[0:8] + main[8:16] + main[16:24], tail[0:8] + tail[8:16] + tail[16:24]

    def three(value):
        return jnp.concatenate([value, value, value], axis=0)

    main, tail = columns_of(0)
    cube_pos = pack(main[0:3], tail[0:3])
    cube_vel = pack(main[3:6], tail[3:6])
    cube_one = pack(three(main[6:7]), three(tail[6:7]))
    main, tail = columns_of(2)
    rate_pos = pack(main[0:3], tail[0:3])
    rate_one = pack(three(main[6:7]), three(tail[6:7]))
    acc = cube_pos - target[0:4] * cube_one
    jerk = (cube_vel - target[4:8] * cube_one) - 3.0 * (rate_pos - target[0:4] * rate_one)
    last = jnp.concatenate([acc[3:4, 0:96], keep_ref[8:9, 0:TAIL]], axis=1)
    forces = jnp.concatenate([acc[0:3], last, jerk], axis=0)
    for z in range(out_ref.shape[0]):
        out_ref[z, 0:8, :] = forces
        out_ref[z, 8:16, :] = keep_ref[0:8, :]


def correct_kernel(scale, targets_ref, got_ref, out_ref):
    target = targets_ref[0]
    total = got_ref[0]
    for z in range(1, targets_ref.shape[0]):
        target = target + targets_ref[z]
        total = total + got_ref[z]
    forces = total[0:8] * scale
    old = total[8:16]
    main = jnp.concatenate([a[r : r + 1, 96:128] for a in (target, old) for r in (3, 7)], axis=1)
    tail = total[3:4, 96:128]
    step = pack(jnp.concatenate([main, main, main], axis=0), jnp.concatenate([tail, tail, tail], axis=0))
    pos, vel = correct(target[0:4], target[4:8], old[0:4], old[4:8], step, forces[0:4], forces[4:8])
    both = jnp.concatenate([pos, vel], axis=0)
    for d in range(out_ref.shape[0]):
        out_ref[d, 0:8, :] = forces
        out_ref[d, 8:16, :] = both


def store_kernel(state_ref, ticks_ref, levels_ref, active_ref, got_ref, new_active_ref, new_state_ref, sums_ref):
    start = first_star()
    mine = lax.axis_index("aa")

    def tails(c, y, row):
        parts = [got_ref[c * X + x, y, row : row + 1, :] for x in range(X)]
        return jnp.concatenate(
            [jnp.concatenate([p[:, q * TAIL : (q + 1) * TAIL] for p in parts], axis=1) for q in range(3)], axis=0
        )

    for c in range(C):
        for x in range(X):
            lanes = slice((c * X + x) * 128, (c * X + x + 1) * 128)
            tile = got_ref[c * X + x, mine]
            new_active_ref[0:3, lanes] = tile[8:11]
            new_active_ref[3:6, lanes] = tile[12:15]
            new_active_ref[6:9, lanes] = tile[0:3]
            new_active_ref[9:12, lanes] = tile[4:7]
        lanes = slice(1024 + c * 128, 1024 + (c + 1) * 128)
        new_active_ref[0:3, lanes] = tails(c, mine, 11)
        new_active_ref[3:6, lanes] = tails(c, mine, 15)
        new_active_ref[6:9, lanes] = tails(c, mine, 3)
        new_active_ref[9:12, lanes] = tails(c, mine, 7)

    row8 = lax.broadcasted_iota(jnp.int32, (8, 128), 0)
    rows = lax.broadcasted_iota(jnp.int32, (128, 128), 0)
    one = jnp.ones((1, 128), f32)
    sums_ref[...] = jnp.zeros_like(sums_ref)

    def block(y, _):
        tiles = [jnp.where(row8 == 3, 1.0, got_ref[c * X + x, y, 0:8, :]) for c in range(C) for x in range(X)]
        for c in range(C):
            tiles.append(jnp.concatenate([tails(c, y, 3), one, tails(c, y, 7), one], axis=0))
        lefts, lows = [], []
        for k, tile in enumerate(tiles):
            local = active_ref[pl.ds(y * 10 + k, 1), :] - start
            high = jnp.broadcast_to(jnp.right_shift(local, 7), (16, 128))
            lows.append(jnp.where(rows == jnp.bitwise_and(local, 127), 1.0, 0.0).astype(bf16))
            first = tile.astype(bf16).astype(f32)
            both = jnp.concatenate([first, tile - first], axis=0)
            lefts.append(jnp.concatenate([jnp.where(high == h, both, 0.0).astype(bf16) for h in range(TILES)], axis=0))
        total = lax.dot_general(
            jnp.concatenate(lefts, axis=1),
            jnp.concatenate(lows, axis=1),
            (((1,), (1,)), ((), ())),
            preferred_element_type=f32,
        )
        sums_ref[...] += total
        return 0

    lax.fori_loop(0, got_ref.shape[1], block, 0, unroll=4)

    for i in range(TILES):
        lanes = slice(i * 128, (i + 1) * 128)
        s = state_ref[:, lanes]
        forces = sums_ref[i * 16 : i * 16 + 8, :] + sums_ref[i * 16 + 8 : i * 16 + 16, :]
        acc, jerk, hit = forces[0:3], forces[4:7], forces[3:4] > 0.5
        dt = ticks_ref[i : i + 1, :].astype(f32) * TICK
        step = step_of(levels_ref[i : i + 1, :])
        pos, vel = predict(s[0:3], s[3:6], s[6:9], s[9:12], dt)
        pos, vel = correct(pos, vel, s[6:9], s[9:12], step, acc, jerk)
        new = jnp.concatenate([pos, vel, acc, jerk], axis=0)
        new_state_ref[:, lanes] = jnp.where(hit, new, s)


def per_device(state, mass, levels, ticks, active):
    z_count, y_count = lax.axis_size("z"), lax.axis_size("aa")
    n_stars = state.shape[1] * z_count * GROUPS
    mass, levels, ticks = [a.reshape(TILES, 128) for a in (mass, levels, ticks)]
    active = active.reshape(-1, 128)

    message = pl.pallas_call(
        pick_kernel,
        out_shape=jax.ShapeDtypeStruct((X, FIELD + 16 * C, 128), f32),
        in_specs=[pl.BlockSpec(memory_space=pltpu.HBM)] * 5,
        out_specs=vmem(1)[0],
        scratch_shapes=[pltpu.VMEM((768, 128), bf16)]
        + [pltpu.VMEM(a.shape, a.dtype) for a in (state, mass, ticks, levels, active)]
        + [pltpu.SemaphoreType.DMA((5,))],
        compiler_params=params(),
    )(*[pltpu.with_memory_space_constraint(a, pltpu.HBM) for a in (state, mass, ticks, levels, active)])
    got = lax.all_to_all(message, "x", 0, 0, tiled=True)
    got = lax.all_gather(got, "c", tiled=True)

    targets, keep = pl.pallas_call(
        sum_kernel,
        out_shape=[jax.ShapeDtypeStruct((z_count, 8, 128), f32), jax.ShapeDtypeStruct((16, 128), f32)],
        in_specs=vmem(1),
        out_specs=vmem(2),
        compiler_params=params(),
    )(got)
    targets = lax.all_to_all(targets, "z", 0, 0, tiled=True)

    n_field = GROUPS * TILES * 128
    stars = pl.pallas_call(
        star_kernel,
        out_shape=[
            jax.ShapeDtypeStruct((32, n_field), bf16),
            jax.ShapeDtypeStruct((64, n_field), bf16),
            jax.ShapeDtypeStruct((8, 128), f32),
        ],
        in_specs=vmem(1),
        out_specs=vmem(3),
        compiler_params=params(),
        cost_estimate=pl.CostEstimate(flops=n_field * 400, bytes_accessed=n_field * 224, transcendentals=0),
    )(got)

    partial = pl.pallas_call(
        force_kernel,
        out_shape=jax.ShapeDtypeStruct((z_count, 16, 128), f32),
        in_specs=vmem(6),
        out_specs=vmem(1)[0],
        scratch_shapes=[
            pltpu.VMEM((3, PER, 128), f32),
            pltpu.VMEM((PER, 64), bf16),
            pltpu.VMEM((32, 4 * PER), f32),
        ],
        compiler_params=params(),
    )(targets, got, keep, *stars)
    partial = lax.all_to_all(partial, "z", 0, 0, tiled=True)

    updates = pl.pallas_call(
        lambda *refs: correct_kernel(1.0 / n_stars, *refs),
        out_shape=jax.ShapeDtypeStruct((y_count * X, 16, 128), f32),
        in_specs=vmem(2),
        out_specs=vmem(1)[0],
        compiler_params=params(),
    )(targets, partial)
    updates = lax.all_to_all(updates, ("x", "aa"), 0, 0, tiled=True)
    updates = lax.all_gather(updates, "c", tiled=True).reshape(GROUPS, y_count, 16, 128)

    new_active, new_state = pl.pallas_call(
        store_kernel,
        out_shape=[jax.ShapeDtypeStruct((12, 1280), f32), jax.ShapeDtypeStruct(state.shape, f32)],
        in_specs=vmem(5),
        out_specs=vmem(2),
        scratch_shapes=[
            pltpu.VMEM((256, 128), f32),
        ],
        compiler_params=params(),
    )(state, ticks, levels, active, updates)
    return new_active, new_state


def solution(mesh):
    shape = (mesh.shape["ja"] // GROUPS, X, C, mesh.shape["aa"])
    fine = Mesh(mesh.devices.reshape(shape), ("z", "x", "c", "aa"))
    ja = ("z", "x", "c")
    return jax.shard_map(
        per_device,
        mesh=fine,
        in_specs=(P(None, ja), P(ja), P(ja), P(ja), P()),
        out_specs=(P(None, "aa"), P(None, ja)),
        check_vma=False,
    )
```

```python
import jax
import jax.numpy as jnp
from jax import lax
from jax.experimental import pallas as pl
from jax.experimental.pallas import tpu as pltpu
from jax.sharding import Mesh, PartitionSpec as P

LEVELS = 5
EPS2 = 0.0001
H_MAX = 0.25
TICK = H_MAX / 2**LEVELS

X, C = 4, 2
GROUPS = X * C
TILES = 16
MAIN, TAIL = 128, 32
PER = MAIN + TAIL
FIELD = 8 * TILES
CHUNK = 1024
ROWS = 16
BLOCKS = PER // ROWS
CROSSED = 8
UNROLL = 8

f32, bf16 = jnp.float32, jnp.bfloat16


def params():
    return pltpu.CompilerParams(vmem_limit_bytes=48 * 1024 * 1024)


def vmem(n):
    return [pl.BlockSpec(memory_space=pltpu.VMEM)] * n


def predict(pos, vel, acc, jerk, dt):
    predicted = pos + dt * (vel + dt * (0.5 * acc + dt * (jerk / 6.0)))
    predicted_vel = vel + dt * (acc + dt * (0.5 * jerk))
    return predicted, predicted_vel


def step_of(levels):
    return jnp.left_shift(jnp.ones_like(levels), LEVELS - levels).astype(f32) * TICK


def correct(pos, vel, old_acc, old_jerk, step, acc_new, jerk_new):
    error = old_acc - acc_new
    second = -6.0 * error - step * (4.0 * old_jerk + 2.0 * jerk_new)
    third = 12.0 * error + 6.0 * step * (old_jerk + jerk_new)
    fixed_pos = pos + step * step * (second / 24.0 + third / 120.0)
    fixed_vel = vel + step * (second / 6.0 + third / 24.0)
    return fixed_pos, fixed_vel


def split3(value):
    first = value.astype(bf16)
    rest = value - first.astype(f32)
    second = rest.astype(bf16)
    return first, second, (rest - second.astype(f32)).astype(bf16)


def pack(main, tail, spare=None):
    if spare is None:
        spare = jnp.zeros((1, TAIL), f32)
    last = jnp.concatenate([tail[0:1], tail[1:2], tail[2:3], spare], axis=1)
    return jnp.concatenate([main, last], axis=0)


def first_star():
    return ((lax.axis_index("z") * X + lax.axis_index("x")) * C + lax.axis_index("c")) * (TILES * 128)


def pick_kernel(*refs):
    given, msg_ref, table_ref, held, sems = refs[:5], refs[5], refs[6], refs[7:12], refs[12]
    copies = [pltpu.make_async_copy(a, b, sems.at[n]) for n, (a, b) in enumerate(zip(given, held))]
    for copy in copies:
        copy.start()
    for copy in copies:
        copy.wait()
    state_ref, mass_ref, ticks_ref, levels_ref, active_ref = held
    start = first_star()
    block = lax.axis_index("aa") * 10
    zero = jnp.zeros((1, 128), f32)
    for i in range(TILES):
        s = state_ref[:, i * 128 : (i + 1) * 128]
        dt = ticks_ref[i : i + 1, :].astype(f32) * TICK
        pos, vel = predict(s[0:3], s[3:6], s[6:9], s[9:12], dt)
        step = step_of(levels_ref[i : i + 1, :])
        field = jnp.concatenate([pos, vel, mass_ref[i : i + 1, :], zero], axis=0)
        both = jnp.concatenate([field, s[6:12], step, zero], axis=0)
        for n, part in enumerate(split3(both)):
            table_ref[n * 256 + i * 16 : n * 256 + (i + 1) * 16, :] = part
        for x in range(X):
            msg_ref[x, i * 8 : (i + 1) * 8, :] = field
    rows = lax.broadcasted_iota(jnp.int32, (128, 128), 0)
    picks = []
    for k in range(10):
        local = active_ref[pl.ds(block + k, 1), :] - start
        high = jnp.broadcast_to(jnp.right_shift(local, 7), (16, 128))
        low = jnp.bitwise_and(local, 127)
        chosen = jnp.where(rows == low, 1.0, 0.0).astype(bf16)
        found = jnp.dot(table_ref[...], chosen, preferred_element_type=f32)
        pick = jnp.zeros((16, 128), f32)
        for h in range(TILES):
            r = slice(h * 16, (h + 1) * 16)
            value = (found[0:256][r] + found[256:512][r]) + found[512:768][r]
            pick = jnp.where(high == h, value, pick)
        picks.append(pick)
    for g in range(GROUPS):
        main = picks[g]
        tail = picks[8 + g // 4][:, (g % 4) * TAIL : (g % 4 + 1) * TAIL]
        step = [main[14:15, n * TAIL : (n + 1) * TAIL] for n in range(4)]
        x, row = g % X, FIELD + 16 * (g // X)
        for n, q in enumerate((0, 3, 8, 11)):
            msg_ref[x, row + 4 * n : row + 4 * n + 4, :] = pack(main[q : q + 3], tail[q : q + 3], step[n])
        msg_ref[x, 8 * (g // X) + 7 : 8 * (g // X) + 8, :] = jnp.concatenate([tail[14:15], jnp.zeros((1, 96), f32)], axis=1)


def sum_kernel(got_ref, out_ref, keep_ref):
    c = lax.axis_index("c")
    picks = pl.ds(pl.multiple_of(FIELD + 16 * c, 16), 16)
    total = got_ref[0, picks, :]
    step = got_ref[0, pl.ds(8 * c + 7, 1), :]
    for g in range(1, GROUPS):
        total = total + got_ref[g, picks, :]
        step = step + got_ref[g, pl.ds(8 * c + 7, 1), :]
    for z in range(out_ref.shape[0]):
        out_ref[z] = total[0:8]
    keep_ref[0:8, :] = total[8:16]
    keep_ref[8:16, :] = jnp.broadcast_to(step, (8, 128))


def weight_rows(tile, row):
    value = jnp.where(row < 6, tile * tile[6:7], jnp.where(row == 6, tile, 0.0))
    first = value.astype(bf16).astype(f32)
    rest = value - first
    second = rest.astype(bf16).astype(f32)
    return jnp.concatenate([first, second, rest - second, jnp.zeros_like(value)], axis=0).astype(bf16)


def cross_rows(tile, row, center):
    tile = tile - center
    dot = jnp.sum(tile[0:3] * tile[3:6], axis=0, keepdims=True)
    value = jnp.where(row < 6, tile, jnp.where(row == 6, 1.0, dot))
    first = value.astype(bf16).astype(f32)
    rest = value - first
    second = rest.astype(bf16).astype(f32)
    third = rest - second
    return jnp.concatenate([first, second, first, second, third, first, third, second], axis=0).astype(bf16)


def target_rows(pos, vel, center):
    pos, vel = pos - center[0:3, 0:1], vel - center[3:6, 0:1]
    value = jnp.concatenate([-vel, -pos, jnp.sum(pos * vel, axis=0, keepdims=True), jnp.ones_like(pos[0:1])], axis=0)
    first = value.astype(bf16).astype(f32)
    rest = value - first
    second = rest.astype(bf16).astype(f32)
    third = rest - second
    return jnp.transpose(jnp.concatenate([first, first, second, second, first, third, second, third], axis=0)).astype(bf16)


def force_kernel(targets_ref, got_ref, keep_ref, out_ref, seen_ref, left_ref, along_ref, sums_ref):
    target = targets_ref[0]
    for z in range(1, targets_ref.shape[0]):
        target = target + targets_ref[z]
    columns = jnp.transpose(target)
    for half in range(2):
        for q in range(3):
            seen_ref[half * 3 + q, 0:MAIN, :] = jnp.broadcast_to(columns[:, half * 4 + q : half * 4 + q + 1], (MAIN, 128))
            seen_ref[half * 3 + q, MAIN:PER, :] = jnp.broadcast_to(
                columns[q * TAIL : (q + 1) * TAIL, half * 4 + 3 : half * 4 + 4], (TAIL, 128)
            )
    row = lax.broadcasted_iota(jnp.int32, (8, 128), 0)
    center = jnp.broadcast_to(jnp.mean(got_ref[0, 0:8, :], axis=1, keepdims=True), (8, 128))
    center = jnp.where(row < 6, center, 0.0)
    left_ref[...] = target_rows(target[0:3], target[4:7], center)[0 : CROSSED * ROWS]
    sums_ref[...] = jnp.zeros_like(sums_ref)

    across = CHUNK // 128
    chunks = GROUPS * TILES // across

    def tiles_of(n):
        g, part = n // (TILES // across), n % (TILES // across)
        return g, pl.multiple_of(part * (CHUNK // 16), 8)

    def cross(n, slot):
        g, base = tiles_of(n)
        right = [cross_rows(got_ref[g, pl.ds(base + j * 8, 8), :], row, center) for j in range(across)]
        along_ref[slot] = jnp.dot(left_ref[...], jnp.concatenate(right, axis=1), preferred_element_type=f32)

    def chunk(n, slot):
        g, base = tiles_of(n)
        star = [
            jnp.concatenate(
                [jnp.broadcast_to(got_ref[g, pl.ds(base + j * 8 + q, 1), :], (ROWS, 128)) for j in range(across)], axis=1
            )
            for q in range(6)
        ]
        weight = jnp.concatenate(
            [weight_rows(got_ref[g, pl.ds(base + j * 8, 8), :], row) for j in range(across)], axis=1
        )
        values = []
        for b in range(BLOCKS):
            r = slice(b * ROWS, (b + 1) * ROWS)
            needed = 3 if b < CROSSED else 6
            apart = [star[q] - jnp.concatenate([seen_ref[q, r, :]] * across, axis=1) for q in range(needed)]
            dx, dy, dz = apart[0:3]
            total = (dx * dx + EPS2) + dy * dy + dz * dz
            if b < CROSSED:
                along = along_ref[slot, r, :]
            else:
                wx, wy, wz = apart[3:6]
                along = dx * wx + dy * wy + dz * wz
            inverse = lax.rsqrt(total)
            square = inverse * inverse
            cube = square * inverse
            rate = cube * (square * along)
            for value in (cube, rate):
                high = value.astype(bf16)
                values += [high, (value - high.astype(f32)).astype(bf16)]
            if (b + 1) * 4 * ROWS % 256 == 0 or b == BLOCKS - 1:
                right = jnp.concatenate(values, axis=0)
                values = []
                end = (b + 1) * 4 * ROWS
                sums_ref[:, end - right.shape[0] : end] += lax.dot_general(
                    weight, right, (((1,), (1,)), ((), ())), preferred_element_type=f32
                )

    cross(0, 0)

    def body(n, _):
        for u in range(UNROLL):
            cross(jnp.minimum(n * UNROLL + u + 1, chunks - 1), (u + 1) % 2)
            chunk(n * UNROLL + u, u % 2)
        return 0

    lax.fori_loop(0, chunks // UNROLL, body, 0)
    sums = jnp.transpose(sums_ref[...])

    def columns_of(part):
        total = jnp.concatenate(
            [
                sums[b * 4 * ROWS + part * ROWS : b * 4 * ROWS + (part + 1) * ROWS]
                + sums[b * 4 * ROWS + (part + 1) * ROWS : b * 4 * ROWS + (part + 2) * ROWS]
                for b in range(BLOCKS)
            ],
            axis=0,
        )
        main = jnp.transpose(total[0:MAIN])
        tail = jnp.transpose(total[MAIN:PER])
        return main[0:8] + main[8:16] + main[16:24], tail[0:8] + tail[8:16] + tail[16:24]

    def three(value):
        return jnp.concatenate([value, value, value], axis=0)

    main, tail = columns_of(0)
    cube_pos = pack(main[0:3], tail[0:3])
    cube_vel = pack(main[3:6], tail[3:6])
    cube_one = pack(three(main[6:7]), three(tail[6:7]))
    main, tail = columns_of(2)
    rate_pos = pack(main[0:3], tail[0:3])
    rate_one = pack(three(main[6:7]), three(tail[6:7]))
    acc = cube_pos - target[0:4] * cube_one
    jerk = (cube_vel - target[4:8] * cube_one) - 3.0 * (rate_pos - target[0:4] * rate_one)
    last = jnp.concatenate([acc[3:4, 0:96], keep_ref[8:9, 0:TAIL]], axis=1)
    forces = jnp.concatenate([acc[0:3], last, jerk], axis=0)
    for z in range(out_ref.shape[0]):
        out_ref[z, 0:8, :] = forces
        out_ref[z, 8:16, :] = keep_ref[0:8, :]


def correct_kernel(scale, targets_ref, got_ref, out_ref):
    target = targets_ref[0]
    total = got_ref[0]
    for z in range(1, targets_ref.shape[0]):
        target = target + targets_ref[z]
        total = total + got_ref[z]
    forces = total[0:8] * scale
    old = total[8:16]
    main = jnp.concatenate([a[r : r + 1, 96:128] for a in (target, old) for r in (3, 7)], axis=1)
    tail = total[3:4, 96:128]
    step = pack(jnp.concatenate([main, main, main], axis=0), jnp.concatenate([tail, tail, tail], axis=0))
    pos, vel = correct(target[0:4], target[4:8], old[0:4], old[4:8], step, forces[0:4], forces[4:8])
    both = jnp.concatenate([pos, vel], axis=0)
    for d in range(out_ref.shape[0]):
        out_ref[d, 0:8, :] = forces
        out_ref[d, 8:16, :] = both


def store_kernel(state_ref, ticks_ref, levels_ref, active_ref, got_ref, new_active_ref, new_state_ref, sums_ref):
    start = first_star()
    mine = lax.axis_index("aa")

    def tails(c, y, row):
        parts = [got_ref[c * X + x, y, row : row + 1, :] for x in range(X)]
        return jnp.concatenate(
            [jnp.concatenate([p[:, q * TAIL : (q + 1) * TAIL] for p in parts], axis=1) for q in range(3)], axis=0
        )

    for c in range(C):
        for x in range(X):
            lanes = slice((c * X + x) * 128, (c * X + x + 1) * 128)
            tile = got_ref[c * X + x, mine]
            new_active_ref[0:3, lanes] = tile[8:11]
            new_active_ref[3:6, lanes] = tile[12:15]
            new_active_ref[6:9, lanes] = tile[0:3]
            new_active_ref[9:12, lanes] = tile[4:7]
        lanes = slice(1024 + c * 128, 1024 + (c + 1) * 128)
        new_active_ref[0:3, lanes] = tails(c, mine, 11)
        new_active_ref[3:6, lanes] = tails(c, mine, 15)
        new_active_ref[6:9, lanes] = tails(c, mine, 3)
        new_active_ref[9:12, lanes] = tails(c, mine, 7)

    row8 = lax.broadcasted_iota(jnp.int32, (8, 128), 0)
    rows = lax.broadcasted_iota(jnp.int32, (128, 128), 0)
    one = jnp.ones((1, 128), f32)
    sums_ref[...] = jnp.zeros_like(sums_ref)

    def block(y, _):
        tiles = [jnp.where(row8 == 3, 1.0, got_ref[c * X + x, y, 0:8, :]) for c in range(C) for x in range(X)]
        for c in range(C):
            tiles.append(jnp.concatenate([tails(c, y, 3), one, tails(c, y, 7), one], axis=0))
        lefts, lows = [], []
        for k, tile in enumerate(tiles):
            local = active_ref[pl.ds(y * 10 + k, 1), :] - start
            high = jnp.broadcast_to(jnp.right_shift(local, 7), (16, 128))
            lows.append(jnp.where(rows == jnp.bitwise_and(local, 127), 1.0, 0.0).astype(bf16))
            first = tile.astype(bf16).astype(f32)
            both = jnp.concatenate([first, tile - first], axis=0)
            lefts.append(jnp.concatenate([jnp.where(high == h, both, 0.0).astype(bf16) for h in range(TILES)], axis=0))
        total = lax.dot_general(
            jnp.concatenate(lefts, axis=1),
            jnp.concatenate(lows, axis=1),
            (((1,), (1,)), ((), ())),
            preferred_element_type=f32,
        )
        sums_ref[...] += total
        return 0

    lax.fori_loop(0, got_ref.shape[1], block, 0, unroll=4)

    for i in range(TILES):
        lanes = slice(i * 128, (i + 1) * 128)
        s = state_ref[:, lanes]
        forces = sums_ref[i * 16 : i * 16 + 8, :] + sums_ref[i * 16 + 8 : i * 16 + 16, :]
        acc, jerk, hit = forces[0:3], forces[4:7], forces[3:4] > 0.5
        dt = ticks_ref[i : i + 1, :].astype(f32) * TICK
        step = step_of(levels_ref[i : i + 1, :])
        pos, vel = predict(s[0:3], s[3:6], s[6:9], s[9:12], dt)
        pos, vel = correct(pos, vel, s[6:9], s[9:12], step, acc, jerk)
        new = jnp.concatenate([pos, vel, acc, jerk], axis=0)
        new_state_ref[:, lanes] = jnp.where(hit, new, s)


def per_device(state, mass, levels, ticks, active):
    z_count, y_count = lax.axis_size("z"), lax.axis_size("aa")
    n_stars = state.shape[1] * z_count * GROUPS
    mass, levels, ticks = [a.reshape(TILES, 128) for a in (mass, levels, ticks)]
    active = active.reshape(-1, 128)

    message = pl.pallas_call(
        pick_kernel,
        out_shape=jax.ShapeDtypeStruct((X, FIELD + 16 * C, 128), f32),
        in_specs=[pl.BlockSpec(memory_space=pltpu.HBM)] * 5,
        out_specs=vmem(1)[0],
        scratch_shapes=[pltpu.VMEM((768, 128), bf16)]
        + [pltpu.VMEM(a.shape, a.dtype) for a in (state, mass, ticks, levels, active)]
        + [pltpu.SemaphoreType.DMA((5,))],
        compiler_params=params(),
    )(*[pltpu.with_memory_space_constraint(a, pltpu.HBM) for a in (state, mass, ticks, levels, active)])
    got = lax.all_to_all(message, "x", 0, 0, tiled=True)
    got = lax.all_gather(got, "c", tiled=True)

    targets, keep = pl.pallas_call(
        sum_kernel,
        out_shape=[jax.ShapeDtypeStruct((z_count, 8, 128), f32), jax.ShapeDtypeStruct((16, 128), f32)],
        in_specs=vmem(1),
        out_specs=vmem(2),
        compiler_params=params(),
    )(got)
    targets = lax.all_to_all(targets, "z", 0, 0, tiled=True)

    partial = pl.pallas_call(
        force_kernel,
        out_shape=jax.ShapeDtypeStruct((z_count, 16, 128), f32),
        in_specs=vmem(3),
        out_specs=vmem(1)[0],
        scratch_shapes=[
            pltpu.VMEM((6, PER, 128), f32),
            pltpu.VMEM((CROSSED * ROWS, 64), bf16),
            pltpu.VMEM((2, CROSSED * ROWS, CHUNK), f32),
            pltpu.VMEM((32, 4 * PER), f32),
        ],
        compiler_params=params(),
    )(targets, got, keep)
    partial = lax.all_to_all(partial, "z", 0, 0, tiled=True)

    updates = pl.pallas_call(
        lambda *refs: correct_kernel(1.0 / n_stars, *refs),
        out_shape=jax.ShapeDtypeStruct((y_count * X, 16, 128), f32),
        in_specs=vmem(2),
        out_specs=vmem(1)[0],
        compiler_params=params(),
    )(targets, partial)
    updates = lax.all_to_all(updates, ("x", "aa"), 0, 0, tiled=True)
    updates = lax.all_gather(updates, "c", tiled=True).reshape(GROUPS, y_count, 16, 128)

    new_active, new_state = pl.pallas_call(
        store_kernel,
        out_shape=[jax.ShapeDtypeStruct((12, 1280), f32), jax.ShapeDtypeStruct(state.shape, f32)],
        in_specs=vmem(5),
        out_specs=vmem(2),
        scratch_shapes=[
            pltpu.VMEM((256, 128), f32),
        ],
        compiler_params=params(),
    )(state, ticks, levels, active, updates)
    return new_active, new_state


def solution(mesh):
    shape = (mesh.shape["ja"] // GROUPS, X, C, mesh.shape["aa"])
    fine = Mesh(mesh.devices.reshape(shape), ("z", "x", "c", "aa"))
    ja = ("z", "x", "c")
    return jax.shard_map(
        per_device,
        mesh=fine,
        in_specs=(P(None, ja), P(ja), P(ja), P(ja), P()),
        out_specs=(P(None, "aa"), P(None, ja)),
        check_vma=False,
    )
```

```python
import jax
import jax.numpy as jnp
from jax import lax
from jax.experimental import pallas as pl
from jax.experimental.pallas import tpu as pltpu
from jax.sharding import Mesh, PartitionSpec as P

LEVELS = 5
EPS2 = 0.0001
H_MAX = 0.25
TICK = H_MAX / 2**LEVELS

X, C = 4, 2
GROUPS = X * C
TILES = 16
MAIN, TAIL = 128, 32
PER = MAIN + TAIL
FIELD = 8 * TILES
CHUNK = 1024
ROWS = 16
BLOCKS = PER // ROWS
CROSSED = MAIN // ROWS
UNROLL = 8

f32, bf16 = jnp.float32, jnp.bfloat16


def params():
    return pltpu.CompilerParams(vmem_limit_bytes=48 * 1024 * 1024)


def vmem(n):
    return [pl.BlockSpec(memory_space=pltpu.VMEM)] * n


def predict(pos, vel, acc, jerk, dt):
    predicted = pos + dt * (vel + dt * (0.5 * acc + dt * (jerk / 6.0)))
    predicted_vel = vel + dt * (acc + dt * (0.5 * jerk))
    return predicted, predicted_vel


def step_of(levels):
    return jnp.left_shift(jnp.ones_like(levels), LEVELS - levels).astype(f32) * TICK


def correct(pos, vel, old_acc, old_jerk, step, acc_new, jerk_new):
    error = old_acc - acc_new
    second = -6.0 * error - step * (4.0 * old_jerk + 2.0 * jerk_new)
    third = 12.0 * error + 6.0 * step * (old_jerk + jerk_new)
    fixed_pos = pos + step * step * (second / 24.0 + third / 120.0)
    fixed_vel = vel + step * (second / 6.0 + third / 24.0)
    return fixed_pos, fixed_vel


def split3(value):
    first = value.astype(bf16)
    rest = value - first.astype(f32)
    second = rest.astype(bf16)
    return first, second, (rest - second.astype(f32)).astype(bf16)


def pack(main, tail, spare=None):
    if spare is None:
        spare = jnp.zeros((1, TAIL), f32)
    last = jnp.concatenate([tail[0:1], tail[1:2], tail[2:3], spare], axis=1)
    return jnp.concatenate([main, last], axis=0)


def first_star():
    return ((lax.axis_index("z") * X + lax.axis_index("x")) * C + lax.axis_index("c")) * (TILES * 128)


def pick_kernel(*refs):
    given, msg_ref, table_ref, chosen_ref, held, sems = refs[:5], refs[5], refs[6], refs[7], refs[8:13], refs[13]
    copies = [pltpu.make_async_copy(a, b, sems.at[n]) for n, (a, b) in enumerate(zip(given, held))]
    for copy in copies:
        copy.start()
    active_ref, state_ref, mass_ref, ticks_ref, levels_ref = held
    start = first_star()
    block = lax.axis_index("aa") * 10
    copies[0].wait()
    rows = lax.broadcasted_iota(jnp.int32, (256, 128), 0)
    highs = []
    for k in range(10):
        local = active_ref[pl.ds(block + k, 1), :] - start
        highs.append(jnp.right_shift(local, 8))
        chosen_ref[:, k * 128 : (k + 1) * 128] = jnp.where(rows == jnp.bitwise_and(local, 255), 1.0, 0.0).astype(bf16)
    for copy in copies[1:]:
        copy.wait()
    zero = jnp.zeros((1, 128), f32)
    for i in range(TILES):
        s = state_ref[:, i * 128 : (i + 1) * 128]
        dt = ticks_ref[i : i + 1, :].astype(f32) * TICK
        pos, vel = predict(s[0:3], s[3:6], s[6:9], s[9:12], dt)
        step = step_of(levels_ref[i : i + 1, :])
        field = jnp.concatenate([pos, vel, mass_ref[i : i + 1, :], zero], axis=0)
        both = jnp.concatenate([field, s[6:12], step, zero], axis=0)
        for n, part in enumerate(split3(both)):
            row = n * 128 + i // 2 * 16
            table_ref[row : row + 16, i % 2 * 128 : (i % 2 + 1) * 128] = part
        for x in range(X):
            msg_ref[x, i * 8 : (i + 1) * 8, :] = field
    picks = []
    for pair in range(5):
        found = jnp.dot(
            table_ref[...], chosen_ref[:, pair * 256 : (pair + 1) * 256], preferred_element_type=f32
        )
        for k in range(2):
            high = jnp.broadcast_to(highs[2 * pair + k], (16, 128))
            pick = jnp.zeros((16, 128), f32)
            for h in range(TILES // 2):
                r = [found[n * 128 + h * 16 : n * 128 + (h + 1) * 16, k * 128 : (k + 1) * 128] for n in range(3)]
                pick = jnp.where(high == h, (r[0] + r[1]) + r[2], pick)
            picks.append(pick)
    for g in range(GROUPS):
        main = picks[g]
        tail = picks[8 + g // 4][:, (g % 4) * TAIL : (g % 4 + 1) * TAIL]
        step = [main[14:15, n * TAIL : (n + 1) * TAIL] for n in range(4)]
        x, row = g % X, FIELD + 16 * (g // X)
        for n, q in enumerate((0, 3, 8, 11)):
            msg_ref[x, row + 4 * n : row + 4 * n + 4, :] = pack(main[q : q + 3], tail[q : q + 3], step[n])
        msg_ref[x, 8 * (g // X) + 7 : 8 * (g // X) + 8, :] = jnp.concatenate([tail[14:15], jnp.zeros((1, 96), f32)], axis=1)


def sum_kernel(got_ref, out_ref, keep_ref):
    c = lax.axis_index("c")
    picks = pl.ds(pl.multiple_of(FIELD + 16 * c, 16), 16)
    total = got_ref[0, picks, :]
    step = got_ref[0, pl.ds(8 * c + 7, 1), :]
    for g in range(1, GROUPS):
        total = total + got_ref[g, picks, :]
        step = step + got_ref[g, pl.ds(8 * c + 7, 1), :]
    for z in range(out_ref.shape[0]):
        out_ref[z] = total[0:8]
    keep_ref[0:8, :] = total[8:16]
    keep_ref[8:16, :] = jnp.broadcast_to(step, (8, 128))


def weight_rows(tile, row):
    value = jnp.where(row < 6, tile * tile[6:7], jnp.where(row == 6, tile, 0.0))
    first = value.astype(bf16).astype(f32)
    rest = value - first
    second = rest.astype(bf16).astype(f32)
    return jnp.concatenate([first, second, rest - second, jnp.zeros_like(value)], axis=0).astype(bf16)


def cross_rows(tile, row, center):
    tile = tile - center
    dot = jnp.sum(tile[0:3] * tile[3:6], axis=0, keepdims=True)
    value = jnp.where(row < 6, tile, jnp.where(row == 6, 1.0, dot))
    first = value.astype(bf16).astype(f32)
    rest = value - first
    second = rest.astype(bf16).astype(f32)
    third = rest - second
    return jnp.concatenate([first, second, first, second, third, first, third, second], axis=0).astype(bf16)


def target_rows(pos, vel, center):
    pos, vel = pos - center[0:3, 0:1], vel - center[3:6, 0:1]
    value = jnp.concatenate([-vel, -pos, jnp.sum(pos * vel, axis=0, keepdims=True), jnp.ones_like(pos[0:1])], axis=0)
    first = value.astype(bf16).astype(f32)
    rest = value - first
    second = rest.astype(bf16).astype(f32)
    third = rest - second
    return jnp.transpose(jnp.concatenate([first, first, second, second, first, third, second, third], axis=0)).astype(bf16)


def force_kernel(targets_ref, got_ref, keep_ref, out_ref, seen_ref, left_ref, along_ref, sums_ref):
    target = targets_ref[0]
    for z in range(1, targets_ref.shape[0]):
        target = target + targets_ref[z]
    columns = jnp.transpose(target)
    for q in range(3):
        seen_ref[q, 0:MAIN, :] = jnp.broadcast_to(columns[:, q : q + 1], (MAIN, 128))
        for half in range(2):
            seen_ref[half * 3 + q, MAIN:PER, :] = jnp.broadcast_to(
                columns[q * TAIL : (q + 1) * TAIL, half * 4 + 3 : half * 4 + 4], (TAIL, 128)
            )
    row = lax.broadcasted_iota(jnp.int32, (8, 128), 0)
    center = jnp.broadcast_to(jnp.mean(got_ref[0, 0:8, :], axis=1, keepdims=True), (8, 128))
    center = jnp.where(row < 6, center, 0.0)
    left_ref[...] = target_rows(target[0:3], target[4:7], center)
    sums_ref[...] = jnp.zeros_like(sums_ref)

    across = CHUNK // 128
    chunks = GROUPS * TILES // across

    def tiles_of(n):
        g, part = n // (TILES // across), n % (TILES // across)
        return g, pl.multiple_of(part * (CHUNK // 16), 8)

    def cross(n, slot):
        g, base = tiles_of(n)
        right = [cross_rows(got_ref[g, pl.ds(base + j * 8, 8), :], row, center) for j in range(across)]
        along_ref[slot] = jnp.dot(left_ref[...], jnp.concatenate(right, axis=1), preferred_element_type=f32)

    def chunk(n, slot):
        g, base = tiles_of(n)
        star = [
            jnp.concatenate(
                [jnp.broadcast_to(got_ref[g, pl.ds(base + j * 8 + q, 1), :], (ROWS, 128)) for j in range(across)], axis=1
            )
            for q in range(6)
        ]
        weight = jnp.concatenate(
            [weight_rows(got_ref[g, pl.ds(base + j * 8, 8), :], row) for j in range(across)], axis=1
        )
        values = []
        for b in range(BLOCKS):
            r = slice(b * ROWS, (b + 1) * ROWS)
            needed = 3 if b < CROSSED else 6
            apart = [star[q] - jnp.concatenate([seen_ref[q, r, :]] * across, axis=1) for q in range(needed)]
            dx, dy, dz = apart[0:3]
            total = (dx * dx + EPS2) + dy * dy + dz * dz
            if b < CROSSED:
                along = along_ref[slot, r, :]
            else:
                wx, wy, wz = apart[3:6]
                along = dx * wx + dy * wy + dz * wz
            inverse = lax.rsqrt(total)
            square = inverse * inverse
            cube = square * inverse
            rate = cube * (square * along)
            for value in (cube, rate):
                high = value.astype(bf16)
                values += [high, (value - high.astype(f32)).astype(bf16)]
            if (b + 1) * 4 * ROWS % 256 == 0 or b == BLOCKS - 1:
                right = jnp.concatenate(values, axis=0)
                values = []
                end = (b + 1) * 4 * ROWS
                sums_ref[:, end - right.shape[0] : end] += lax.dot_general(
                    weight, right, (((1,), (1,)), ((), ())), preferred_element_type=f32
                )

    cross(0, 0)

    def body(n, _):
        for u in range(UNROLL):
            cross(jnp.minimum(n * UNROLL + u + 1, chunks - 1), (u + 1) % 2)
            chunk(n * UNROLL + u, u % 2)
        return 0

    lax.fori_loop(0, chunks // UNROLL, body, 0)
    sums = jnp.transpose(sums_ref[...])

    def columns_of(part):
        total = jnp.concatenate(
            [
                sums[b * 4 * ROWS + part * ROWS : b * 4 * ROWS + (part + 1) * ROWS]
                + sums[b * 4 * ROWS + (part + 1) * ROWS : b * 4 * ROWS + (part + 2) * ROWS]
                for b in range(BLOCKS)
            ],
            axis=0,
        )
        main = jnp.transpose(total[0:MAIN])
        tail = jnp.transpose(total[MAIN:PER])
        return main[0:8] + main[8:16] + main[16:24], tail[0:8] + tail[8:16] + tail[16:24]

    def three(value):
        return jnp.concatenate([value, value, value], axis=0)

    main, tail = columns_of(0)
    cube_pos = pack(main[0:3], tail[0:3])
    cube_vel = pack(main[3:6], tail[3:6])
    cube_one = pack(three(main[6:7]), three(tail[6:7]))
    main, tail = columns_of(2)
    rate_pos = pack(main[0:3], tail[0:3])
    rate_one = pack(three(main[6:7]), three(tail[6:7]))
    acc = cube_pos - target[0:4] * cube_one
    jerk = (cube_vel - target[4:8] * cube_one) - 3.0 * (rate_pos - target[0:4] * rate_one)
    last = jnp.concatenate([acc[3:4, 0:96], keep_ref[8:9, 0:TAIL]], axis=1)
    forces = jnp.concatenate([acc[0:3], last, jerk], axis=0)
    for z in range(out_ref.shape[0]):
        out_ref[z, 0:8, :] = forces
        out_ref[z, 8:16, :] = keep_ref[0:8, :]


def correct_kernel(scale, targets_ref, got_ref, out_ref):
    target = targets_ref[0]
    total = got_ref[0]
    for z in range(1, targets_ref.shape[0]):
        target = target + targets_ref[z]
        total = total + got_ref[z]
    forces = total[0:8] * scale
    old = total[8:16]
    main = jnp.concatenate([a[r : r + 1, 96:128] for a in (target, old) for r in (3, 7)], axis=1)
    tail = total[3:4, 96:128]
    step = pack(jnp.concatenate([main, main, main], axis=0), jnp.concatenate([tail, tail, tail], axis=0))
    pos, vel = correct(target[0:4], target[4:8], old[0:4], old[4:8], step, forces[0:4], forces[4:8])
    both = jnp.concatenate([pos, vel], axis=0)
    for d in range(out_ref.shape[0]):
        out_ref[d, 0:8, :] = forces
        out_ref[d, 8:16, :] = both


def store_kernel(state_ref, ticks_ref, levels_ref, active_ref, got_ref, new_active_ref, new_state_ref, sums_ref):
    start = first_star()
    mine = lax.axis_index("aa")

    def tails(c, y, row):
        parts = [got_ref[c * X + x, y, row : row + 1, :] for x in range(X)]
        return jnp.concatenate(
            [jnp.concatenate([p[:, q * TAIL : (q + 1) * TAIL] for p in parts], axis=1) for q in range(3)], axis=0
        )

    for c in range(C):
        for x in range(X):
            lanes = slice((c * X + x) * 128, (c * X + x + 1) * 128)
            tile = got_ref[c * X + x, mine]
            new_active_ref[0:3, lanes] = tile[8:11]
            new_active_ref[3:6, lanes] = tile[12:15]
            new_active_ref[6:9, lanes] = tile[0:3]
            new_active_ref[9:12, lanes] = tile[4:7]
        lanes = slice(1024 + c * 128, 1024 + (c + 1) * 128)
        new_active_ref[0:3, lanes] = tails(c, mine, 11)
        new_active_ref[3:6, lanes] = tails(c, mine, 15)
        new_active_ref[6:9, lanes] = tails(c, mine, 3)
        new_active_ref[9:12, lanes] = tails(c, mine, 7)

    row8 = lax.broadcasted_iota(jnp.int32, (8, 128), 0)
    rows = lax.broadcasted_iota(jnp.int32, (128, 128), 0)
    one = jnp.ones((1, 128), f32)
    sums_ref[...] = jnp.zeros_like(sums_ref)

    def block(y):
        tiles = [jnp.where(row8 == 3, 1.0, got_ref[c * X + x, y, 0:8, :]) for c in range(C) for x in range(X)]
        for c in range(C):
            tiles.append(jnp.concatenate([tails(c, y, 3), one, tails(c, y, 7), one], axis=0))
        lefts, lows = [], []
        for k, tile in enumerate(tiles):
            local = active_ref[pl.ds(y * 10 + k, 1), :] - start
            high = jnp.broadcast_to(jnp.right_shift(local, 7), (16, 128))
            lows.append(jnp.where(rows == jnp.bitwise_and(local, 127), 1.0, 0.0).astype(bf16))
            first = tile.astype(bf16).astype(f32)
            both = jnp.concatenate([first, tile - first], axis=0)
            lefts.append(jnp.concatenate([jnp.where(high == h, both, 0.0).astype(bf16) for h in range(TILES)], axis=0))
        total = lax.dot_general(
            jnp.concatenate(lefts, axis=1),
            jnp.concatenate(lows, axis=1),
            (((1,), (1,)), ((), ())),
            preferred_element_type=f32,
        )
        sums_ref[...] += total

    for y in range(got_ref.shape[1]):
        block(y)

    for i in range(TILES):
        lanes = slice(i * 128, (i + 1) * 128)
        s = state_ref[:, lanes]
        forces = sums_ref[i * 16 : i * 16 + 8, :] + sums_ref[i * 16 + 8 : i * 16 + 16, :]
        acc, jerk, hit = forces[0:3], forces[4:7], forces[3:4] > 0.5
        dt = ticks_ref[i : i + 1, :].astype(f32) * TICK
        step = step_of(levels_ref[i : i + 1, :])
        pos, vel = predict(s[0:3], s[3:6], s[6:9], s[9:12], dt)
        pos, vel = correct(pos, vel, s[6:9], s[9:12], step, acc, jerk)
        new = jnp.concatenate([pos, vel, acc, jerk], axis=0)
        new_state_ref[:, lanes] = jnp.where(hit, new, s)


def per_device(state, mass, levels, ticks, active):
    z_count, y_count = lax.axis_size("z"), lax.axis_size("aa")
    n_stars = state.shape[1] * z_count * GROUPS
    mass, levels, ticks = [a.reshape(TILES, 128) for a in (mass, levels, ticks)]
    active = active.reshape(-1, 128)

    message = pl.pallas_call(
        pick_kernel,
        out_shape=jax.ShapeDtypeStruct((X, FIELD + 16 * C, 128), f32),
        in_specs=[pl.BlockSpec(memory_space=pltpu.HBM)] * 5,
        out_specs=vmem(1)[0],
        scratch_shapes=[pltpu.VMEM((384, 256), bf16), pltpu.VMEM((256, 1280), bf16)]
        + [pltpu.VMEM(a.shape, a.dtype) for a in (active, state, mass, ticks, levels)]
        + [pltpu.SemaphoreType.DMA((5,))],
        compiler_params=params(),
    )(*[pltpu.with_memory_space_constraint(a, pltpu.HBM) for a in (active, state, mass, ticks, levels)])
    got = lax.all_to_all(message, "x", 0, 0, tiled=True)
    got = lax.all_gather(got, "c", tiled=True)

    targets, keep = pl.pallas_call(
        sum_kernel,
        out_shape=[jax.ShapeDtypeStruct((z_count, 8, 128), f32), jax.ShapeDtypeStruct((16, 128), f32)],
        in_specs=vmem(1),
        out_specs=vmem(2),
        compiler_params=params(),
    )(got)
    targets = lax.all_to_all(targets, "z", 0, 0, tiled=True)

    partial = pl.pallas_call(
        force_kernel,
        out_shape=jax.ShapeDtypeStruct((z_count, 16, 128), f32),
        in_specs=vmem(3),
        out_specs=vmem(1)[0],
        scratch_shapes=[
            pltpu.VMEM((6, PER, 128), f32),
            pltpu.VMEM((CROSSED * ROWS, 64), bf16),
            pltpu.VMEM((2, CROSSED * ROWS, CHUNK), f32),
            pltpu.VMEM((32, 4 * PER), f32),
        ],
        compiler_params=params(),
    )(targets, got, keep)
    partial = lax.all_to_all(partial, "z", 0, 0, tiled=True)

    updates = pl.pallas_call(
        lambda *refs: correct_kernel(1.0 / n_stars, *refs),
        out_shape=jax.ShapeDtypeStruct((y_count * X, 16, 128), f32),
        in_specs=vmem(2),
        out_specs=vmem(1)[0],
        compiler_params=params(),
    )(targets, partial)
    updates = lax.all_to_all(updates, ("x", "aa"), 0, 0, tiled=True)
    updates = lax.all_gather(updates, "c", tiled=True).reshape(GROUPS, y_count, 16, 128)

    new_active, new_state = pl.pallas_call(
        store_kernel,
        out_shape=[jax.ShapeDtypeStruct((12, 1280), f32), jax.ShapeDtypeStruct(state.shape, f32)],
        in_specs=vmem(5),
        out_specs=vmem(2),
        scratch_shapes=[
            pltpu.VMEM((256, 128), f32),
        ],
        compiler_params=params(),
    )(state, ticks, levels, active, updates)
    return new_active, new_state


def solution(mesh):
    shape = (mesh.shape["ja"] // GROUPS, X, C, mesh.shape["aa"])
    fine = Mesh(mesh.devices.reshape(shape), ("z", "x", "c", "aa"))
    ja = ("z", "x", "c")
    return jax.shard_map(
        per_device,
        mesh=fine,
        in_specs=(P(None, ja), P(ja), P(ja), P(ja), P()),
        out_specs=(P(None, "aa"), P(None, ja)),
        check_vma=False,
    )
```

```python
import jax
import jax.numpy as jnp
from jax import lax
from jax.experimental import pallas as pl
from jax.experimental.pallas import tpu as pltpu
from jax.sharding import Mesh, PartitionSpec as P

LEVELS = 5
EPS2 = 0.0001
H_MAX = 0.25
TICK = H_MAX / 2**LEVELS

X, C = 4, 2
GROUPS = X * C
TILES = 16
MAIN, TAIL = 128, 32
PER = MAIN + TAIL
FIELD = 8 * TILES
CHUNK = 1024
ROWS = 16
BLOCKS = PER // ROWS
CROSSED = MAIN // ROWS
UNROLL = 8

f32, bf16 = jnp.float32, jnp.bfloat16


def params():
    return pltpu.CompilerParams(vmem_limit_bytes=48 * 1024 * 1024)


def vmem(n):
    return [pl.BlockSpec(memory_space=pltpu.VMEM)] * n


def predict(pos, vel, acc, jerk, dt):
    predicted = pos + dt * (vel + dt * (0.5 * acc + dt * (jerk / 6.0)))
    predicted_vel = vel + dt * (acc + dt * (0.5 * jerk))
    return predicted, predicted_vel


def step_of(levels):
    return jnp.left_shift(jnp.ones_like(levels), LEVELS - levels).astype(f32) * TICK


def correct(pos, vel, old_acc, old_jerk, step, acc_new, jerk_new):
    error = old_acc - acc_new
    second = -6.0 * error - step * (4.0 * old_jerk + 2.0 * jerk_new)
    third = 12.0 * error + 6.0 * step * (old_jerk + jerk_new)
    fixed_pos = pos + step * step * (second / 24.0 + third / 120.0)
    fixed_vel = vel + step * (second / 6.0 + third / 24.0)
    return fixed_pos, fixed_vel


def split3(value):
    first = value.astype(bf16)
    rest = value - first.astype(f32)
    second = rest.astype(bf16)
    return first, second, (rest - second.astype(f32)).astype(bf16)


def pack(main, tail, spare=None):
    if spare is None:
        spare = jnp.zeros((1, TAIL), f32)
    last = jnp.concatenate([tail[0:1], tail[1:2], tail[2:3], spare], axis=1)
    return jnp.concatenate([main, last], axis=0)


def first_star():
    return ((lax.axis_index("z") * X + lax.axis_index("x")) * C + lax.axis_index("c")) * (TILES * 128)


def pick_kernel(*refs):
    given, msg_ref, table_ref, chosen_ref, held, sems = refs[:5], refs[5], refs[6], refs[7], refs[8:13], refs[13]
    copies = [pltpu.make_async_copy(a, b, sems.at[n]) for n, (a, b) in enumerate(zip(given, held))]
    for copy in copies:
        copy.start()
    active_ref, state_ref, mass_ref, ticks_ref, levels_ref = held
    start = first_star()
    block = lax.axis_index("aa") * 10
    copies[0].wait()
    rows = lax.broadcasted_iota(jnp.int32, (256, 128), 0)
    highs = []
    for k in range(10):
        local = active_ref[pl.ds(block + k, 1), :] - start
        highs.append(jnp.right_shift(local, 8))
        chosen_ref[:, k * 128 : (k + 1) * 128] = jnp.where(rows == jnp.bitwise_and(local, 255), 1.0, 0.0).astype(bf16)
    for copy in copies[1:]:
        copy.wait()
    zero = jnp.zeros((1, 128), f32)
    for i in range(TILES):
        s = state_ref[:, i * 128 : (i + 1) * 128]
        dt = ticks_ref[i : i + 1, :].astype(f32) * TICK
        pos, vel = predict(s[0:3], s[3:6], s[6:9], s[9:12], dt)
        step = step_of(levels_ref[i : i + 1, :])
        field = jnp.concatenate([pos, vel, mass_ref[i : i + 1, :], zero], axis=0)
        both = jnp.concatenate([field, s[6:12], step, zero], axis=0)
        for n, part in enumerate(split3(both)):
            row = n * 128 + i // 2 * 16
            table_ref[row : row + 16, i % 2 * 128 : (i % 2 + 1) * 128] = part
        for x in range(X):
            msg_ref[x, i * 8 : (i + 1) * 8, :] = field
    picks = []
    for pair in range(5):
        found = jnp.dot(
            table_ref[...], chosen_ref[:, pair * 256 : (pair + 1) * 256], preferred_element_type=f32
        )
        for k in range(2):
            high = jnp.broadcast_to(highs[2 * pair + k], (16, 128))
            pick = jnp.zeros((16, 128), f32)
            for h in range(TILES // 2):
                r = [found[n * 128 + h * 16 : n * 128 + (h + 1) * 16, k * 128 : (k + 1) * 128] for n in range(3)]
                pick = jnp.where(high == h, (r[0] + r[1]) + r[2], pick)
            picks.append(pick)
    for g in range(GROUPS):
        main = picks[g]
        tail = picks[8 + g // 4][:, (g % 4) * TAIL : (g % 4 + 1) * TAIL]
        step = [main[14:15, n * TAIL : (n + 1) * TAIL] for n in range(4)]
        x, row = g % X, FIELD + 16 * (g // X)
        for n, q in enumerate((0, 3, 8, 11)):
            msg_ref[x, row + 4 * n : row + 4 * n + 4, :] = pack(main[q : q + 3], tail[q : q + 3], step[n])
        msg_ref[x, 8 * (g // X) + 7 : 8 * (g // X) + 8, :] = jnp.concatenate([tail[14:15], jnp.zeros((1, 96), f32)], axis=1)


def sum_kernel(got_ref, out_ref, keep_ref):
    c = lax.axis_index("c")
    picks = pl.ds(pl.multiple_of(FIELD + 16 * c, 16), 16)
    total = got_ref[0, picks, :]
    step = got_ref[0, pl.ds(8 * c + 7, 1), :]
    for g in range(1, GROUPS):
        total = total + got_ref[g, picks, :]
        step = step + got_ref[g, pl.ds(8 * c + 7, 1), :]
    for z in range(out_ref.shape[0]):
        out_ref[z] = total[0:8]
    keep_ref[0:8, :] = total[8:16]
    keep_ref[8:16, :] = jnp.broadcast_to(step, (8, 128))


def weight_rows(tile, row, center):
    value = (jnp.where(row < 6, tile, 1.0) - center) * tile[6:7]
    first = value.astype(bf16).astype(f32)
    rest = value - first
    second = rest.astype(bf16).astype(f32)
    return jnp.concatenate([first, second, rest - second, jnp.zeros_like(value)], axis=0).astype(bf16)


def cross_rows(tile, row, center):
    tile = jnp.where(row < 6, tile, 1.0) - center
    dot = jnp.sum(tile[0:3] * tile[3:6], axis=0, keepdims=True)
    value = jnp.where(row == 7, dot, tile)
    first = value.astype(bf16).astype(f32)
    rest = value - first
    second = rest.astype(bf16).astype(f32)
    third = rest - second
    return jnp.concatenate([first, second, first, second, third, first, third, second], axis=0).astype(bf16)


def target_rows(pos, vel, center):
    pos, vel = pos - center[0:3, 0:1], vel - center[3:6, 0:1]
    value = jnp.concatenate([-vel, -pos, jnp.sum(pos * vel, axis=0, keepdims=True), jnp.ones_like(pos[0:1])], axis=0)
    first = value.astype(bf16).astype(f32)
    rest = value - first
    second = rest.astype(bf16).astype(f32)
    third = rest - second
    return jnp.transpose(jnp.concatenate([first, first, second, second, first, third, second, third], axis=0)).astype(bf16)


def force_kernel(targets_ref, got_ref, keep_ref, out_ref, seen_ref, left_ref, along_ref, sums_ref):
    target = targets_ref[0]
    for z in range(1, targets_ref.shape[0]):
        target = target + targets_ref[z]
    columns = jnp.transpose(target)
    for q in range(3):
        seen_ref[q, 0:MAIN, :] = jnp.broadcast_to(columns[:, q : q + 1], (MAIN, 128))
        for half in range(2):
            seen_ref[half * 3 + q, MAIN:PER, :] = jnp.broadcast_to(
                columns[q * TAIL : (q + 1) * TAIL, half * 4 + 3 : half * 4 + 4], (TAIL, 128)
            )
    row = lax.broadcasted_iota(jnp.int32, (8, 128), 0)
    center = jnp.broadcast_to(jnp.mean(got_ref[0, 0:8, :], axis=1, keepdims=True), (8, 128))
    center = jnp.where(row < 6, center, 0.0)
    left_ref[...] = target_rows(target[0:3], target[4:7], center)
    sums_ref[...] = jnp.zeros_like(sums_ref)

    across = CHUNK // 128
    chunks = GROUPS * TILES // across

    def tiles_of(n):
        g, part = n // (TILES // across), n % (TILES // across)
        return g, pl.multiple_of(part * (CHUNK // 16), 8)

    def cross(n, slot):
        g, base = tiles_of(n)
        right = [cross_rows(got_ref[g, pl.ds(base + j * 8, 8), :], row, center) for j in range(across)]
        along_ref[slot] = jnp.dot(left_ref[...], jnp.concatenate(right, axis=1), preferred_element_type=f32)

    def chunk(n, slot):
        g, base = tiles_of(n)
        star = [
            jnp.concatenate(
                [jnp.broadcast_to(got_ref[g, pl.ds(base + j * 8 + q, 1), :], (ROWS, 128)) for j in range(across)], axis=1
            )
            for q in range(6)
        ]
        weight = jnp.concatenate(
            [weight_rows(got_ref[g, pl.ds(base + j * 8, 8), :], row, center) for j in range(across)], axis=1
        )
        values = []
        for b in range(BLOCKS):
            r = slice(b * ROWS, (b + 1) * ROWS)
            needed = 3 if b < CROSSED else 6
            apart = [star[q] - jnp.concatenate([seen_ref[q, r, :]] * across, axis=1) for q in range(needed)]
            dx, dy, dz = apart[0:3]
            total = (dx * dx + EPS2) + dy * dy + dz * dz
            if b < CROSSED:
                along = along_ref[slot, r, :]
            else:
                wx, wy, wz = apart[3:6]
                along = dx * wx + dy * wy + dz * wz
            inverse = lax.rsqrt(total)
            square = inverse * inverse
            cube = square * inverse
            rate = cube * (square * along)
            for value in (cube, rate):
                high = value.astype(bf16)
                values += [high, (value - high.astype(f32)).astype(bf16)]
            if (b + 1) * 4 * ROWS % 256 == 0 or b == BLOCKS - 1:
                right = jnp.concatenate(values, axis=0)
                values = []
                end = (b + 1) * 4 * ROWS
                sums_ref[:, end - right.shape[0] : end] += lax.dot_general(
                    weight, right, (((1,), (1,)), ((), ())), preferred_element_type=f32
                )

    cross(0, 0)

    def body(n, _):
        for u in range(UNROLL):
            cross(jnp.minimum(n * UNROLL + u + 1, chunks - 1), (u + 1) % 2)
            chunk(n * UNROLL + u, u % 2)
        return 0

    lax.fori_loop(0, chunks // UNROLL, body, 0)
    sums = jnp.transpose(sums_ref[...])

    def columns_of(part):
        total = jnp.concatenate(
            [
                sums[b * 4 * ROWS + part * ROWS : b * 4 * ROWS + (part + 1) * ROWS]
                + sums[b * 4 * ROWS + (part + 1) * ROWS : b * 4 * ROWS + (part + 2) * ROWS]
                for b in range(BLOCKS)
            ],
            axis=0,
        )
        main = jnp.transpose(total[0:MAIN])
        tail = jnp.transpose(total[MAIN:PER])
        return main[0:8] + main[8:16] + main[16:24], tail[0:8] + tail[8:16] + tail[16:24]

    def three(value):
        return jnp.concatenate([value, value, value], axis=0)

    main, tail = columns_of(0)
    cube_pos = pack(main[0:3], tail[0:3])
    cube_vel = pack(main[3:6], tail[3:6])
    cube_one = pack(three(main[6:7]), three(tail[6:7]))
    main, tail = columns_of(2)
    rate_pos = pack(main[0:3], tail[0:3])
    rate_one = pack(three(main[6:7]), three(tail[6:7]))
    pos = target[0:4] - pack(center[0:3], center[0:3, 0:TAIL])
    vel = target[4:8] - pack(center[3:6], center[3:6, 0:TAIL])
    acc = cube_pos - pos * cube_one
    jerk = (cube_vel - vel * cube_one) - 3.0 * (rate_pos - pos * rate_one)
    last = jnp.concatenate([acc[3:4, 0:96], keep_ref[8:9, 0:TAIL]], axis=1)
    forces = jnp.concatenate([acc[0:3], last, jerk], axis=0)
    for z in range(out_ref.shape[0]):
        out_ref[z, 0:8, :] = forces
        out_ref[z, 8:16, :] = keep_ref[0:8, :]


def correct_kernel(scale, targets_ref, got_ref, out_ref):
    target = targets_ref[0]
    total = got_ref[0]
    for z in range(1, targets_ref.shape[0]):
        target = target + targets_ref[z]
        total = total + got_ref[z]
    forces = total[0:8] * scale
    old = total[8:16]
    main = jnp.concatenate([a[r : r + 1, 96:128] for a in (target, old) for r in (3, 7)], axis=1)
    tail = total[3:4, 96:128]
    step = pack(jnp.concatenate([main, main, main], axis=0), jnp.concatenate([tail, tail, tail], axis=0))
    pos, vel = correct(target[0:4], target[4:8], old[0:4], old[4:8], step, forces[0:4], forces[4:8])
    both = jnp.concatenate([pos, vel], axis=0)
    for d in range(out_ref.shape[0]):
        out_ref[d, 0:8, :] = forces
        out_ref[d, 8:16, :] = both


def store_kernel(state_ref, ticks_ref, levels_ref, active_ref, got_ref, new_active_ref, new_state_ref, sums_ref):
    start = first_star()
    mine = lax.axis_index("aa")

    def tails(c, y, row):
        parts = [got_ref[c * X + x, y, row : row + 1, :] for x in range(X)]
        return jnp.concatenate(
            [jnp.concatenate([p[:, q * TAIL : (q + 1) * TAIL] for p in parts], axis=1) for q in range(3)], axis=0
        )

    for c in range(C):
        for x in range(X):
            lanes = slice((c * X + x) * 128, (c * X + x + 1) * 128)
            tile = got_ref[c * X + x, mine]
            new_active_ref[0:3, lanes] = tile[8:11]
            new_active_ref[3:6, lanes] = tile[12:15]
            new_active_ref[6:9, lanes] = tile[0:3]
            new_active_ref[9:12, lanes] = tile[4:7]
        lanes = slice(1024 + c * 128, 1024 + (c + 1) * 128)
        new_active_ref[0:3, lanes] = tails(c, mine, 11)
        new_active_ref[3:6, lanes] = tails(c, mine, 15)
        new_active_ref[6:9, lanes] = tails(c, mine, 3)
        new_active_ref[9:12, lanes] = tails(c, mine, 7)

    row8 = lax.broadcasted_iota(jnp.int32, (8, 128), 0)
    rows = lax.broadcasted_iota(jnp.int32, (128, 128), 0)
    one = jnp.ones((1, 128), f32)
    sums_ref[...] = jnp.zeros_like(sums_ref)

    def block(y):
        tiles = [jnp.where(row8 == 3, 1.0, got_ref[c * X + x, y, 0:8, :]) for c in range(C) for x in range(X)]
        for c in range(C):
            tiles.append(jnp.concatenate([tails(c, y, 3), one, tails(c, y, 7), one], axis=0))
        lefts, lows = [], []
        for k, tile in enumerate(tiles):
            local = active_ref[pl.ds(y * 10 + k, 1), :] - start
            high = jnp.broadcast_to(jnp.right_shift(local, 7), (16, 128))
            lows.append(jnp.where(rows == jnp.bitwise_and(local, 127), 1.0, 0.0).astype(bf16))
            first = tile.astype(bf16).astype(f32)
            both = jnp.concatenate([first, tile - first], axis=0)
            lefts.append(jnp.concatenate([jnp.where(high == h, both, 0.0).astype(bf16) for h in range(TILES)], axis=0))
        total = lax.dot_general(
            jnp.concatenate(lefts, axis=1),
            jnp.concatenate(lows, axis=1),
            (((1,), (1,)), ((), ())),
            preferred_element_type=f32,
        )
        sums_ref[...] += total

    for y in range(got_ref.shape[1]):
        block(y)

    for i in range(TILES):
        lanes = slice(i * 128, (i + 1) * 128)
        s = state_ref[:, lanes]
        forces = sums_ref[i * 16 : i * 16 + 8, :] + sums_ref[i * 16 + 8 : i * 16 + 16, :]
        acc, jerk, hit = forces[0:3], forces[4:7], forces[3:4] > 0.5
        dt = ticks_ref[i : i + 1, :].astype(f32) * TICK
        step = step_of(levels_ref[i : i + 1, :])
        pos, vel = predict(s[0:3], s[3:6], s[6:9], s[9:12], dt)
        pos, vel = correct(pos, vel, s[6:9], s[9:12], step, acc, jerk)
        new = jnp.concatenate([pos, vel, acc, jerk], axis=0)
        new_state_ref[:, lanes] = jnp.where(hit, new, s)


def per_device(state, mass, levels, ticks, active):
    z_count, y_count = lax.axis_size("z"), lax.axis_size("aa")
    n_stars = state.shape[1] * z_count * GROUPS
    mass, levels, ticks = [a.reshape(TILES, 128) for a in (mass, levels, ticks)]
    active = active.reshape(-1, 128)

    message = pl.pallas_call(
        pick_kernel,
        out_shape=jax.ShapeDtypeStruct((X, FIELD + 16 * C, 128), f32),
        in_specs=[pl.BlockSpec(memory_space=pltpu.HBM)] * 5,
        out_specs=vmem(1)[0],
        scratch_shapes=[pltpu.VMEM((384, 256), bf16), pltpu.VMEM((256, 1280), bf16)]
        + [pltpu.VMEM(a.shape, a.dtype) for a in (active, state, mass, ticks, levels)]
        + [pltpu.SemaphoreType.DMA((5,))],
        compiler_params=params(),
    )(*[pltpu.with_memory_space_constraint(a, pltpu.HBM) for a in (active, state, mass, ticks, levels)])
    got = lax.all_to_all(message, "x", 0, 0, tiled=True)
    got = lax.all_gather(got, "c", tiled=True)

    targets, keep = pl.pallas_call(
        sum_kernel,
        out_shape=[jax.ShapeDtypeStruct((z_count, 8, 128), f32), jax.ShapeDtypeStruct((16, 128), f32)],
        in_specs=vmem(1),
        out_specs=vmem(2),
        compiler_params=params(),
    )(got)
    targets = lax.all_to_all(targets, "z", 0, 0, tiled=True)

    partial = pl.pallas_call(
        force_kernel,
        out_shape=jax.ShapeDtypeStruct((z_count, 16, 128), f32),
        in_specs=vmem(3),
        out_specs=vmem(1)[0],
        scratch_shapes=[
            pltpu.VMEM((6, PER, 128), f32),
            pltpu.VMEM((CROSSED * ROWS, 64), bf16),
            pltpu.VMEM((2, CROSSED * ROWS, CHUNK), f32),
            pltpu.VMEM((32, 4 * PER), f32),
        ],
        compiler_params=params(),
    )(targets, got, keep)
    partial = lax.all_to_all(partial, "z", 0, 0, tiled=True)

    updates = pl.pallas_call(
        lambda *refs: correct_kernel(1.0 / n_stars, *refs),
        out_shape=jax.ShapeDtypeStruct((y_count * X, 16, 128), f32),
        in_specs=vmem(2),
        out_specs=vmem(1)[0],
        compiler_params=params(),
    )(targets, partial)
    updates = lax.all_to_all(updates, ("x", "aa"), 0, 0, tiled=True)
    updates = lax.all_gather(updates, "c", tiled=True).reshape(GROUPS, y_count, 16, 128)

    new_active, new_state = pl.pallas_call(
        store_kernel,
        out_shape=[jax.ShapeDtypeStruct((12, 1280), f32), jax.ShapeDtypeStruct(state.shape, f32)],
        in_specs=vmem(5),
        out_specs=vmem(2),
        scratch_shapes=[
            pltpu.VMEM((256, 128), f32),
        ],
        compiler_params=params(),
    )(state, ticks, levels, active, updates)
    return new_active, new_state


def solution(mesh):
    shape = (mesh.shape["ja"] // GROUPS, X, C, mesh.shape["aa"])
    fine = Mesh(mesh.devices.reshape(shape), ("z", "x", "c", "aa"))
    ja = ("z", "x", "c")
    return jax.shard_map(
        per_device,
        mesh=fine,
        in_specs=(P(None, ja), P(ja), P(ja), P(ja), P()),
        out_specs=(P(None, "aa"), P(None, ja)),
        check_vma=False,
    )
```

```python
import jax
import jax.numpy as jnp
from jax import lax
from jax.experimental import pallas as pl
from jax.experimental.pallas import tpu as pltpu
from jax.sharding import Mesh, PartitionSpec as P

LEVELS = 5
EPS2 = 0.0001
H_MAX = 0.25
TICK = H_MAX / 2**LEVELS

X, C = 4, 2
GROUPS = X * C
TILES = 16
MAIN, TAIL = 128, 32
PER = MAIN + TAIL
FIELD = 8 * TILES
CHUNK = 1024
ROWS = 16
BLOCKS = PER // ROWS
CROSSED = MAIN // ROWS
UNROLL = 8

f32, bf16 = jnp.float32, jnp.bfloat16


def params():
    return pltpu.CompilerParams(vmem_limit_bytes=48 * 1024 * 1024)


def vmem(n):
    return [pl.BlockSpec(memory_space=pltpu.VMEM)] * n


def predict(pos, vel, acc, jerk, dt):
    predicted = pos + dt * (vel + dt * (0.5 * acc + dt * (jerk / 6.0)))
    predicted_vel = vel + dt * (acc + dt * (0.5 * jerk))
    return predicted, predicted_vel


def step_of(levels):
    return jnp.left_shift(jnp.ones_like(levels), LEVELS - levels).astype(f32) * TICK


def correct(pos, vel, old_acc, old_jerk, step, acc_new, jerk_new):
    error = old_acc - acc_new
    second = -6.0 * error - step * (4.0 * old_jerk + 2.0 * jerk_new)
    third = 12.0 * error + 6.0 * step * (old_jerk + jerk_new)
    fixed_pos = pos + step * step * (second / 24.0 + third / 120.0)
    fixed_vel = vel + step * (second / 6.0 + third / 24.0)
    return fixed_pos, fixed_vel


def split3(value):
    first = value.astype(bf16)
    rest = value - first.astype(f32)
    second = rest.astype(bf16)
    return first, second, (rest - second.astype(f32)).astype(bf16)


def pack(main, tail, spare=None):
    if spare is None:
        spare = jnp.zeros((1, TAIL), f32)
    last = jnp.concatenate([tail[0:1], tail[1:2], tail[2:3], spare], axis=1)
    return jnp.concatenate([main, last], axis=0)


def first_star():
    return ((lax.axis_index("z") * X + lax.axis_index("x")) * C + lax.axis_index("c")) * (TILES * 128)


def pick_kernel(*refs):
    given, msg_ref, table_ref, chosen_ref, held, sems = refs[:5], refs[5], refs[6], refs[7], refs[8:13], refs[13]
    copies = [pltpu.make_async_copy(a, b, sems.at[n]) for n, (a, b) in enumerate(zip(given, held))]
    for copy in copies:
        copy.start()
    active_ref, state_ref, mass_ref, ticks_ref, levels_ref = held
    start = first_star()
    block = lax.axis_index("aa") * 10
    copies[0].wait()
    rows = lax.broadcasted_iota(jnp.int32, (256, 128), 0)
    highs = []
    for k in range(10):
        local = active_ref[pl.ds(block + k, 1), :] - start
        highs.append(jnp.right_shift(local, 8))
        chosen_ref[:, k * 128 : (k + 1) * 128] = jnp.where(rows == jnp.bitwise_and(local, 255), 1.0, 0.0).astype(bf16)
    for copy in copies[1:]:
        copy.wait()
    zero = jnp.zeros((1, 128), f32)
    for i in range(TILES):
        s = state_ref[:, i * 128 : (i + 1) * 128]
        dt = ticks_ref[i : i + 1, :].astype(f32) * TICK
        pos, vel = predict(s[0:3], s[3:6], s[6:9], s[9:12], dt)
        step = step_of(levels_ref[i : i + 1, :])
        field = jnp.concatenate([pos, vel, mass_ref[i : i + 1, :], zero], axis=0)
        both = jnp.concatenate([field, s[6:12], step, zero], axis=0)
        for n, part in enumerate(split3(both)):
            row = n * 128 + i // 2 * 16
            table_ref[row : row + 16, i % 2 * 128 : (i % 2 + 1) * 128] = part
        for x in range(X):
            msg_ref[x, i * 8 : (i + 1) * 8, :] = field
    picks = []
    for pair in range(5):
        found = jnp.dot(
            table_ref[...], chosen_ref[:, pair * 256 : (pair + 1) * 256], preferred_element_type=f32
        )
        for k in range(2):
            high = jnp.broadcast_to(highs[2 * pair + k], (16, 128))
            pick = jnp.zeros((16, 128), f32)
            for h in range(TILES // 2):
                r = [found[n * 128 + h * 16 : n * 128 + (h + 1) * 16, k * 128 : (k + 1) * 128] for n in range(3)]
                pick = jnp.where(high == h, (r[0] + r[1]) + r[2], pick)
            picks.append(pick)
    for g in range(GROUPS):
        main = picks[g]
        tail = picks[8 + g // 4][:, (g % 4) * TAIL : (g % 4 + 1) * TAIL]
        step = [main[14:15, n * TAIL : (n + 1) * TAIL] for n in range(4)]
        x, row = g % X, FIELD + 16 * (g // X)
        for n, q in enumerate((0, 3, 8, 11)):
            msg_ref[x, row + 4 * n : row + 4 * n + 4, :] = pack(main[q : q + 3], tail[q : q + 3], step[n])
        msg_ref[x, 8 * (g // X) + 7 : 8 * (g // X) + 8, :] = jnp.concatenate([tail[14:15], jnp.zeros((1, 96), f32)], axis=1)


def sum_kernel(got_ref, out_ref, keep_ref):
    c = lax.axis_index("c")
    picks = pl.ds(pl.multiple_of(FIELD + 16 * c, 16), 16)
    total = got_ref[0, picks, :]
    step = got_ref[0, pl.ds(8 * c + 7, 1), :]
    for g in range(1, GROUPS):
        total = total + got_ref[g, picks, :]
        step = step + got_ref[g, pl.ds(8 * c + 7, 1), :]
    for z in range(out_ref.shape[0]):
        out_ref[z] = total[0:8]
    keep_ref[0:8, :] = total[8:16]
    keep_ref[8:16, :] = jnp.broadcast_to(step, (8, 128))


def weight_rows(tile, row, center):
    value = (jnp.where(row < 6, tile, 1.0) - center) * tile[6:7]
    first = value.astype(bf16).astype(f32)
    rest = value - first
    second = rest.astype(bf16).astype(f32)
    return jnp.concatenate([first, second, rest - second, jnp.zeros_like(value)], axis=0).astype(bf16)


def cross_rows(tile, row, center):
    tile = jnp.where(row < 6, tile, 1.0) - center
    dot = jnp.sum(tile[0:3] * tile[3:6], axis=0, keepdims=True)
    value = jnp.where(row == 7, dot, tile)
    first = value.astype(bf16).astype(f32)
    rest = value - first
    second = rest.astype(bf16).astype(f32)
    third = rest - second
    return jnp.concatenate([first, second, first, second, third, first, third, second], axis=0).astype(bf16)


def target_rows(pos, vel, center):
    pos, vel = pos - center[0:3, 0:1], vel - center[3:6, 0:1]
    value = jnp.concatenate([-vel, -pos, jnp.sum(pos * vel, axis=0, keepdims=True), jnp.ones_like(pos[0:1])], axis=0)
    first = value.astype(bf16).astype(f32)
    rest = value - first
    second = rest.astype(bf16).astype(f32)
    third = rest - second
    return jnp.transpose(jnp.concatenate([first, first, second, second, first, third, second, third], axis=0)).astype(bf16)


def force_kernel(targets_ref, got_ref, keep_ref, out_ref, seen_ref, left_ref, along_ref, sums_ref):
    target = targets_ref[0]
    for z in range(1, targets_ref.shape[0]):
        target = target + targets_ref[z]
    columns = jnp.transpose(target)
    for q in range(3):
        seen_ref[q, 0:MAIN, :] = jnp.broadcast_to(columns[:, q : q + 1], (MAIN, 128))
        for half in range(2):
            seen_ref[half * 3 + q, MAIN:PER, :] = jnp.broadcast_to(
                columns[q * TAIL : (q + 1) * TAIL, half * 4 + 3 : half * 4 + 4], (TAIL, 128)
            )
    row = lax.broadcasted_iota(jnp.int32, (8, 128), 0)
    center = jnp.broadcast_to(jnp.mean(got_ref[0, 0:8, :], axis=1, keepdims=True), (8, 128))
    center = jnp.where(row < 6, center, 0.0)
    left_ref[...] = target_rows(target[0:3], target[4:7], center)
    sums_ref[...] = jnp.zeros_like(sums_ref)

    across = CHUNK // 128
    chunks = GROUPS * TILES // across

    def tiles_of(n):
        g, part = n // (TILES // across), n % (TILES // across)
        return g, pl.multiple_of(part * (CHUNK // 16), 8)

    def cross(n, slot):
        g, base = tiles_of(n)
        right = [cross_rows(got_ref[g, pl.ds(base + j * 8, 8), :], row, center) for j in range(across)]
        along_ref[slot] = jnp.dot(left_ref[...], jnp.concatenate(right, axis=1), preferred_element_type=f32)

    def chunk(n, slot):
        g, base = tiles_of(n)
        star = [
            jnp.concatenate(
                [jnp.broadcast_to(got_ref[g, pl.ds(base + j * 8 + q, 1), :], (ROWS, 128)) for j in range(across)], axis=1
            )
            for q in range(6)
        ]
        weight = jnp.concatenate(
            [weight_rows(got_ref[g, pl.ds(base + j * 8, 8), :], row, center) for j in range(across)], axis=1
        )
        values = []
        for b in range(BLOCKS):
            r = slice(b * ROWS, (b + 1) * ROWS)
            needed = 3 if b < CROSSED else 6
            apart = [star[q] - jnp.concatenate([seen_ref[q, r, :]] * across, axis=1) for q in range(needed)]
            dx, dy, dz = apart[0:3]
            total = (dx * dx + EPS2) + dy * dy + dz * dz
            if b < CROSSED:
                along = along_ref[slot, r, :]
            else:
                wx, wy, wz = apart[3:6]
                along = dx * wx + dy * wy + dz * wz
            inverse = lax.rsqrt(total)
            square = inverse * inverse
            cube = square * inverse
            rate = cube * (square * along)
            for value in (cube, rate):
                high = value.astype(bf16)
                values += [high, (value - high.astype(f32)).astype(bf16)]
            if (b + 1) * 4 * ROWS % 256 == 0 or b == BLOCKS - 1:
                right = jnp.concatenate(values, axis=0)
                values = []
                end = (b + 1) * 4 * ROWS
                sums_ref[:, end - right.shape[0] : end] += lax.dot_general(
                    weight, right, (((1,), (1,)), ((), ())), preferred_element_type=f32
                )

    cross(0, 0)

    def body(n, _):
        for u in range(UNROLL):
            cross(jnp.minimum(n * UNROLL + u + 1, chunks - 1), (u + 1) % 2)
            chunk(n * UNROLL + u, u % 2)
        return 0

    lax.fori_loop(0, chunks // UNROLL, body, 0)
    sums = jnp.transpose(sums_ref[...])

    def columns_of(part):
        total = jnp.concatenate(
            [
                sums[b * 4 * ROWS + part * ROWS : b * 4 * ROWS + (part + 1) * ROWS]
                + sums[b * 4 * ROWS + (part + 1) * ROWS : b * 4 * ROWS + (part + 2) * ROWS]
                for b in range(BLOCKS)
            ],
            axis=0,
        )
        main = jnp.transpose(total[0:MAIN])
        tail = jnp.transpose(total[MAIN:PER])
        return main[0:8] + main[8:16] + main[16:24], tail[0:8] + tail[8:16] + tail[16:24]

    def three(value):
        return jnp.concatenate([value, value, value], axis=0)

    main, tail = columns_of(0)
    cube_pos = pack(main[0:3], tail[0:3])
    cube_vel = pack(main[3:6], tail[3:6])
    cube_one = pack(three(main[6:7]), three(tail[6:7]))
    main, tail = columns_of(2)
    rate_pos = pack(main[0:3], tail[0:3])
    rate_one = pack(three(main[6:7]), three(tail[6:7]))
    pos = target[0:4] - pack(center[0:3], center[0:3, 0:TAIL])
    vel = target[4:8] - pack(center[3:6], center[3:6, 0:TAIL])
    acc = cube_pos - pos * cube_one
    jerk = (cube_vel - vel * cube_one) - 3.0 * (rate_pos - pos * rate_one)
    last = jnp.concatenate([acc[3:4, 0:96], keep_ref[8:9, 0:TAIL]], axis=1)
    forces = jnp.concatenate([acc[0:3], last, jerk], axis=0)
    for z in range(out_ref.shape[0]):
        out_ref[z, 0:8, :] = forces
        out_ref[z, 8:16, :] = keep_ref[0:8, :]


def correct_kernel(scale, targets_ref, got_ref, out_ref):
    target = targets_ref[0]
    total = got_ref[0]
    for z in range(1, targets_ref.shape[0]):
        target = target + targets_ref[z]
        total = total + got_ref[z]
    forces = total[0:8] * scale
    old = total[8:16]
    main = jnp.concatenate([a[r : r + 1, 96:128] for a in (target, old) for r in (3, 7)], axis=1)
    tail = total[3:4, 96:128]
    step = pack(jnp.concatenate([main, main, main], axis=0), jnp.concatenate([tail, tail, tail], axis=0))
    pos, vel = correct(target[0:4], target[4:8], old[0:4], old[4:8], step, forces[0:4], forces[4:8])
    both = jnp.concatenate([pos, vel], axis=0)
    for d in range(out_ref.shape[0]):
        out_ref[d, 0:8, :] = forces
        out_ref[d, 8:16, :] = both


def store_kernel(state_ref, ticks_ref, levels_ref, active_ref, got_ref, new_active_ref, new_state_ref, sums_ref):
    start = first_star()
    mine = lax.axis_index("aa")

    def tails(c, y, row):
        parts = [got_ref[c * X + x, y, row : row + 1, :] for x in range(X)]
        return jnp.concatenate(
            [jnp.concatenate([p[:, q * TAIL : (q + 1) * TAIL] for p in parts], axis=1) for q in range(3)], axis=0
        )

    for c in range(C):
        for x in range(X):
            lanes = slice((c * X + x) * 128, (c * X + x + 1) * 128)
            tile = got_ref[c * X + x, mine]
            new_active_ref[0:3, lanes] = tile[8:11]
            new_active_ref[3:6, lanes] = tile[12:15]
            new_active_ref[6:9, lanes] = tile[0:3]
            new_active_ref[9:12, lanes] = tile[4:7]
        lanes = slice(1024 + c * 128, 1024 + (c + 1) * 128)
        new_active_ref[0:3, lanes] = tails(c, mine, 11)
        new_active_ref[3:6, lanes] = tails(c, mine, 15)
        new_active_ref[6:9, lanes] = tails(c, mine, 3)
        new_active_ref[9:12, lanes] = tails(c, mine, 7)

    row8 = lax.broadcasted_iota(jnp.int32, (8, 128), 0)
    rows = lax.broadcasted_iota(jnp.int32, (128, 128), 0).astype(f32).astype(bf16)
    nothing, unit = jnp.zeros((16, 128), bf16), jnp.ones((128, 128), bf16)
    one = jnp.ones((1, 128), f32)
    sums_ref[...] = jnp.zeros_like(sums_ref)

    def block(y):
        tiles = [jnp.where(row8 == 3, 1.0, got_ref[c * X + x, y, 0:8, :]) for c in range(C) for x in range(X)]
        for c in range(C):
            tiles.append(jnp.concatenate([tails(c, y, 3), one, tails(c, y, 7), one], axis=0))
        lefts, lows = [], []
        for k, tile in enumerate(tiles):
            local = active_ref[pl.ds(y * 10 + k, 1), :] - start
            high = jnp.broadcast_to(jnp.right_shift(local, 7).astype(f32), (16, 128)).astype(bf16)
            low = jnp.broadcast_to(jnp.bitwise_and(local, 127).astype(f32), (128, 128)).astype(bf16)
            lows.append(jnp.where(rows == low, unit, jnp.zeros_like(unit)))
            first = tile.astype(bf16).astype(f32)
            both = jnp.concatenate([first, tile - first], axis=0).astype(bf16)
            lefts.append(jnp.concatenate([jnp.where(high == h, both, nothing) for h in range(TILES)], axis=0))
        total = lax.dot_general(
            jnp.concatenate(lefts, axis=1),
            jnp.concatenate(lows, axis=1),
            (((1,), (1,)), ((), ())),
            preferred_element_type=f32,
        )
        sums_ref[...] += total

    for y in range(got_ref.shape[1]):
        block(y)

    for i in range(TILES):
        lanes = slice(i * 128, (i + 1) * 128)
        s = state_ref[:, lanes]
        forces = sums_ref[i * 16 : i * 16 + 8, :] + sums_ref[i * 16 + 8 : i * 16 + 16, :]
        acc, jerk, hit = forces[0:3], forces[4:7], forces[3:4] > 0.5
        dt = ticks_ref[i : i + 1, :].astype(f32) * TICK
        step = step_of(levels_ref[i : i + 1, :])
        pos, vel = predict(s[0:3], s[3:6], s[6:9], s[9:12], dt)
        pos, vel = correct(pos, vel, s[6:9], s[9:12], step, acc, jerk)
        new = jnp.concatenate([pos, vel, acc, jerk], axis=0)
        new_state_ref[:, lanes] = jnp.where(hit, new, s)


def per_device(state, mass, levels, ticks, active):
    z_count, y_count = lax.axis_size("z"), lax.axis_size("aa")
    n_stars = state.shape[1] * z_count * GROUPS
    mass, levels, ticks = [a.reshape(TILES, 128) for a in (mass, levels, ticks)]
    active = active.reshape(-1, 128)

    message = pl.pallas_call(
        pick_kernel,
        out_shape=jax.ShapeDtypeStruct((X, FIELD + 16 * C, 128), f32),
        in_specs=[pl.BlockSpec(memory_space=pltpu.HBM)] * 5,
        out_specs=vmem(1)[0],
        scratch_shapes=[pltpu.VMEM((384, 256), bf16), pltpu.VMEM((256, 1280), bf16)]
        + [pltpu.VMEM(a.shape, a.dtype) for a in (active, state, mass, ticks, levels)]
        + [pltpu.SemaphoreType.DMA((5,))],
        compiler_params=params(),
    )(*[pltpu.with_memory_space_constraint(a, pltpu.HBM) for a in (active, state, mass, ticks, levels)])
    got = lax.all_to_all(message, "x", 0, 0, tiled=True)
    got = lax.all_gather(got, "c", tiled=True)

    targets, keep = pl.pallas_call(
        sum_kernel,
        out_shape=[jax.ShapeDtypeStruct((z_count, 8, 128), f32), jax.ShapeDtypeStruct((16, 128), f32)],
        in_specs=vmem(1),
        out_specs=vmem(2),
        compiler_params=params(),
    )(got)
    targets = lax.all_to_all(targets, "z", 0, 0, tiled=True)

    partial = pl.pallas_call(
        force_kernel,
        out_shape=jax.ShapeDtypeStruct((z_count, 16, 128), f32),
        in_specs=vmem(3),
        out_specs=vmem(1)[0],
        scratch_shapes=[
            pltpu.VMEM((6, PER, 128), f32),
            pltpu.VMEM((CROSSED * ROWS, 64), bf16),
            pltpu.VMEM((2, CROSSED * ROWS, CHUNK), f32),
            pltpu.VMEM((32, 4 * PER), f32),
        ],
        compiler_params=params(),
    )(targets, got, keep)
    partial = lax.all_to_all(partial, "z", 0, 0, tiled=True)

    updates = pl.pallas_call(
        lambda *refs: correct_kernel(1.0 / n_stars, *refs),
        out_shape=jax.ShapeDtypeStruct((y_count * X, 16, 128), f32),
        in_specs=vmem(2),
        out_specs=vmem(1)[0],
        compiler_params=params(),
    )(targets, partial)
    updates = lax.all_to_all(updates, ("x", "aa"), 0, 0, tiled=True)
    updates = lax.all_gather(updates, "c", tiled=True).reshape(GROUPS, y_count, 16, 128)

    new_active, new_state = pl.pallas_call(
        store_kernel,
        out_shape=[jax.ShapeDtypeStruct((12, 1280), f32), jax.ShapeDtypeStruct(state.shape, f32)],
        in_specs=vmem(5),
        out_specs=vmem(2),
        scratch_shapes=[
            pltpu.VMEM((256, 128), f32),
        ],
        compiler_params=params(),
    )(state, ticks, levels, active, updates)
    return new_active, new_state


def solution(mesh):
    shape = (mesh.shape["ja"] // GROUPS, X, C, mesh.shape["aa"])
    fine = Mesh(mesh.devices.reshape(shape), ("z", "x", "c", "aa"))
    ja = ("z", "x", "c")
    return jax.shard_map(
        per_device,
        mesh=fine,
        in_specs=(P(None, ja), P(ja), P(ja), P(ja), P()),
        out_specs=(P(None, "aa"), P(None, ja)),
        check_vma=False,
    )
```

```python
import jax
import jax.numpy as jnp
from jax import lax
from jax.experimental import pallas as pl
from jax.experimental.pallas import tpu as pltpu
from jax.sharding import Mesh, PartitionSpec as P

LEVELS = 5
EPS2 = 0.0001
H_MAX = 0.25
TICK = H_MAX / 2**LEVELS

X, C = 4, 2
GROUPS = X * C
TILES = 16
MAIN, TAIL = 128, 32
PER = MAIN + TAIL
FIELD = 8 * TILES
CHUNK = 1024
ROWS = 16
BLOCKS = PER // ROWS
CROSSED = MAIN // ROWS
UNROLL = 8

f32, bf16 = jnp.float32, jnp.bfloat16


def params():
    return pltpu.CompilerParams(vmem_limit_bytes=48 * 1024 * 1024)


def vmem(n):
    return [pl.BlockSpec(memory_space=pltpu.VMEM)] * n


def predict(pos, vel, acc, jerk, dt):
    predicted = pos + dt * (vel + dt * (0.5 * acc + dt * (jerk / 6.0)))
    predicted_vel = vel + dt * (acc + dt * (0.5 * jerk))
    return predicted, predicted_vel


def step_of(levels):
    return jnp.left_shift(jnp.ones_like(levels), LEVELS - levels).astype(f32) * TICK


def correct(pos, vel, old_acc, old_jerk, step, acc_new, jerk_new):
    error = old_acc - acc_new
    second = -6.0 * error - step * (4.0 * old_jerk + 2.0 * jerk_new)
    third = 12.0 * error + 6.0 * step * (old_jerk + jerk_new)
    fixed_pos = pos + step * step * (second / 24.0 + third / 120.0)
    fixed_vel = vel + step * (second / 6.0 + third / 24.0)
    return fixed_pos, fixed_vel


def split3(value):
    first = value.astype(bf16)
    rest = value - first.astype(f32)
    second = rest.astype(bf16)
    return first, second, (rest - second.astype(f32)).astype(bf16)


def pack(main, tail, spare=None):
    if spare is None:
        spare = jnp.zeros((1, TAIL), f32)
    last = jnp.concatenate([tail[0:1], tail[1:2], tail[2:3], spare], axis=1)
    return jnp.concatenate([main, last], axis=0)


def first_star():
    return ((lax.axis_index("z") * X + lax.axis_index("x")) * C + lax.axis_index("c")) * (TILES * 128)


def pick_kernel(*refs):
    given, msg_ref, table_ref, chosen_ref, held, sems = refs[:5], refs[5], refs[6], refs[7], refs[8:13], refs[13]
    copies = [pltpu.make_async_copy(a, b, sems.at[n]) for n, (a, b) in enumerate(zip(given, held))]
    for copy in copies:
        copy.start()
    active_ref, state_ref, mass_ref, ticks_ref, levels_ref = held
    start = first_star()
    block = lax.axis_index("aa") * 10
    copies[0].wait()
    rows = lax.broadcasted_iota(jnp.int32, (256, 128), 0)
    highs = []
    for k in range(10):
        local = active_ref[pl.ds(block + k, 1), :] - start
        highs.append(jnp.right_shift(local, 8))
        chosen_ref[:, k * 128 : (k + 1) * 128] = jnp.where(rows == jnp.bitwise_and(local, 255), 1.0, 0.0).astype(bf16)
    for copy in copies[1:]:
        copy.wait()
    zero = jnp.zeros((1, 128), f32)
    for i in range(TILES):
        s = state_ref[:, i * 128 : (i + 1) * 128]
        dt = ticks_ref[i : i + 1, :].astype(f32) * TICK
        pos, vel = predict(s[0:3], s[3:6], s[6:9], s[9:12], dt)
        step = step_of(levels_ref[i : i + 1, :])
        field = jnp.concatenate([pos, vel, mass_ref[i : i + 1, :], zero], axis=0)
        both = jnp.concatenate([field, s[6:12], step, zero], axis=0)
        for n, part in enumerate(split3(both)):
            row = n * 128 + i // 2 * 16
            table_ref[row : row + 16, i % 2 * 128 : (i % 2 + 1) * 128] = part
        for x in range(X):
            msg_ref[x, i * 8 : (i + 1) * 8, :] = field
    picks = []
    for pair in range(5):
        found = jnp.dot(
            table_ref[...], chosen_ref[:, pair * 256 : (pair + 1) * 256], preferred_element_type=f32
        )
        for k in range(2):
            high = jnp.broadcast_to(highs[2 * pair + k], (16, 128))
            pick = jnp.zeros((16, 128), f32)
            for h in range(TILES // 2):
                r = [found[n * 128 + h * 16 : n * 128 + (h + 1) * 16, k * 128 : (k + 1) * 128] for n in range(3)]
                pick = jnp.where(high == h, (r[0] + r[1]) + r[2], pick)
            picks.append(pick)
    for g in range(GROUPS):
        main = picks[g]
        tail = picks[8 + g // 4][:, (g % 4) * TAIL : (g % 4 + 1) * TAIL]
        step = [main[14:15, n * TAIL : (n + 1) * TAIL] for n in range(4)]
        x, row = g % X, FIELD + 16 * (g // X)
        for n, q in enumerate((0, 3, 8, 11)):
            msg_ref[x, row + 4 * n : row + 4 * n + 4, :] = pack(main[q : q + 3], tail[q : q + 3], step[n])
        msg_ref[x, 8 * (g // X) + 7 : 8 * (g // X) + 8, :] = jnp.concatenate([tail[14:15], jnp.zeros((1, 96), f32)], axis=1)


def sum_kernel(got_ref, out_ref, keep_ref):
    c = lax.axis_index("c")
    picks = pl.ds(pl.multiple_of(FIELD + 16 * c, 16), 16)
    total = got_ref[0, picks, :]
    step = got_ref[0, pl.ds(8 * c + 7, 1), :]
    for g in range(1, GROUPS):
        total = total + got_ref[g, picks, :]
        step = step + got_ref[g, pl.ds(8 * c + 7, 1), :]
    for z in range(out_ref.shape[0]):
        out_ref[z] = total[0:8]
    keep_ref[0:8, :] = total[8:16]
    keep_ref[8:16, :] = jnp.broadcast_to(step, (8, 128))


def weight_rows(tile, row, center):
    value = (jnp.where(row < 6, tile, 1.0) - center) * tile[6:7]
    first = value.astype(bf16).astype(f32)
    rest = value - first
    second = rest.astype(bf16).astype(f32)
    return jnp.concatenate([first, second, rest - second, jnp.zeros_like(value)], axis=0).astype(bf16)


def cross_rows(tile, row, center):
    tile = jnp.where(row < 6, tile, 1.0) - center
    dot = jnp.sum(tile[0:3] * tile[3:6], axis=0, keepdims=True)
    value = jnp.where(row == 7, dot, tile)
    first = value.astype(bf16).astype(f32)
    rest = value - first
    second = rest.astype(bf16).astype(f32)
    third = rest - second
    return jnp.concatenate([first, second, first, second, third, first, third, second], axis=0).astype(bf16)


def target_rows(pos, vel, center):
    pos, vel = pos - center[0:3, 0:1], vel - center[3:6, 0:1]
    value = jnp.concatenate([-vel, -pos, jnp.sum(pos * vel, axis=0, keepdims=True), jnp.ones_like(pos[0:1])], axis=0)
    first = value.astype(bf16).astype(f32)
    rest = value - first
    second = rest.astype(bf16).astype(f32)
    third = rest - second
    return jnp.transpose(jnp.concatenate([first, first, second, second, first, third, second, third], axis=0)).astype(bf16)


def force_kernel(targets_ref, got_ref, keep_ref, out_ref, seen_ref, left_ref, along_ref, sums_ref):
    target = targets_ref[0]
    for z in range(1, targets_ref.shape[0]):
        target = target + targets_ref[z]
    columns = jnp.transpose(target)
    for q in range(3):
        seen_ref[q, 0:MAIN, :] = jnp.broadcast_to(columns[:, q : q + 1], (MAIN, 128))
        for half in range(2):
            seen_ref[half * 3 + q, MAIN:PER, :] = jnp.broadcast_to(
                columns[q * TAIL : (q + 1) * TAIL, half * 4 + 3 : half * 4 + 4], (TAIL, 128)
            )
    row = lax.broadcasted_iota(jnp.int32, (8, 128), 0)
    center = jnp.broadcast_to(jnp.mean(got_ref[0, 0:8, :], axis=1, keepdims=True), (8, 128))
    center = jnp.where(row < 6, center, 0.0)
    left_ref[...] = target_rows(target[0:3], target[4:7], center)
    sums_ref[...] = jnp.zeros_like(sums_ref)

    across = CHUNK // 128
    chunks = GROUPS * TILES // across

    def tiles_of(n):
        g, part = n // (TILES // across), n % (TILES // across)
        return g, pl.multiple_of(part * (CHUNK // 16), 8)

    def cross(n, slot):
        g, base = tiles_of(n)
        right = [cross_rows(got_ref[g, pl.ds(base + j * 8, 8), :], row, center) for j in range(across)]
        along_ref[slot] = jnp.dot(left_ref[...], jnp.concatenate(right, axis=1), preferred_element_type=f32)

    def chunk(n, slot):
        g, base = tiles_of(n)
        star = [
            jnp.concatenate(
                [jnp.broadcast_to(got_ref[g, pl.ds(base + j * 8 + q, 1), :], (ROWS, 128)) for j in range(across)], axis=1
            )
            for q in range(6)
        ]
        weight = jnp.concatenate(
            [weight_rows(got_ref[g, pl.ds(base + j * 8, 8), :], row, center) for j in range(across)], axis=1
        )
        values = []
        for b in range(BLOCKS):
            r = slice(b * ROWS, (b + 1) * ROWS)
            needed = 3 if b < CROSSED else 6
            apart = [star[q] - jnp.concatenate([seen_ref[q, r, :]] * across, axis=1) for q in range(needed)]
            dx, dy, dz = apart[0:3]
            total = (dx * dx + EPS2) + dy * dy + dz * dz
            if b < CROSSED:
                along = along_ref[slot, r, :]
            else:
                wx, wy, wz = apart[3:6]
                along = dx * wx + dy * wy + dz * wz
            inverse = lax.rsqrt(total)
            square = inverse * inverse
            cube = square * inverse
            rate = cube * (square * along)
            for value in (cube, rate):
                high = value.astype(bf16)
                values += [high, (value - high.astype(f32)).astype(bf16)]
            if (b + 1) * 4 * ROWS % 256 == 0 or b == BLOCKS - 1:
                right = jnp.concatenate(values, axis=0)
                values = []
                end = (b + 1) * 4 * ROWS
                sums_ref[:, end - right.shape[0] : end] += lax.dot_general(
                    weight, right, (((1,), (1,)), ((), ())), preferred_element_type=f32
                )

    cross(0, 0)

    def body(n, _):
        for u in range(UNROLL):
            cross(jnp.minimum(n * UNROLL + u + 1, chunks - 1), (u + 1) % 2)
            chunk(n * UNROLL + u, u % 2)
        return 0

    lax.fori_loop(0, chunks // UNROLL, body, 0)
    sums = jnp.transpose(sums_ref[...])

    def columns_of(part):
        total = jnp.concatenate(
            [
                sums[b * 4 * ROWS + part * ROWS : b * 4 * ROWS + (part + 1) * ROWS]
                + sums[b * 4 * ROWS + (part + 1) * ROWS : b * 4 * ROWS + (part + 2) * ROWS]
                for b in range(BLOCKS)
            ],
            axis=0,
        )
        main = jnp.transpose(total[0:MAIN])
        tail = jnp.transpose(total[MAIN:PER])
        return main[0:8] + main[8:16] + main[16:24], tail[0:8] + tail[8:16] + tail[16:24]

    def three(value):
        return jnp.concatenate([value, value, value], axis=0)

    main, tail = columns_of(0)
    cube_pos = pack(main[0:3], tail[0:3])
    cube_vel = pack(main[3:6], tail[3:6])
    cube_one = pack(three(main[6:7]), three(tail[6:7]))
    main, tail = columns_of(2)
    rate_pos = pack(main[0:3], tail[0:3])
    rate_one = pack(three(main[6:7]), three(tail[6:7]))
    pos = target[0:4] - pack(center[0:3], center[0:3, 0:TAIL])
    vel = target[4:8] - pack(center[3:6], center[3:6, 0:TAIL])
    acc = cube_pos - pos * cube_one
    jerk = (cube_vel - vel * cube_one) - 3.0 * (rate_pos - pos * rate_one)
    last = jnp.concatenate([acc[3:4, 0:96], keep_ref[8:9, 0:TAIL]], axis=1)
    forces = jnp.concatenate([acc[0:3], last, jerk], axis=0)
    for z in range(out_ref.shape[0]):
        out_ref[z, 0:8, :] = forces
        out_ref[z, 8:16, :] = keep_ref[0:8, :]


def correct_kernel(scale, targets_ref, got_ref, out_ref):
    target = targets_ref[0]
    total = got_ref[0]
    for z in range(1, targets_ref.shape[0]):
        target = target + targets_ref[z]
        total = total + got_ref[z]
    forces = total[0:8] * scale
    old = total[8:16]
    main = jnp.concatenate([a[r : r + 1, 96:128] for a in (target, old) for r in (3, 7)], axis=1)
    tail = total[3:4, 96:128]
    step = pack(jnp.concatenate([main, main, main], axis=0), jnp.concatenate([tail, tail, tail], axis=0))
    pos, vel = correct(target[0:4], target[4:8], old[0:4], old[4:8], step, forces[0:4], forces[4:8])
    both = jnp.concatenate([pos, vel], axis=0)
    for d in range(out_ref.shape[0]):
        out_ref[d, 0:8, :] = forces
        out_ref[d, 8:16, :] = both


def store_kernel(state_ref, ticks_ref, levels_ref, active_ref, got_ref, new_active_ref, new_state_ref, sums_ref):
    start = first_star()
    mine = lax.axis_index("aa")

    def tails(c, y, row):
        parts = [got_ref[c * X + x, y, row : row + 1, :] for x in range(X)]
        return jnp.concatenate(
            [jnp.concatenate([p[:, q * TAIL : (q + 1) * TAIL] for p in parts], axis=1) for q in range(3)], axis=0
        )

    for c in range(C):
        for x in range(X):
            lanes = slice((c * X + x) * 128, (c * X + x + 1) * 128)
            tile = got_ref[c * X + x, mine]
            new_active_ref[0:3, lanes] = tile[8:11]
            new_active_ref[3:6, lanes] = tile[12:15]
            new_active_ref[6:9, lanes] = tile[0:3]
            new_active_ref[9:12, lanes] = tile[4:7]
        lanes = slice(1024 + c * 128, 1024 + (c + 1) * 128)
        new_active_ref[0:3, lanes] = tails(c, mine, 11)
        new_active_ref[3:6, lanes] = tails(c, mine, 15)
        new_active_ref[6:9, lanes] = tails(c, mine, 3)
        new_active_ref[9:12, lanes] = tails(c, mine, 7)

    row16 = lax.broadcasted_iota(jnp.int32, (16, 128), 0)
    owners = [
        jnp.where(row16 < edge, float(n), n + 1.0).astype(bf16) for n, edge in enumerate((12, 8, 4))
    ]
    rows = lax.broadcasted_iota(jnp.int32, (128, 128), 0).astype(f32).astype(bf16)
    nothing, unit = jnp.zeros((16, 128), bf16), jnp.ones((128, 128), bf16)
    sums_ref[...] = jnp.zeros_like(sums_ref)

    def block(y):
        tiles = [
            jnp.concatenate([got_ref[c * X + x, y, 0:3, :], got_ref[c * X + x, y, 4:7, :]], axis=0)
            for c in range(C)
            for x in range(X)
        ]
        for c in range(C):
            tiles.append(jnp.concatenate([tails(c, y, 3), tails(c, y, 7)], axis=0))
        lefts, lows = [], []
        for k, tile in enumerate(tiles):
            local = active_ref[pl.ds(y * 10 + k, 1), :] - start
            high = jnp.broadcast_to(jnp.right_shift(local, 7).astype(f32), (16, 128)).astype(bf16)
            low = jnp.broadcast_to(jnp.bitwise_and(local, 127).astype(f32), (128, 128)).astype(bf16)
            lows.append(jnp.where(rows == low, unit, jnp.zeros_like(unit)))
            first = tile.astype(bf16).astype(f32)
            both = jnp.concatenate([first, tile - first], axis=0)
            groups = [
                jnp.concatenate([both, both[0:4]], axis=0).astype(bf16),
                jnp.concatenate([both[4:12], both[0:8]], axis=0).astype(bf16),
                jnp.concatenate([both[8:12], both], axis=0).astype(bf16),
            ]
            aims = [high - owner for owner in owners]
            left = [
                jnp.where(aim == h, group, nothing) for h in range(0, TILES, 4) for aim, group in zip(aims, groups)
            ]
            lefts.append(jnp.concatenate(left, axis=0))
        total = lax.dot_general(
            jnp.concatenate(lefts, axis=1),
            jnp.concatenate(lows, axis=1),
            (((1,), (1,)), ((), ())),
            preferred_element_type=f32,
        )
        sums_ref[...] += total

    for y in range(got_ref.shape[1]):
        block(y)

    for i in range(TILES):
        lanes = slice(i * 128, (i + 1) * 128)
        s = state_ref[:, lanes]
        forces = sums_ref[i * 12 : i * 12 + 6, :] + sums_ref[i * 12 + 6 : i * 12 + 12, :]
        acc, jerk = forces[0:3], forces[3:6]
        ticks, levels = ticks_ref[i : i + 1, :], levels_ref[i : i + 1, :]
        hit = ticks == jnp.left_shift(jnp.ones_like(levels), LEVELS - levels)
        dt = ticks.astype(f32) * TICK
        step = step_of(levels)
        pos, vel = predict(s[0:3], s[3:6], s[6:9], s[9:12], dt)
        pos, vel = correct(pos, vel, s[6:9], s[9:12], step, acc, jerk)
        new = jnp.concatenate([pos, vel, acc, jerk], axis=0)
        new_state_ref[:, lanes] = jnp.where(hit, new, s)


def per_device(state, mass, levels, ticks, active):
    z_count, y_count = lax.axis_size("z"), lax.axis_size("aa")
    n_stars = state.shape[1] * z_count * GROUPS
    mass, levels, ticks = [a.reshape(TILES, 128) for a in (mass, levels, ticks)]
    active = active.reshape(-1, 128)

    message = pl.pallas_call(
        pick_kernel,
        out_shape=jax.ShapeDtypeStruct((X, FIELD + 16 * C, 128), f32),
        in_specs=[pl.BlockSpec(memory_space=pltpu.HBM)] * 5,
        out_specs=vmem(1)[0],
        scratch_shapes=[pltpu.VMEM((384, 256), bf16), pltpu.VMEM((256, 1280), bf16)]
        + [pltpu.VMEM(a.shape, a.dtype) for a in (active, state, mass, ticks, levels)]
        + [pltpu.SemaphoreType.DMA((5,))],
        compiler_params=params(),
    )(*[pltpu.with_memory_space_constraint(a, pltpu.HBM) for a in (active, state, mass, ticks, levels)])
    got = lax.all_to_all(message, "x", 0, 0, tiled=True)
    got = lax.all_gather(got, "c", tiled=True)

    targets, keep = pl.pallas_call(
        sum_kernel,
        out_shape=[jax.ShapeDtypeStruct((z_count, 8, 128), f32), jax.ShapeDtypeStruct((16, 128), f32)],
        in_specs=vmem(1),
        out_specs=vmem(2),
        compiler_params=params(),
    )(got)
    targets = lax.all_to_all(targets, "z", 0, 0, tiled=True)

    partial = pl.pallas_call(
        force_kernel,
        out_shape=jax.ShapeDtypeStruct((z_count, 16, 128), f32),
        in_specs=vmem(3),
        out_specs=vmem(1)[0],
        scratch_shapes=[
            pltpu.VMEM((6, PER, 128), f32),
            pltpu.VMEM((CROSSED * ROWS, 64), bf16),
            pltpu.VMEM((2, CROSSED * ROWS, CHUNK), f32),
            pltpu.VMEM((32, 4 * PER), f32),
        ],
        compiler_params=params(),
    )(targets, got, keep)
    partial = lax.all_to_all(partial, "z", 0, 0, tiled=True)

    updates = pl.pallas_call(
        lambda *refs: correct_kernel(1.0 / n_stars, *refs),
        out_shape=jax.ShapeDtypeStruct((y_count * X, 16, 128), f32),
        in_specs=vmem(2),
        out_specs=vmem(1)[0],
        compiler_params=params(),
    )(targets, partial)
    updates = lax.all_to_all(updates, ("x", "aa"), 0, 0, tiled=True)
    updates = lax.all_gather(updates, "c", tiled=True).reshape(GROUPS, y_count, 16, 128)

    new_active, new_state = pl.pallas_call(
        store_kernel,
        out_shape=[jax.ShapeDtypeStruct((12, 1280), f32), jax.ShapeDtypeStruct(state.shape, f32)],
        in_specs=vmem(5),
        out_specs=vmem(2),
        scratch_shapes=[
            pltpu.VMEM((192, 128), f32),
        ],
        compiler_params=params(),
    )(state, ticks, levels, active, updates)
    return new_active, new_state


def solution(mesh):
    shape = (mesh.shape["ja"] // GROUPS, X, C, mesh.shape["aa"])
    fine = Mesh(mesh.devices.reshape(shape), ("z", "x", "c", "aa"))
    ja = ("z", "x", "c")
    return jax.shard_map(
        per_device,
        mesh=fine,
        in_specs=(P(None, ja), P(ja), P(ja), P(ja), P()),
        out_specs=(P(None, "aa"), P(None, ja)),
        check_vma=False,
    )
```

```python
import jax
import jax.numpy as jnp
from jax import lax
from jax.experimental import pallas as pl
from jax.experimental.pallas import tpu as pltpu
from jax.sharding import Mesh, PartitionSpec as P

LEVELS = 5
EPS2 = 0.0001
H_MAX = 0.25
TICK = H_MAX / 2**LEVELS

X, C = 4, 2
GROUPS = X * C
TILES = 16
MAIN, TAIL = 128, 32
PER = MAIN + TAIL
FIELD = 8 * TILES
CHUNK = 1024
ROWS = 16
BLOCKS = PER // ROWS
CROSSED = MAIN // ROWS
UNROLL = 8

f32, bf16 = jnp.float32, jnp.bfloat16


def params():
    return pltpu.CompilerParams(vmem_limit_bytes=48 * 1024 * 1024)


def vmem(n):
    return [pl.BlockSpec(memory_space=pltpu.VMEM)] * n


def predict(pos, vel, acc, jerk, dt):
    predicted = pos + dt * (vel + dt * (0.5 * acc + dt * (jerk / 6.0)))
    predicted_vel = vel + dt * (acc + dt * (0.5 * jerk))
    return predicted, predicted_vel


def step_of(levels):
    return jnp.left_shift(jnp.ones_like(levels), LEVELS - levels).astype(f32) * TICK


def correct(pos, vel, old_acc, old_jerk, step, acc_new, jerk_new):
    error = old_acc - acc_new
    second = -6.0 * error - step * (4.0 * old_jerk + 2.0 * jerk_new)
    third = 12.0 * error + 6.0 * step * (old_jerk + jerk_new)
    fixed_pos = pos + step * step * (second / 24.0 + third / 120.0)
    fixed_vel = vel + step * (second / 6.0 + third / 24.0)
    return fixed_pos, fixed_vel


def split3(value):
    first = value.astype(bf16)
    rest = value - first.astype(f32)
    second = rest.astype(bf16)
    return first, second, (rest - second.astype(f32)).astype(bf16)


def pack(main, tail, spare=None):
    if spare is None:
        spare = jnp.zeros((1, TAIL), f32)
    last = jnp.concatenate([tail[0:1], tail[1:2], tail[2:3], spare], axis=1)
    return jnp.concatenate([main, last], axis=0)


def first_star():
    return ((lax.axis_index("z") * X + lax.axis_index("x")) * C + lax.axis_index("c")) * (TILES * 128)


def pick_kernel(*refs):
    given, msg_ref, table_ref, chosen_ref, held, sems = refs[:5], refs[5], refs[6], refs[7], refs[8:13], refs[13]
    copies = [pltpu.make_async_copy(a, b, sems.at[n]) for n, (a, b) in enumerate(zip(given, held))]
    for copy in copies:
        copy.start()
    active_ref, state_ref, mass_ref, ticks_ref, levels_ref = held
    start = first_star()
    block = lax.axis_index("aa") * 10
    copies[0].wait()
    rows = lax.broadcasted_iota(jnp.int32, (256, 128), 0)
    highs = []
    for k in range(10):
        local = active_ref[pl.ds(block + k, 1), :] - start
        highs.append(jnp.right_shift(local, 8))
        chosen_ref[:, k * 128 : (k + 1) * 128] = jnp.where(rows == jnp.bitwise_and(local, 255), 1.0, 0.0).astype(bf16)
    for copy in copies[1:]:
        copy.wait()
    zero = jnp.zeros((1, 128), f32)
    for i in range(TILES):
        s = state_ref[:, i * 128 : (i + 1) * 128]
        dt = ticks_ref[i : i + 1, :].astype(f32) * TICK
        pos, vel = predict(s[0:3], s[3:6], s[6:9], s[9:12], dt)
        step = step_of(levels_ref[i : i + 1, :])
        field = jnp.concatenate([pos, vel, mass_ref[i : i + 1, :], zero], axis=0)
        both = jnp.concatenate([field, s[6:12], step, zero], axis=0)
        for n, part in enumerate(split3(both)):
            row = n * 128 + i // 2 * 16
            table_ref[row : row + 16, i % 2 * 128 : (i % 2 + 1) * 128] = part
        for x in range(X):
            msg_ref[x, i * 8 : (i + 1) * 8, :] = field
    picks = []
    for pair in range(5):
        found = jnp.dot(
            table_ref[...], chosen_ref[:, pair * 256 : (pair + 1) * 256], preferred_element_type=f32
        )
        for k in range(2):
            high = jnp.broadcast_to(highs[2 * pair + k], (16, 128))
            pick = jnp.zeros((16, 128), f32)
            for h in range(TILES // 2):
                r = [found[n * 128 + h * 16 : n * 128 + (h + 1) * 16, k * 128 : (k + 1) * 128] for n in range(3)]
                pick = jnp.where(high == h, (r[0] + r[1]) + r[2], pick)
            picks.append(pick)
    for g in range(GROUPS):
        main = picks[g]
        tail = picks[8 + g // 4][:, (g % 4) * TAIL : (g % 4 + 1) * TAIL]
        step = [main[14:15, n * TAIL : (n + 1) * TAIL] for n in range(4)]
        x, c = g % X, g // X
        packs = [pack(main[q : q + 3], tail[q : q + 3], step[n]) for n, q in enumerate((0, 3, 8, 11))]
        msg_ref[x, FIELD + 8 * c : FIELD + 8 * c + 4, :] = packs[0]
        msg_ref[x, FIELD + 8 * c + 4 : FIELD + 8 * c + 8, :] = packs[1]
        for r in range(8):
            row = 8 * (8 * c + r) + 7
            msg_ref[x, row : row + 1, :] = packs[2 + r // 4][r % 4 : r % 4 + 1]
        row = FIELD + 8 * C + c
        msg_ref[x, row : row + 1, :] = jnp.concatenate([tail[14:15], jnp.zeros((1, 96), f32)], axis=1)


def sum_kernel(got_ref, out_ref, keep_ref):
    c = lax.axis_index("c")
    picks = pl.ds(pl.multiple_of(FIELD + 8 * c, 8), 8)
    olds = pl.ds(64 * c + 7, 8, stride=8)
    steps = pl.ds(FIELD + 8 * C + c, 1)
    total, old, step = got_ref[0, picks, :], got_ref[0, olds, :], got_ref[0, steps, :]
    for g in range(1, GROUPS):
        total = total + got_ref[g, picks, :]
        old = old + got_ref[g, olds, :]
        step = step + got_ref[g, steps, :]
    for z in range(out_ref.shape[0]):
        out_ref[z] = total
    keep_ref[0:8, :] = old
    keep_ref[8:16, :] = jnp.broadcast_to(step, (8, 128))


def weight_rows(tile, row, center):
    value = (jnp.where(row < 6, tile, 1.0) - center) * tile[6:7]
    first = value.astype(bf16).astype(f32)
    rest = value - first
    second = rest.astype(bf16).astype(f32)
    return jnp.concatenate([first, second, rest - second, jnp.zeros_like(value)], axis=0).astype(bf16)


def cross_rows(tile, row, center):
    tile = jnp.where(row < 6, tile, 1.0) - center
    dot = jnp.sum(tile[0:3] * tile[3:6], axis=0, keepdims=True)
    value = jnp.where(row == 7, dot, tile)
    first = value.astype(bf16).astype(f32)
    rest = value - first
    second = rest.astype(bf16).astype(f32)
    third = rest - second
    return jnp.concatenate([first, second, first, second, third, first, third, second], axis=0).astype(bf16)


def target_rows(pos, vel, center):
    pos, vel = pos - center[0:3, 0:1], vel - center[3:6, 0:1]
    value = jnp.concatenate([-vel, -pos, jnp.sum(pos * vel, axis=0, keepdims=True), jnp.ones_like(pos[0:1])], axis=0)
    first = value.astype(bf16).astype(f32)
    rest = value - first
    second = rest.astype(bf16).astype(f32)
    third = rest - second
    return jnp.transpose(jnp.concatenate([first, first, second, second, first, third, second, third], axis=0)).astype(bf16)


def force_kernel(targets_ref, got_ref, keep_ref, out_ref, seen_ref, left_ref, along_ref, sums_ref):
    target = targets_ref[0]
    for z in range(1, targets_ref.shape[0]):
        target = target + targets_ref[z]
    columns = jnp.transpose(target)
    for q in range(3):
        seen_ref[q, 0:MAIN, :] = jnp.broadcast_to(columns[:, q : q + 1], (MAIN, 128))
        for half in range(2):
            seen_ref[half * 3 + q, MAIN:PER, :] = jnp.broadcast_to(
                columns[q * TAIL : (q + 1) * TAIL, half * 4 + 3 : half * 4 + 4], (TAIL, 128)
            )
    row = lax.broadcasted_iota(jnp.int32, (8, 128), 0)
    center = jnp.broadcast_to(jnp.mean(got_ref[0, 0:8, :], axis=1, keepdims=True), (8, 128))
    center = jnp.where(row < 6, center, 0.0)
    left_ref[...] = target_rows(target[0:3], target[4:7], center)
    sums_ref[...] = jnp.zeros_like(sums_ref)

    across = CHUNK // 128
    chunks = GROUPS * TILES // across

    def tiles_of(n):
        g, part = n // (TILES // across), n % (TILES // across)
        return g, pl.multiple_of(part * (CHUNK // 16), 8)

    def cross(n, slot):
        g, base = tiles_of(n)
        right = [cross_rows(got_ref[g, pl.ds(base + j * 8, 8), :], row, center) for j in range(across)]
        along_ref[slot] = jnp.dot(left_ref[...], jnp.concatenate(right, axis=1), preferred_element_type=f32)

    def chunk(n, slot):
        g, base = tiles_of(n)
        star = [
            jnp.concatenate(
                [jnp.broadcast_to(got_ref[g, pl.ds(base + j * 8 + q, 1), :], (ROWS, 128)) for j in range(across)], axis=1
            )
            for q in range(6)
        ]
        weight = jnp.concatenate(
            [weight_rows(got_ref[g, pl.ds(base + j * 8, 8), :], row, center) for j in range(across)], axis=1
        )
        values = []
        for b in range(BLOCKS):
            r = slice(b * ROWS, (b + 1) * ROWS)
            needed = 3 if b < CROSSED else 6
            apart = [star[q] - jnp.concatenate([seen_ref[q, r, :]] * across, axis=1) for q in range(needed)]
            dx, dy, dz = apart[0:3]
            total = (dx * dx + EPS2) + dy * dy + dz * dz
            if b < CROSSED:
                along = along_ref[slot, r, :]
            else:
                wx, wy, wz = apart[3:6]
                along = dx * wx + dy * wy + dz * wz
            inverse = lax.rsqrt(total)
            square = inverse * inverse
            cube = square * inverse
            rate = cube * (square * along)
            for value in (cube, rate):
                high = value.astype(bf16)
                values += [high, (value - high.astype(f32)).astype(bf16)]
            if (b + 1) * 4 * ROWS % 256 == 0 or b == BLOCKS - 1:
                right = jnp.concatenate(values, axis=0)
                values = []
                end = (b + 1) * 4 * ROWS
                sums_ref[:, end - right.shape[0] : end] += lax.dot_general(
                    weight, right, (((1,), (1,)), ((), ())), preferred_element_type=f32
                )

    cross(0, 0)

    def body(n, _):
        for u in range(UNROLL):
            cross(jnp.minimum(n * UNROLL + u + 1, chunks - 1), (u + 1) % 2)
            chunk(n * UNROLL + u, u % 2)
        return 0

    lax.fori_loop(0, chunks // UNROLL, body, 0)
    sums = jnp.transpose(sums_ref[...])

    def columns_of(part):
        total = jnp.concatenate(
            [
                sums[b * 4 * ROWS + part * ROWS : b * 4 * ROWS + (part + 1) * ROWS]
                + sums[b * 4 * ROWS + (part + 1) * ROWS : b * 4 * ROWS + (part + 2) * ROWS]
                for b in range(BLOCKS)
            ],
            axis=0,
        )
        main = jnp.transpose(total[0:MAIN])
        tail = jnp.transpose(total[MAIN:PER])
        return main[0:8] + main[8:16] + main[16:24], tail[0:8] + tail[8:16] + tail[16:24]

    def three(value):
        return jnp.concatenate([value, value, value], axis=0)

    main, tail = columns_of(0)
    cube_pos = pack(main[0:3], tail[0:3])
    cube_vel = pack(main[3:6], tail[3:6])
    cube_one = pack(three(main[6:7]), three(tail[6:7]))
    main, tail = columns_of(2)
    rate_pos = pack(main[0:3], tail[0:3])
    rate_one = pack(three(main[6:7]), three(tail[6:7]))
    pos = target[0:4] - pack(center[0:3], center[0:3, 0:TAIL])
    vel = target[4:8] - pack(center[3:6], center[3:6, 0:TAIL])
    acc = cube_pos - pos * cube_one
    jerk = (cube_vel - vel * cube_one) - 3.0 * (rate_pos - pos * rate_one)
    last = jnp.concatenate([acc[3:4, 0:96], keep_ref[8:9, 0:TAIL]], axis=1)
    forces = jnp.concatenate([acc[0:3], last, jerk], axis=0)
    for z in range(out_ref.shape[0]):
        out_ref[z, 0:8, :] = forces
        out_ref[z, 8:16, :] = keep_ref[0:8, :]


def correct_kernel(scale, targets_ref, got_ref, out_ref):
    target = targets_ref[0]
    total = got_ref[0]
    for z in range(1, targets_ref.shape[0]):
        target = target + targets_ref[z]
        total = total + got_ref[z]
    forces = total[0:8] * scale
    old = total[8:16]
    main = jnp.concatenate([a[r : r + 1, 96:128] for a in (target, old) for r in (3, 7)], axis=1)
    tail = total[3:4, 96:128]
    step = pack(jnp.concatenate([main, main, main], axis=0), jnp.concatenate([tail, tail, tail], axis=0))
    pos, vel = correct(target[0:4], target[4:8], old[0:4], old[4:8], step, forces[0:4], forces[4:8])
    both = jnp.concatenate([pos, vel], axis=0)
    for d in range(out_ref.shape[0]):
        out_ref[d, 0:8, :] = forces
        out_ref[d, 8:16, :] = both


def store_kernel(state_ref, ticks_ref, levels_ref, active_ref, got_ref, new_active_ref, new_state_ref, sums_ref):
    start = first_star()
    mine = lax.axis_index("aa")

    def tails(c, y, row):
        parts = [got_ref[c * X + x, y, row : row + 1, :] for x in range(X)]
        return jnp.concatenate(
            [jnp.concatenate([p[:, q * TAIL : (q + 1) * TAIL] for p in parts], axis=1) for q in range(3)], axis=0
        )

    for c in range(C):
        for x in range(X):
            lanes = slice((c * X + x) * 128, (c * X + x + 1) * 128)
            tile = got_ref[c * X + x, mine]
            new_active_ref[0:3, lanes] = tile[8:11]
            new_active_ref[3:6, lanes] = tile[12:15]
            new_active_ref[6:9, lanes] = tile[0:3]
            new_active_ref[9:12, lanes] = tile[4:7]
        lanes = slice(1024 + c * 128, 1024 + (c + 1) * 128)
        new_active_ref[0:3, lanes] = tails(c, mine, 11)
        new_active_ref[3:6, lanes] = tails(c, mine, 15)
        new_active_ref[6:9, lanes] = tails(c, mine, 3)
        new_active_ref[9:12, lanes] = tails(c, mine, 7)

    row16 = lax.broadcasted_iota(jnp.int32, (16, 128), 0)
    owners = [
        jnp.where(row16 < edge, float(n), n + 1.0).astype(bf16) for n, edge in enumerate((12, 8, 4))
    ]
    rows = lax.broadcasted_iota(jnp.int32, (128, 128), 0).astype(f32).astype(bf16)
    nothing, unit = jnp.zeros((16, 128), bf16), jnp.ones((128, 128), bf16)
    sums_ref[...] = jnp.zeros_like(sums_ref)

    def block(y):
        tiles = [
            jnp.concatenate([got_ref[c * X + x, y, 0:3, :], got_ref[c * X + x, y, 4:7, :]], axis=0)
            for c in range(C)
            for x in range(X)
        ]
        for c in range(C):
            tiles.append(jnp.concatenate([tails(c, y, 3), tails(c, y, 7)], axis=0))
        lefts, lows = [], []
        for k, tile in enumerate(tiles):
            local = active_ref[pl.ds(y * 10 + k, 1), :] - start
            high = jnp.broadcast_to(jnp.right_shift(local, 7).astype(f32), (16, 128)).astype(bf16)
            low = jnp.broadcast_to(jnp.bitwise_and(local, 127).astype(f32), (128, 128)).astype(bf16)
            lows.append(jnp.where(rows == low, unit, jnp.zeros_like(unit)))
            first = tile.astype(bf16).astype(f32)
            both = jnp.concatenate([first, tile - first], axis=0)
            groups = [
                jnp.concatenate([both, both[0:4]], axis=0).astype(bf16),
                jnp.concatenate([both[4:12], both[0:8]], axis=0).astype(bf16),
                jnp.concatenate([both[8:12], both], axis=0).astype(bf16),
            ]
            aims = [high - owner for owner in owners]
            left = [
                jnp.where(aim == h, group, nothing) for h in range(0, TILES, 4) for aim, group in zip(aims, groups)
            ]
            lefts.append(jnp.concatenate(left, axis=0))
        total = lax.dot_general(
            jnp.concatenate(lefts, axis=1),
            jnp.concatenate(lows, axis=1),
            (((1,), (1,)), ((), ())),
            preferred_element_type=f32,
        )
        sums_ref[...] += total

    for y in range(got_ref.shape[1]):
        block(y)

    for i in range(TILES):
        lanes = slice(i * 128, (i + 1) * 128)
        s = state_ref[:, lanes]
        forces = sums_ref[i * 12 : i * 12 + 6, :] + sums_ref[i * 12 + 6 : i * 12 + 12, :]
        acc, jerk = forces[0:3], forces[3:6]
        ticks, levels = ticks_ref[i : i + 1, :], levels_ref[i : i + 1, :]
        hit = ticks == jnp.left_shift(jnp.ones_like(levels), LEVELS - levels)
        dt = ticks.astype(f32) * TICK
        step = step_of(levels)
        pos, vel = predict(s[0:3], s[3:6], s[6:9], s[9:12], dt)
        pos, vel = correct(pos, vel, s[6:9], s[9:12], step, acc, jerk)
        new = jnp.concatenate([pos, vel, acc, jerk], axis=0)
        new_state_ref[:, lanes] = jnp.where(hit, new, s)


def per_device(state, mass, levels, ticks, active):
    z_count, y_count = lax.axis_size("z"), lax.axis_size("aa")
    n_stars = state.shape[1] * z_count * GROUPS
    mass, levels, ticks = [a.reshape(TILES, 128) for a in (mass, levels, ticks)]
    active = active.reshape(-1, 128)

    message = pl.pallas_call(
        pick_kernel,
        out_shape=jax.ShapeDtypeStruct((X, FIELD + 8 * C + 8, 128), f32),
        in_specs=[pl.BlockSpec(memory_space=pltpu.HBM)] * 5,
        out_specs=vmem(1)[0],
        scratch_shapes=[pltpu.VMEM((384, 256), bf16), pltpu.VMEM((256, 1280), bf16)]
        + [pltpu.VMEM(a.shape, a.dtype) for a in (active, state, mass, ticks, levels)]
        + [pltpu.SemaphoreType.DMA((5,))],
        compiler_params=params(),
    )(*[pltpu.with_memory_space_constraint(a, pltpu.HBM) for a in (active, state, mass, ticks, levels)])
    got = lax.all_to_all(message, "x", 0, 0, tiled=True)
    got = lax.all_gather(got, "c", tiled=True)

    targets, keep = pl.pallas_call(
        sum_kernel,
        out_shape=[jax.ShapeDtypeStruct((z_count, 8, 128), f32), jax.ShapeDtypeStruct((16, 128), f32)],
        in_specs=vmem(1),
        out_specs=vmem(2),
        compiler_params=params(),
    )(got)
    targets = lax.all_to_all(targets, "z", 0, 0, tiled=True)

    partial = pl.pallas_call(
        force_kernel,
        out_shape=jax.ShapeDtypeStruct((z_count, 16, 128), f32),
        in_specs=vmem(3),
        out_specs=vmem(1)[0],
        scratch_shapes=[
            pltpu.VMEM((6, PER, 128), f32),
            pltpu.VMEM((CROSSED * ROWS, 64), bf16),
            pltpu.VMEM((2, CROSSED * ROWS, CHUNK), f32),
            pltpu.VMEM((32, 4 * PER), f32),
        ],
        compiler_params=params(),
    )(targets, got, keep)
    partial = lax.all_to_all(partial, "z", 0, 0, tiled=True)

    updates = pl.pallas_call(
        lambda *refs: correct_kernel(1.0 / n_stars, *refs),
        out_shape=jax.ShapeDtypeStruct((y_count * X, 16, 128), f32),
        in_specs=vmem(2),
        out_specs=vmem(1)[0],
        compiler_params=params(),
    )(targets, partial)
    updates = lax.all_to_all(updates, ("x", "aa"), 0, 0, tiled=True)
    updates = lax.all_gather(updates, "c", tiled=True).reshape(GROUPS, y_count, 16, 128)

    new_active, new_state = pl.pallas_call(
        store_kernel,
        out_shape=[jax.ShapeDtypeStruct((12, 1280), f32), jax.ShapeDtypeStruct(state.shape, f32)],
        in_specs=vmem(5),
        out_specs=vmem(2),
        scratch_shapes=[
            pltpu.VMEM((192, 128), f32),
        ],
        compiler_params=params(),
    )(state, ticks, levels, active, updates)
    return new_active, new_state


def solution(mesh):
    shape = (mesh.shape["ja"] // GROUPS, X, C, mesh.shape["aa"])
    fine = Mesh(mesh.devices.reshape(shape), ("z", "x", "c", "aa"))
    ja = ("z", "x", "c")
    return jax.shard_map(
        per_device,
        mesh=fine,
        in_specs=(P(None, ja), P(ja), P(ja), P(ja), P()),
        out_specs=(P(None, "aa"), P(None, ja)),
        check_vma=False,
    )
```

```python
import jax
import jax.numpy as jnp
from jax import lax
from jax.experimental import pallas as pl
from jax.experimental.pallas import tpu as pltpu
from jax.sharding import Mesh, PartitionSpec as P

LEVELS = 5
EPS2 = 0.0001
H_MAX = 0.25
TICK = H_MAX / 2**LEVELS

X, C = 4, 2
GROUPS = X * C
TILES = 16
MAIN, TAIL = 128, 32
PER = MAIN + TAIL
FIELD = 8 * TILES
CHUNK = 1024
ROWS = 32
BLOCKS = PER // ROWS
CROSSED = MAIN // ROWS
UNROLL = 8

f32, bf16 = jnp.float32, jnp.bfloat16


def params():
    return pltpu.CompilerParams(vmem_limit_bytes=48 * 1024 * 1024)


def vmem(n):
    return [pl.BlockSpec(memory_space=pltpu.VMEM)] * n


def predict(pos, vel, acc, jerk, dt):
    predicted = pos + dt * (vel + dt * (0.5 * acc + dt * (jerk / 6.0)))
    predicted_vel = vel + dt * (acc + dt * (0.5 * jerk))
    return predicted, predicted_vel


def step_of(levels):
    return jnp.left_shift(jnp.ones_like(levels), LEVELS - levels).astype(f32) * TICK


def correct(pos, vel, old_acc, old_jerk, step, acc_new, jerk_new):
    error = old_acc - acc_new
    second = -6.0 * error - step * (4.0 * old_jerk + 2.0 * jerk_new)
    third = 12.0 * error + 6.0 * step * (old_jerk + jerk_new)
    fixed_pos = pos + step * step * (second / 24.0 + third / 120.0)
    fixed_vel = vel + step * (second / 6.0 + third / 24.0)
    return fixed_pos, fixed_vel


def split3(value):
    first = value.astype(bf16)
    rest = value - first.astype(f32)
    second = rest.astype(bf16)
    return first, second, (rest - second.astype(f32)).astype(bf16)


def pack(main, tail, spare=None):
    if spare is None:
        spare = jnp.zeros((1, TAIL), f32)
    last = jnp.concatenate([tail[0:1], tail[1:2], tail[2:3], spare], axis=1)
    return jnp.concatenate([main, last], axis=0)


def first_star():
    return ((lax.axis_index("z") * X + lax.axis_index("x")) * C + lax.axis_index("c")) * (TILES * 128)


def pick_kernel(*refs):
    given, msg_ref, table_ref, chosen_ref, held, sems = refs[:5], refs[5], refs[6], refs[7], refs[8:13], refs[13]
    copies = [pltpu.make_async_copy(a, b, sems.at[n]) for n, (a, b) in enumerate(zip(given, held))]
    for copy in copies:
        copy.start()
    active_ref, state_ref, mass_ref, ticks_ref, levels_ref = held
    start = first_star()
    block = lax.axis_index("aa") * 10
    copies[0].wait()
    rows = lax.broadcasted_iota(jnp.int32, (256, 128), 0)
    highs = []
    for k in range(10):
        local = active_ref[pl.ds(block + k, 1), :] - start
        highs.append(jnp.right_shift(local, 8))
        chosen_ref[:, k * 128 : (k + 1) * 128] = jnp.where(rows == jnp.bitwise_and(local, 255), 1.0, 0.0).astype(bf16)
    for copy in copies[1:]:
        copy.wait()
    zero = jnp.zeros((1, 128), f32)
    for i in range(TILES):
        s = state_ref[:, i * 128 : (i + 1) * 128]
        dt = ticks_ref[i : i + 1, :].astype(f32) * TICK
        pos, vel = predict(s[0:3], s[3:6], s[6:9], s[9:12], dt)
        step = step_of(levels_ref[i : i + 1, :])
        field = jnp.concatenate([pos, vel, mass_ref[i : i + 1, :], zero], axis=0)
        both = jnp.concatenate([field, s[6:12], step, zero], axis=0)
        for n, part in enumerate(split3(both)):
            row = n * 128 + i // 2 * 16
            table_ref[row : row + 16, i % 2 * 128 : (i % 2 + 1) * 128] = part
        for x in range(X):
            msg_ref[x, i * 8 : (i + 1) * 8, :] = field
    picks = []
    for pair in range(5):
        found = jnp.dot(
            table_ref[...], chosen_ref[:, pair * 256 : (pair + 1) * 256], preferred_element_type=f32
        )
        for k in range(2):
            high = jnp.broadcast_to(highs[2 * pair + k], (16, 128))
            pick = jnp.zeros((16, 128), f32)
            for h in range(TILES // 2):
                r = [found[n * 128 + h * 16 : n * 128 + (h + 1) * 16, k * 128 : (k + 1) * 128] for n in range(3)]
                pick = jnp.where(high == h, (r[0] + r[1]) + r[2], pick)
            picks.append(pick)
    for g in range(GROUPS):
        main = picks[g]
        tail = picks[8 + g // 4][:, (g % 4) * TAIL : (g % 4 + 1) * TAIL]
        step = [main[14:15, n * TAIL : (n + 1) * TAIL] for n in range(4)]
        x, c = g % X, g // X
        packs = [pack(main[q : q + 3], tail[q : q + 3], step[n]) for n, q in enumerate((0, 3, 8, 11))]
        msg_ref[x, FIELD + 8 * c : FIELD + 8 * c + 4, :] = packs[0]
        msg_ref[x, FIELD + 8 * c + 4 : FIELD + 8 * c + 8, :] = packs[1]
        for r in range(8):
            row = 8 * (8 * c + r) + 7
            msg_ref[x, row : row + 1, :] = packs[2 + r // 4][r % 4 : r % 4 + 1]
        row = FIELD + 8 * C + c
        msg_ref[x, row : row + 1, :] = jnp.concatenate([tail[14:15], jnp.zeros((1, 96), f32)], axis=1)


def sum_kernel(got_ref, out_ref, keep_ref):
    c = lax.axis_index("c")
    picks = pl.ds(pl.multiple_of(FIELD + 8 * c, 8), 8)
    olds = pl.ds(64 * c + 7, 8, stride=8)
    steps = pl.ds(FIELD + 8 * C + c, 1)
    total, old, step = got_ref[0, picks, :], got_ref[0, olds, :], got_ref[0, steps, :]
    for g in range(1, GROUPS):
        total = total + got_ref[g, picks, :]
        old = old + got_ref[g, olds, :]
        step = step + got_ref[g, steps, :]
    for z in range(out_ref.shape[0]):
        out_ref[z] = total
    keep_ref[0:8, :] = old
    keep_ref[8:16, :] = jnp.broadcast_to(step, (8, 128))


def weight_rows(tile, row, center):
    value = (jnp.where(row < 6, tile, 1.0) - center) * tile[6:7]
    first = value.astype(bf16).astype(f32)
    rest = value - first
    second = rest.astype(bf16).astype(f32)
    return jnp.concatenate([first, second, rest - second, jnp.zeros_like(value)], axis=0).astype(bf16)


def cross_rows(tile, row, center):
    tile = jnp.where(row < 6, tile, 1.0) - center
    dot = jnp.sum(tile[0:3] * tile[3:6], axis=0, keepdims=True)
    value = jnp.where(row == 7, dot, tile)
    first = value.astype(bf16).astype(f32)
    rest = value - first
    second = rest.astype(bf16).astype(f32)
    third = rest - second
    return jnp.concatenate([first, second, first, second, third, first, third, second], axis=0).astype(bf16)


def target_rows(pos, vel, center):
    pos, vel = pos - center[0:3, 0:1], vel - center[3:6, 0:1]
    value = jnp.concatenate([-vel, -pos, jnp.sum(pos * vel, axis=0, keepdims=True), jnp.ones_like(pos[0:1])], axis=0)
    first = value.astype(bf16).astype(f32)
    rest = value - first
    second = rest.astype(bf16).astype(f32)
    third = rest - second
    return jnp.transpose(jnp.concatenate([first, first, second, second, first, third, second, third], axis=0)).astype(bf16)


def force_kernel(targets_ref, got_ref, keep_ref, out_ref, seen_ref, left_ref, along_ref, sums_ref):
    target = targets_ref[0]
    for z in range(1, targets_ref.shape[0]):
        target = target + targets_ref[z]
    columns = jnp.transpose(target)
    for q in range(3):
        seen_ref[q, 0:MAIN, :] = jnp.broadcast_to(columns[:, q : q + 1], (MAIN, 128))
        for half in range(2):
            seen_ref[half * 3 + q, MAIN:PER, :] = jnp.broadcast_to(
                columns[q * TAIL : (q + 1) * TAIL, half * 4 + 3 : half * 4 + 4], (TAIL, 128)
            )
    row = lax.broadcasted_iota(jnp.int32, (8, 128), 0)
    center = jnp.broadcast_to(jnp.mean(got_ref[0, 0:8, :], axis=1, keepdims=True), (8, 128))
    center = jnp.where(row < 6, center, 0.0)
    left_ref[...] = target_rows(target[0:3], target[4:7], center)
    sums_ref[...] = jnp.zeros_like(sums_ref)

    across = CHUNK // 128
    chunks = GROUPS * TILES // across

    def tiles_of(n):
        g, part = n // (TILES // across), n % (TILES // across)
        return g, pl.multiple_of(part * (CHUNK // 16), 8)

    def cross(n, slot):
        g, base = tiles_of(n)
        right = [cross_rows(got_ref[g, pl.ds(base + j * 8, 8), :], row, center) for j in range(across)]
        along_ref[slot] = jnp.dot(left_ref[...], jnp.concatenate(right, axis=1), preferred_element_type=f32)

    def chunk(n, slot):
        g, base = tiles_of(n)
        star = [
            jnp.concatenate(
                [jnp.broadcast_to(got_ref[g, pl.ds(base + j * 8 + q, 1), :], (ROWS, 128)) for j in range(across)], axis=1
            )
            for q in range(6)
        ]
        weight = jnp.concatenate(
            [weight_rows(got_ref[g, pl.ds(base + j * 8, 8), :], row, center) for j in range(across)], axis=1
        )
        values = []
        for b in range(BLOCKS):
            r = slice(b * ROWS, (b + 1) * ROWS)
            needed = 3 if b < CROSSED else 6
            apart = [star[q] - jnp.concatenate([seen_ref[q, r, :]] * across, axis=1) for q in range(needed)]
            dx, dy, dz = apart[0:3]
            total = (dx * dx + EPS2) + dy * dy + dz * dz
            if b < CROSSED:
                along = along_ref[slot, r, :]
            else:
                wx, wy, wz = apart[3:6]
                along = dx * wx + dy * wy + dz * wz
            inverse = lax.rsqrt(total)
            square = inverse * inverse
            cube = square * inverse
            rate = cube * (square * along)
            for value in (cube, rate):
                high = value.astype(bf16)
                values += [high, (value - high.astype(f32)).astype(bf16)]
            if (b + 1) * 4 * ROWS % 256 == 0 or b == BLOCKS - 1:
                right = jnp.concatenate(values, axis=0)
                values = []
                end = (b + 1) * 4 * ROWS
                sums_ref[:, end - right.shape[0] : end] += lax.dot_general(
                    weight, right, (((1,), (1,)), ((), ())), preferred_element_type=f32
                )

    cross(0, 0)

    def body(n, _):
        for u in range(UNROLL):
            cross(jnp.minimum(n * UNROLL + u + 1, chunks - 1), (u + 1) % 2)
            chunk(n * UNROLL + u, u % 2)
        return 0

    lax.fori_loop(0, chunks // UNROLL, body, 0)
    sums = jnp.transpose(sums_ref[...])

    def columns_of(part):
        total = jnp.concatenate(
            [
                sums[b * 4 * ROWS + part * ROWS : b * 4 * ROWS + (part + 1) * ROWS]
                + sums[b * 4 * ROWS + (part + 1) * ROWS : b * 4 * ROWS + (part + 2) * ROWS]
                for b in range(BLOCKS)
            ],
            axis=0,
        )
        main = jnp.transpose(total[0:MAIN])
        tail = jnp.transpose(total[MAIN:PER])
        return main[0:8] + main[8:16] + main[16:24], tail[0:8] + tail[8:16] + tail[16:24]

    def three(value):
        return jnp.concatenate([value, value, value], axis=0)

    main, tail = columns_of(0)
    cube_pos = pack(main[0:3], tail[0:3])
    cube_vel = pack(main[3:6], tail[3:6])
    cube_one = pack(three(main[6:7]), three(tail[6:7]))
    main, tail = columns_of(2)
    rate_pos = pack(main[0:3], tail[0:3])
    rate_one = pack(three(main[6:7]), three(tail[6:7]))
    pos = target[0:4] - pack(center[0:3], center[0:3, 0:TAIL])
    vel = target[4:8] - pack(center[3:6], center[3:6, 0:TAIL])
    acc = cube_pos - pos * cube_one
    jerk = (cube_vel - vel * cube_one) - 3.0 * (rate_pos - pos * rate_one)
    last = jnp.concatenate([acc[3:4, 0:96], keep_ref[8:9, 0:TAIL]], axis=1)
    forces = jnp.concatenate([acc[0:3], last, jerk], axis=0)
    for z in range(out_ref.shape[0]):
        out_ref[z, 0:8, :] = forces
        out_ref[z, 8:16, :] = keep_ref[0:8, :]


def correct_kernel(scale, targets_ref, got_ref, out_ref):
    target = targets_ref[0]
    total = got_ref[0]
    for z in range(1, targets_ref.shape[0]):
        target = target + targets_ref[z]
        total = total + got_ref[z]
    forces = total[0:8] * scale
    old = total[8:16]
    main = jnp.concatenate([a[r : r + 1, 96:128] for a in (target, old) for r in (3, 7)], axis=1)
    tail = total[3:4, 96:128]
    step = pack(jnp.concatenate([main, main, main], axis=0), jnp.concatenate([tail, tail, tail], axis=0))
    pos, vel = correct(target[0:4], target[4:8], old[0:4], old[4:8], step, forces[0:4], forces[4:8])
    both = jnp.concatenate([pos, vel], axis=0)
    for d in range(out_ref.shape[0]):
        out_ref[d, 0:8, :] = forces
        out_ref[d, 8:16, :] = both


def store_kernel(state_ref, ticks_ref, levels_ref, active_ref, got_ref, new_active_ref, new_state_ref, sums_ref):
    start = first_star()
    mine = lax.axis_index("aa")

    def tails(c, y, row):
        parts = [got_ref[c * X + x, y, row : row + 1, :] for x in range(X)]
        return jnp.concatenate(
            [jnp.concatenate([p[:, q * TAIL : (q + 1) * TAIL] for p in parts], axis=1) for q in range(3)], axis=0
        )

    for c in range(C):
        for x in range(X):
            lanes = slice((c * X + x) * 128, (c * X + x + 1) * 128)
            tile = got_ref[c * X + x, mine]
            new_active_ref[0:3, lanes] = tile[8:11]
            new_active_ref[3:6, lanes] = tile[12:15]
            new_active_ref[6:9, lanes] = tile[0:3]
            new_active_ref[9:12, lanes] = tile[4:7]
        lanes = slice(1024 + c * 128, 1024 + (c + 1) * 128)
        new_active_ref[0:3, lanes] = tails(c, mine, 11)
        new_active_ref[3:6, lanes] = tails(c, mine, 15)
        new_active_ref[6:9, lanes] = tails(c, mine, 3)
        new_active_ref[9:12, lanes] = tails(c, mine, 7)

    row16 = lax.broadcasted_iota(jnp.int32, (16, 128), 0)
    owners = [
        jnp.where(row16 < edge, float(n), n + 1.0).astype(bf16) for n, edge in enumerate((12, 8, 4))
    ]
    rows = lax.broadcasted_iota(jnp.int32, (128, 128), 0).astype(f32).astype(bf16)
    nothing, unit = jnp.zeros((16, 128), bf16), jnp.ones((128, 128), bf16)
    sums_ref[...] = jnp.zeros_like(sums_ref)

    def block(y):
        tiles = [
            jnp.concatenate([got_ref[c * X + x, y, 0:3, :], got_ref[c * X + x, y, 4:7, :]], axis=0)
            for c in range(C)
            for x in range(X)
        ]
        for c in range(C):
            tiles.append(jnp.concatenate([tails(c, y, 3), tails(c, y, 7)], axis=0))
        lefts, lows = [], []
        for k, tile in enumerate(tiles):
            local = active_ref[pl.ds(y * 10 + k, 1), :] - start
            high = jnp.broadcast_to(jnp.right_shift(local, 7).astype(f32), (16, 128)).astype(bf16)
            low = jnp.broadcast_to(jnp.bitwise_and(local, 127).astype(f32), (128, 128)).astype(bf16)
            lows.append(jnp.where(rows == low, unit, jnp.zeros_like(unit)))
            first = tile.astype(bf16).astype(f32)
            both = jnp.concatenate([first, tile - first], axis=0)
            groups = [
                jnp.concatenate([both, both[0:4]], axis=0).astype(bf16),
                jnp.concatenate([both[4:12], both[0:8]], axis=0).astype(bf16),
                jnp.concatenate([both[8:12], both], axis=0).astype(bf16),
            ]
            aims = [high - owner for owner in owners]
            left = [
                jnp.where(aim == h, group, nothing) for h in range(0, TILES, 4) for aim, group in zip(aims, groups)
            ]
            lefts.append(jnp.concatenate(left, axis=0))
        total = lax.dot_general(
            jnp.concatenate(lefts, axis=1),
            jnp.concatenate(lows, axis=1),
            (((1,), (1,)), ((), ())),
            preferred_element_type=f32,
        )
        sums_ref[...] += total

    for y in range(got_ref.shape[1]):
        block(y)

    for i in range(TILES):
        lanes = slice(i * 128, (i + 1) * 128)
        s = state_ref[:, lanes]
        forces = sums_ref[i * 12 : i * 12 + 6, :] + sums_ref[i * 12 + 6 : i * 12 + 12, :]
        acc, jerk = forces[0:3], forces[3:6]
        ticks, levels = ticks_ref[i : i + 1, :], levels_ref[i : i + 1, :]
        hit = ticks == jnp.left_shift(jnp.ones_like(levels), LEVELS - levels)
        dt = ticks.astype(f32) * TICK
        step = step_of(levels)
        pos, vel = predict(s[0:3], s[3:6], s[6:9], s[9:12], dt)
        pos, vel = correct(pos, vel, s[6:9], s[9:12], step, acc, jerk)
        new = jnp.concatenate([pos, vel, acc, jerk], axis=0)
        new_state_ref[:, lanes] = jnp.where(hit, new, s)


def per_device(state, mass, levels, ticks, active):
    z_count, y_count = lax.axis_size("z"), lax.axis_size("aa")
    n_stars = state.shape[1] * z_count * GROUPS
    mass, levels, ticks = [a.reshape(TILES, 128) for a in (mass, levels, ticks)]
    active = active.reshape(-1, 128)

    message = pl.pallas_call(
        pick_kernel,
        out_shape=jax.ShapeDtypeStruct((X, FIELD + 8 * C + 8, 128), f32),
        in_specs=[pl.BlockSpec(memory_space=pltpu.HBM)] * 5,
        out_specs=vmem(1)[0],
        scratch_shapes=[pltpu.VMEM((384, 256), bf16), pltpu.VMEM((256, 1280), bf16)]
        + [pltpu.VMEM(a.shape, a.dtype) for a in (active, state, mass, ticks, levels)]
        + [pltpu.SemaphoreType.DMA((5,))],
        compiler_params=params(),
    )(*[pltpu.with_memory_space_constraint(a, pltpu.HBM) for a in (active, state, mass, ticks, levels)])
    got = lax.all_to_all(message, "x", 0, 0, tiled=True)
    got = lax.all_gather(got, "c", tiled=True)

    targets, keep = pl.pallas_call(
        sum_kernel,
        out_shape=[jax.ShapeDtypeStruct((z_count, 8, 128), f32), jax.ShapeDtypeStruct((16, 128), f32)],
        in_specs=vmem(1),
        out_specs=vmem(2),
        compiler_params=params(),
    )(got)
    targets = lax.all_to_all(targets, "z", 0, 0, tiled=True)

    partial = pl.pallas_call(
        force_kernel,
        out_shape=jax.ShapeDtypeStruct((z_count, 16, 128), f32),
        in_specs=vmem(3),
        out_specs=vmem(1)[0],
        scratch_shapes=[
            pltpu.VMEM((6, PER, 128), f32),
            pltpu.VMEM((CROSSED * ROWS, 64), bf16),
            pltpu.VMEM((2, CROSSED * ROWS, CHUNK), f32),
            pltpu.VMEM((32, 4 * PER), f32),
        ],
        compiler_params=params(),
    )(targets, got, keep)
    partial = lax.all_to_all(partial, "z", 0, 0, tiled=True)

    updates = pl.pallas_call(
        lambda *refs: correct_kernel(1.0 / n_stars, *refs),
        out_shape=jax.ShapeDtypeStruct((y_count * X, 16, 128), f32),
        in_specs=vmem(2),
        out_specs=vmem(1)[0],
        compiler_params=params(),
    )(targets, partial)
    updates = lax.all_to_all(updates, ("x", "aa"), 0, 0, tiled=True)
    updates = lax.all_gather(updates, "c", tiled=True).reshape(GROUPS, y_count, 16, 128)

    new_active, new_state = pl.pallas_call(
        store_kernel,
        out_shape=[jax.ShapeDtypeStruct((12, 1280), f32), jax.ShapeDtypeStruct(state.shape, f32)],
        in_specs=vmem(5),
        out_specs=vmem(2),
        scratch_shapes=[
            pltpu.VMEM((192, 128), f32),
        ],
        compiler_params=params(),
    )(state, ticks, levels, active, updates)
    return new_active, new_state


def solution(mesh):
    shape = (mesh.shape["ja"] // GROUPS, X, C, mesh.shape["aa"])
    fine = Mesh(mesh.devices.reshape(shape), ("z", "x", "c", "aa"))
    ja = ("z", "x", "c")
    return jax.shard_map(
        per_device,
        mesh=fine,
        in_specs=(P(None, ja), P(ja), P(ja), P(ja), P()),
        out_specs=(P(None, "aa"), P(None, ja)),
        check_vma=False,
    )
```

```python
import jax
import jax.numpy as jnp
from jax import lax
from jax.experimental import pallas as pl
from jax.experimental.pallas import tpu as pltpu
from jax.sharding import Mesh, PartitionSpec as P

LEVELS = 5
EPS2 = 0.0001
H_MAX = 0.25
TICK = H_MAX / 2**LEVELS

X, C = 4, 2
GROUPS = X * C
TILES = 16
MAIN, TAIL = 128, 32
PER = MAIN + TAIL
FIELD = 8 * TILES
CHUNK = 1024
ROWS = 16
BLOCKS = PER // ROWS
CROSSED = MAIN // ROWS
UNROLL = 8

f32, bf16 = jnp.float32, jnp.bfloat16


def params():
    return pltpu.CompilerParams(vmem_limit_bytes=48 * 1024 * 1024)


def vmem(n):
    return [pl.BlockSpec(memory_space=pltpu.VMEM)] * n


def predict(pos, vel, acc, jerk, dt):
    predicted = pos + dt * (vel + dt * (0.5 * acc + dt * (jerk / 6.0)))
    predicted_vel = vel + dt * (acc + dt * (0.5 * jerk))
    return predicted, predicted_vel


def step_of(levels):
    return jnp.left_shift(jnp.ones_like(levels), LEVELS - levels).astype(f32) * TICK


def correct(pos, vel, old_acc, old_jerk, step, acc_new, jerk_new):
    error = old_acc - acc_new
    second = -6.0 * error - step * (4.0 * old_jerk + 2.0 * jerk_new)
    third = 12.0 * error + 6.0 * step * (old_jerk + jerk_new)
    fixed_pos = pos + step * step * (second / 24.0 + third / 120.0)
    fixed_vel = vel + step * (second / 6.0 + third / 24.0)
    return fixed_pos, fixed_vel


def split3(value):
    first = value.astype(bf16)
    rest = value - first.astype(f32)
    second = rest.astype(bf16)
    return first, second, (rest - second.astype(f32)).astype(bf16)


def pack(main, tail, spare=None):
    if spare is None:
        spare = jnp.zeros((1, TAIL), f32)
    last = jnp.concatenate([tail[0:1], tail[1:2], tail[2:3], spare], axis=1)
    return jnp.concatenate([main, last], axis=0)


def first_star():
    return ((lax.axis_index("z") * X + lax.axis_index("x")) * C + lax.axis_index("c")) * (TILES * 128)


def pick_kernel(*refs):
    given, msg_ref, table_ref, chosen_ref, held, sems = refs[:5], refs[5], refs[6], refs[7], refs[8:13], refs[13]
    copies = [pltpu.make_async_copy(a, b, sems.at[n]) for n, (a, b) in enumerate(zip(given, held))]
    for copy in copies:
        copy.start()
    active_ref, state_ref, mass_ref, ticks_ref, levels_ref = held
    start = first_star()
    block = lax.axis_index("aa") * 10
    copies[0].wait()
    rows = lax.broadcasted_iota(jnp.int32, (256, 128), 0)
    highs = []
    for k in range(10):
        local = active_ref[pl.ds(block + k, 1), :] - start
        highs.append(jnp.right_shift(local, 8))
        chosen_ref[:, k * 128 : (k + 1) * 128] = jnp.where(rows == jnp.bitwise_and(local, 255), 1.0, 0.0).astype(bf16)
    for copy in copies[1:]:
        copy.wait()
    zero = jnp.zeros((1, 128), f32)
    for i in range(TILES):
        s = state_ref[:, i * 128 : (i + 1) * 128]
        dt = ticks_ref[i : i + 1, :].astype(f32) * TICK
        pos, vel = predict(s[0:3], s[3:6], s[6:9], s[9:12], dt)
        step = step_of(levels_ref[i : i + 1, :])
        field = jnp.concatenate([pos, vel, mass_ref[i : i + 1, :], zero], axis=0)
        both = jnp.concatenate([field, s[6:12], step, zero], axis=0)
        for n, part in enumerate(split3(both)):
            row = n * 128 + i // 2 * 16
            table_ref[row : row + 16, i % 2 * 128 : (i % 2 + 1) * 128] = part
        for x in range(X):
            msg_ref[x, i * 8 : (i + 1) * 8, :] = field
    picks = []
    for pair in range(5):
        found = jnp.dot(
            table_ref[...], chosen_ref[:, pair * 256 : (pair + 1) * 256], preferred_element_type=f32
        )
        for k in range(2):
            high = jnp.broadcast_to(highs[2 * pair + k], (16, 128))
            pick = jnp.zeros((16, 128), f32)
            for h in range(TILES // 2):
                r = [found[n * 128 + h * 16 : n * 128 + (h + 1) * 16, k * 128 : (k + 1) * 128] for n in range(3)]
                pick = jnp.where(high == h, (r[0] + r[1]) + r[2], pick)
            picks.append(pick)
    for g in range(GROUPS):
        main = picks[g]
        tail = picks[8 + g // 4][:, (g % 4) * TAIL : (g % 4 + 1) * TAIL]
        step = [main[14:15, n * TAIL : (n + 1) * TAIL] for n in range(4)]
        x, c = g % X, g // X
        packs = [pack(main[q : q + 3], tail[q : q + 3], step[n]) for n, q in enumerate((0, 3, 8, 11))]
        msg_ref[x, FIELD + 8 * c : FIELD + 8 * c + 4, :] = packs[0]
        msg_ref[x, FIELD + 8 * c + 4 : FIELD + 8 * c + 8, :] = packs[1]
        for r in range(8):
            row = 8 * (8 * c + r) + 7
            msg_ref[x, row : row + 1, :] = packs[2 + r // 4][r % 4 : r % 4 + 1]
        row = FIELD + 8 * C + c
        msg_ref[x, row : row + 1, :] = jnp.concatenate([tail[14:15], jnp.zeros((1, 96), f32)], axis=1)


def sum_kernel(got_ref, out_ref, keep_ref):
    c = lax.axis_index("c")
    picks = pl.ds(pl.multiple_of(FIELD + 8 * c, 8), 8)
    olds = pl.ds(64 * c + 7, 8, stride=8)
    steps = pl.ds(FIELD + 8 * C + c, 1)
    total, old, step = got_ref[0, picks, :], got_ref[0, olds, :], got_ref[0, steps, :]
    for g in range(1, GROUPS):
        total = total + got_ref[g, picks, :]
        old = old + got_ref[g, olds, :]
        step = step + got_ref[g, steps, :]
    for z in range(out_ref.shape[0]):
        out_ref[z, 0:8, :] = total
        out_ref[z, 8:16, :] = old
    keep_ref[...] = jnp.broadcast_to(step, (8, 128))


def weight_rows(tile, row, center):
    value = (jnp.where(row < 6, tile, 1.0) - center) * tile[6:7]
    first = value.astype(bf16).astype(f32)
    rest = value - first
    second = rest.astype(bf16).astype(f32)
    return jnp.concatenate([first, second, rest - second, jnp.zeros_like(value)], axis=0).astype(bf16)


def cross_rows(tile, row, center):
    tile = jnp.where(row < 6, tile, 1.0) - center
    dot = jnp.sum(tile[0:3] * tile[3:6], axis=0, keepdims=True)
    value = jnp.where(row == 7, dot, tile)
    first = value.astype(bf16).astype(f32)
    rest = value - first
    second = rest.astype(bf16).astype(f32)
    third = rest - second
    return jnp.concatenate([first, second, first, second, third, first, third, second], axis=0).astype(bf16)


def target_rows(pos, vel, center):
    pos, vel = pos - center[0:3, 0:1], vel - center[3:6, 0:1]
    value = jnp.concatenate([-vel, -pos, jnp.sum(pos * vel, axis=0, keepdims=True), jnp.ones_like(pos[0:1])], axis=0)
    first = value.astype(bf16).astype(f32)
    rest = value - first
    second = rest.astype(bf16).astype(f32)
    third = rest - second
    return jnp.transpose(jnp.concatenate([first, first, second, second, first, third, second, third], axis=0)).astype(bf16)


def force_kernel(targets_ref, got_ref, keep_ref, out_ref, seen_ref, left_ref, along_ref, sums_ref):
    target = targets_ref[0, 0:8, :]
    for z in range(1, targets_ref.shape[0]):
        target = target + targets_ref[z, 0:8, :]
    columns = jnp.transpose(target)
    for q in range(3):
        seen_ref[q, 0:MAIN, :] = jnp.broadcast_to(columns[:, q : q + 1], (MAIN, 128))
        for half in range(2):
            seen_ref[half * 3 + q, MAIN:PER, :] = jnp.broadcast_to(
                columns[q * TAIL : (q + 1) * TAIL, half * 4 + 3 : half * 4 + 4], (TAIL, 128)
            )
    row = lax.broadcasted_iota(jnp.int32, (8, 128), 0)
    center = jnp.broadcast_to(jnp.mean(got_ref[0, 0:8, :], axis=1, keepdims=True), (8, 128))
    center = jnp.where(row < 6, center, 0.0)
    left_ref[...] = target_rows(target[0:3], target[4:7], center)
    sums_ref[...] = jnp.zeros_like(sums_ref)

    across = CHUNK // 128
    chunks = GROUPS * TILES // across

    def tiles_of(n):
        g, part = n // (TILES // across), n % (TILES // across)
        return g, pl.multiple_of(part * (CHUNK // 16), 8)

    def cross(n, slot):
        g, base = tiles_of(n)
        right = [cross_rows(got_ref[g, pl.ds(base + j * 8, 8), :], row, center) for j in range(across)]
        along_ref[slot] = jnp.dot(left_ref[...], jnp.concatenate(right, axis=1), preferred_element_type=f32)

    def chunk(n, slot):
        g, base = tiles_of(n)
        star = [
            jnp.concatenate(
                [jnp.broadcast_to(got_ref[g, pl.ds(base + j * 8 + q, 1), :], (ROWS, 128)) for j in range(across)], axis=1
            )
            for q in range(6)
        ]
        weight = jnp.concatenate(
            [weight_rows(got_ref[g, pl.ds(base + j * 8, 8), :], row, center) for j in range(across)], axis=1
        )
        values = []
        for b in range(BLOCKS):
            r = slice(b * ROWS, (b + 1) * ROWS)
            needed = 3 if b < CROSSED else 6
            apart = [star[q] - jnp.concatenate([seen_ref[q, r, :]] * across, axis=1) for q in range(needed)]
            dx, dy, dz = apart[0:3]
            total = (dx * dx + EPS2) + dy * dy + dz * dz
            if b < CROSSED:
                along = along_ref[slot, r, :]
            else:
                wx, wy, wz = apart[3:6]
                along = dx * wx + dy * wy + dz * wz
            inverse = lax.rsqrt(total)
            square = inverse * inverse
            cube = square * inverse
            rate = cube * (square * along)
            for value in (cube, rate):
                high = value.astype(bf16)
                values += [high, (value - high.astype(f32)).astype(bf16)]
            if (b + 1) * 4 * ROWS % 256 == 0 or b == BLOCKS - 1:
                right = jnp.concatenate(values, axis=0)
                values = []
                end = (b + 1) * 4 * ROWS
                sums_ref[:, end - right.shape[0] : end] += lax.dot_general(
                    weight, right, (((1,), (1,)), ((), ())), preferred_element_type=f32
                )

    cross(0, 0)

    def body(n, _):
        for u in range(UNROLL):
            cross(jnp.minimum(n * UNROLL + u + 1, chunks - 1), (u + 1) % 2)
            chunk(n * UNROLL + u, u % 2)
        return 0

    lax.fori_loop(0, chunks // UNROLL, body, 0)
    sums = jnp.transpose(sums_ref[...])

    def columns_of(part):
        total = jnp.concatenate(
            [
                sums[b * 4 * ROWS + part * ROWS : b * 4 * ROWS + (part + 1) * ROWS]
                + sums[b * 4 * ROWS + (part + 1) * ROWS : b * 4 * ROWS + (part + 2) * ROWS]
                for b in range(BLOCKS)
            ],
            axis=0,
        )
        main = jnp.transpose(total[0:MAIN])
        tail = jnp.transpose(total[MAIN:PER])
        return main[0:8] + main[8:16] + main[16:24], tail[0:8] + tail[8:16] + tail[16:24]

    def three(value):
        return jnp.concatenate([value, value, value], axis=0)

    main, tail = columns_of(0)
    cube_pos = pack(main[0:3], tail[0:3])
    cube_vel = pack(main[3:6], tail[3:6])
    cube_one = pack(three(main[6:7]), three(tail[6:7]))
    main, tail = columns_of(2)
    rate_pos = pack(main[0:3], tail[0:3])
    rate_one = pack(three(main[6:7]), three(tail[6:7]))
    pos = target[0:4] - pack(center[0:3], center[0:3, 0:TAIL])
    vel = target[4:8] - pack(center[3:6], center[3:6, 0:TAIL])
    acc = cube_pos - pos * cube_one
    jerk = (cube_vel - vel * cube_one) - 3.0 * (rate_pos - pos * rate_one)
    last = jnp.concatenate([acc[3:4, 0:96], keep_ref[0:1, 0:TAIL]], axis=1)
    forces = jnp.concatenate([acc[0:3], last, jerk], axis=0)
    for z in range(out_ref.shape[0]):
        out_ref[z] = forces


def correct_kernel(scale, targets_ref, got_ref, out_ref):
    target = targets_ref[0]
    total = got_ref[0]
    for z in range(1, targets_ref.shape[0]):
        target = target + targets_ref[z]
        total = total + got_ref[z]
    forces = total * scale
    old = target[8:16]
    main = jnp.concatenate([a[r : r + 1, 96:128] for a in (target[0:8], old) for r in (3, 7)], axis=1)
    tail = total[3:4, 96:128]
    step = pack(jnp.concatenate([main, main, main], axis=0), jnp.concatenate([tail, tail, tail], axis=0))
    pos, vel = correct(target[0:4], target[4:8], old[0:4], old[4:8], step, forces[0:4], forces[4:8])
    both = jnp.concatenate([pos, vel], axis=0)
    for d in range(out_ref.shape[0]):
        out_ref[d, 0:8, :] = forces
        out_ref[d, 8:16, :] = both


def store_kernel(state_ref, ticks_ref, levels_ref, active_ref, got_ref, new_active_ref, new_state_ref, sums_ref):
    start = first_star()
    mine = lax.axis_index("aa")

    def tails(c, y, row):
        parts = [got_ref[c * X + x, y, row : row + 1, :] for x in range(X)]
        return jnp.concatenate(
            [jnp.concatenate([p[:, q * TAIL : (q + 1) * TAIL] for p in parts], axis=1) for q in range(3)], axis=0
        )

    for c in range(C):
        for x in range(X):
            lanes = slice((c * X + x) * 128, (c * X + x + 1) * 128)
            tile = got_ref[c * X + x, mine]
            new_active_ref[0:3, lanes] = tile[8:11]
            new_active_ref[3:6, lanes] = tile[12:15]
            new_active_ref[6:9, lanes] = tile[0:3]
            new_active_ref[9:12, lanes] = tile[4:7]
        lanes = slice(1024 + c * 128, 1024 + (c + 1) * 128)
        new_active_ref[0:3, lanes] = tails(c, mine, 11)
        new_active_ref[3:6, lanes] = tails(c, mine, 15)
        new_active_ref[6:9, lanes] = tails(c, mine, 3)
        new_active_ref[9:12, lanes] = tails(c, mine, 7)

    row16 = lax.broadcasted_iota(jnp.int32, (16, 128), 0)
    owners = [
        jnp.where(row16 < edge, float(n), n + 1.0).astype(bf16) for n, edge in enumerate((12, 8, 4))
    ]
    rows = lax.broadcasted_iota(jnp.int32, (128, 128), 0).astype(f32).astype(bf16)
    nothing, unit = jnp.zeros((16, 128), bf16), jnp.ones((128, 128), bf16)
    sums_ref[...] = jnp.zeros_like(sums_ref)

    def block(y):
        tiles = [
            jnp.concatenate([got_ref[c * X + x, y, 0:3, :], got_ref[c * X + x, y, 4:7, :]], axis=0)
            for c in range(C)
            for x in range(X)
        ]
        for c in range(C):
            tiles.append(jnp.concatenate([tails(c, y, 3), tails(c, y, 7)], axis=0))
        lefts, lows = [], []
        for k, tile in enumerate(tiles):
            local = active_ref[pl.ds(y * 10 + k, 1), :] - start
            high = jnp.broadcast_to(jnp.right_shift(local, 7).astype(f32), (16, 128)).astype(bf16)
            low = jnp.broadcast_to(jnp.bitwise_and(local, 127).astype(f32), (128, 128)).astype(bf16)
            lows.append(jnp.where(rows == low, unit, jnp.zeros_like(unit)))
            first = tile.astype(bf16).astype(f32)
            both = jnp.concatenate([first, tile - first], axis=0)
            groups = [
                jnp.concatenate([both, both[0:4]], axis=0).astype(bf16),
                jnp.concatenate([both[4:12], both[0:8]], axis=0).astype(bf16),
                jnp.concatenate([both[8:12], both], axis=0).astype(bf16),
            ]
            aims = [high - owner for owner in owners]
            left = [
                jnp.where(aim == h, group, nothing) for h in range(0, TILES, 4) for aim, group in zip(aims, groups)
            ]
            lefts.append(jnp.concatenate(left, axis=0))
        total = lax.dot_general(
            jnp.concatenate(lefts, axis=1),
            jnp.concatenate(lows, axis=1),
            (((1,), (1,)), ((), ())),
            preferred_element_type=f32,
        )
        sums_ref[...] += total

    for y in range(got_ref.shape[1]):
        block(y)

    for i in range(TILES):
        lanes = slice(i * 128, (i + 1) * 128)
        s = state_ref[:, lanes]
        forces = sums_ref[i * 12 : i * 12 + 6, :] + sums_ref[i * 12 + 6 : i * 12 + 12, :]
        acc, jerk = forces[0:3], forces[3:6]
        ticks, levels = ticks_ref[i : i + 1, :], levels_ref[i : i + 1, :]
        hit = ticks == jnp.left_shift(jnp.ones_like(levels), LEVELS - levels)
        dt = ticks.astype(f32) * TICK
        step = step_of(levels)
        pos, vel = predict(s[0:3], s[3:6], s[6:9], s[9:12], dt)
        pos, vel = correct(pos, vel, s[6:9], s[9:12], step, acc, jerk)
        new = jnp.concatenate([pos, vel, acc, jerk], axis=0)
        new_state_ref[:, lanes] = jnp.where(hit, new, s)


def per_device(state, mass, levels, ticks, active):
    z_count, y_count = lax.axis_size("z"), lax.axis_size("aa")
    n_stars = state.shape[1] * z_count * GROUPS
    mass, levels, ticks = [a.reshape(TILES, 128) for a in (mass, levels, ticks)]
    active = active.reshape(-1, 128)

    message = pl.pallas_call(
        pick_kernel,
        out_shape=jax.ShapeDtypeStruct((X, FIELD + 8 * C + 8, 128), f32),
        in_specs=[pl.BlockSpec(memory_space=pltpu.HBM)] * 5,
        out_specs=vmem(1)[0],
        scratch_shapes=[pltpu.VMEM((384, 256), bf16), pltpu.VMEM((256, 1280), bf16)]
        + [pltpu.VMEM(a.shape, a.dtype) for a in (active, state, mass, ticks, levels)]
        + [pltpu.SemaphoreType.DMA((5,))],
        compiler_params=params(),
    )(*[pltpu.with_memory_space_constraint(a, pltpu.HBM) for a in (active, state, mass, ticks, levels)])
    got = lax.all_to_all(message, "x", 0, 0, tiled=True)
    got = lax.all_gather(got, "c", tiled=True)

    targets, keep = pl.pallas_call(
        sum_kernel,
        out_shape=[jax.ShapeDtypeStruct((z_count, 16, 128), f32), jax.ShapeDtypeStruct((8, 128), f32)],
        in_specs=vmem(1),
        out_specs=vmem(2),
        compiler_params=params(),
    )(got)
    targets = lax.all_to_all(targets, "z", 0, 0, tiled=True)

    partial = pl.pallas_call(
        force_kernel,
        out_shape=jax.ShapeDtypeStruct((z_count, 8, 128), f32),
        in_specs=vmem(3),
        out_specs=vmem(1)[0],
        scratch_shapes=[
            pltpu.VMEM((6, PER, 128), f32),
            pltpu.VMEM((CROSSED * ROWS, 64), bf16),
            pltpu.VMEM((2, CROSSED * ROWS, CHUNK), f32),
            pltpu.VMEM((32, 4 * PER), f32),
        ],
        compiler_params=params(),
    )(targets, got, keep)
    partial = lax.all_to_all(partial, "z", 0, 0, tiled=True)

    updates = pl.pallas_call(
        lambda *refs: correct_kernel(1.0 / n_stars, *refs),
        out_shape=jax.ShapeDtypeStruct((y_count * X, 16, 128), f32),
        in_specs=vmem(2),
        out_specs=vmem(1)[0],
        compiler_params=params(),
    )(targets, partial)
    updates = lax.all_to_all(updates, ("x", "aa"), 0, 0, tiled=True)
    updates = lax.all_gather(updates, "c", tiled=True).reshape(GROUPS, y_count, 16, 128)

    new_active, new_state = pl.pallas_call(
        store_kernel,
        out_shape=[jax.ShapeDtypeStruct((12, 1280), f32), jax.ShapeDtypeStruct(state.shape, f32)],
        in_specs=vmem(5),
        out_specs=vmem(2),
        scratch_shapes=[
            pltpu.VMEM((192, 128), f32),
        ],
        compiler_params=params(),
    )(state, ticks, levels, active, updates)
    return new_active, new_state


def solution(mesh):
    shape = (mesh.shape["ja"] // GROUPS, X, C, mesh.shape["aa"])
    fine = Mesh(mesh.devices.reshape(shape), ("z", "x", "c", "aa"))
    ja = ("z", "x", "c")
    return jax.shard_map(
        per_device,
        mesh=fine,
        in_specs=(P(None, ja), P(ja), P(ja), P(ja), P()),
        out_specs=(P(None, "aa"), P(None, ja)),
        check_vma=False,
    )
```
